32 devices in a mesh: space: 16 (over z, y, core), event: 2 (over x).
Axes of the slice: x: 2, y: 2, z: 4, core: 2. Of those that a mesh axis runs over, the one named last changes fastest.
Arguments:
- fwd_now: float32 [4, 64, 16384], P('event', None, 'space'), as said below
- fwd_prev: float32 [4, 64, 16384], P('event', None, 'space'), as said below
- adj_now: float32 [4, 64, 16384], P('event', None, 'space'), as said below
- adj_prev: float32 [4, 64, 16384], P('event', None, 'space'), as said below
- shear_mod: float32 [64, 16384], P(None, 'space'), may hold values from 0.5 to 2
- density: float32 [16384], P('space'), may hold values from 0.5 to 2
- station_owner: int32 [32768, 1], P('space'), may hold values from 0 to 15; in each aligned block of 2048 rows (0 to 2047, 2048 to 4095, ...) at most 256 rows name the same one
- receiver_local: int32 [32768], P('space'), may hold values from 0 to 1023
- station_weights: float32 [64, 32768], P(None, 'space'), may hold values from -6 to 6
- adj_records: float32 [4, 2, 32768], P('event', None, 'space'), may hold values from -6 to 6
Outputs:
- fwd_last: float32 [4, 64, 16384], P('event', None, 'space')
- fwd_before: float32 [4, 64, 16384], P('event', None, 'space')
- adj_last: float32 [4, 64, 16384], P('event', None, 'space')
- adj_before: float32 [4, 64, 16384], P('event', None, 'space')
- kernel: float32 [64, 16384], P(None, ('space', 'event'))
The draws below stay inside these ranges and needn't reach their ends.
Inputs may be any that keep to these rules, and one draw needn't show every extreme that they name: `station_owner`: the 2048 stations of one index of space name at most 256 with the same owner. `fwd_now`: each displacement is continuous: element-local copies of a shared node hold equal values. `fwd_prev`: continuous like fwd_now. `adj_now`: continuous like fwd_now. `adj_prev`: continuous like fwd_now.
All inputs are finite; a program needn't handle non-finite values.
Results may differ from the reference program's by a relative error of at most 0.0001.
Values sent between devices are 32-bit elements; how exact they have to be, the bound alone decides.
No kernel may reach another device: no remote copies, remote signals or barrier semaphores. Data moves between devices by JAX's collectives and lax.ppermute only.
A program may use at most 64 MiB of HBM per device.

```python
import math
import jax
import jax.numpy as jnp
import numpy as np
from jax import lax

NODES = 64
EX = 16
EY = 16
LAYERS = 4
ST_DEV = 2048
STEPS = 2
CAP = 256
ELEM_DEV = 1024
ELEMENTS = 16384
EVENTS = 4
STATIONS = 32768
N_SPACE = 16


def nodal_field(key):
    depth = ELEMENTS // (EX * EY)
    shape = (EVENTS, 3 * depth + 1, 3 * EY + 1, 3 * EX + 1)
    values = jax.random.normal(key, shape, jnp.float32)
    element = jnp.arange(ELEMENTS, dtype=jnp.int32)
    node = jnp.arange(64, dtype=jnp.int32)
    col_x = 3 * (element % EX)[None, :] + (node % 4)[:, None]
    col_y = 3 * (element // EX % EY)[None, :] + (node // 4 % 4)[:, None]
    col_z = 3 * (element // (EX * EY))[None, :] + (node // 16)[:, None]
    return values[:, col_z, col_y, col_x]


def draw_fwd_now(key, part):
    return nodal_field(jax.random.fold_in(key, 11))


def draw_fwd_prev(key, part):
    return nodal_field(jax.random.fold_in(key, 23))


def draw_adj_now(key, part):
    return nodal_field(jax.random.fold_in(key, 37))


def draw_adj_prev(key, part):
    return nodal_field(jax.random.fold_in(key, 41))


def plant(result, key, least, top_value):
    longest = result.shape.index(max(result.shape))
    spots = []
    for shift in (0, 1):
        where = [jax.random.randint(jax.random.fold_in(key, axis), (), 0, length) for axis, length in enumerate(result.shape)]
        where[longest] = (where[longest] + shift) % result.shape[longest]
        spots.append(tuple(where))
    return result.at[spots[0]].set(least).at[spots[1]].set(top_value)


def block_scale(stream_key, extent, split, low, top_value):
    def one(axis_at, blocks):
        draws = jax.random.uniform(jax.random.fold_in(jax.random.fold_in(stream_key, 6), axis_at), (blocks,), jnp.float32, low / len(split), top_value / len(split))
        return jnp.repeat(jnp.exp(draws), extent[axis_at] // blocks).reshape((-1,) + (1,) * (len(extent) - axis_at - 1))

    factor_of = one(*split[0])
    for cut in split[1:]:
        factor_of = factor_of * one(*cut)
    return factor_of


def deal_out(stream_key, own, number, rows, amount, top, limit, lean):
    sequence = jax.random.permutation(stream_key, amount)
    heavy_load, ordinary = load_shares(amount, rows * top, limit, lean, True), load_shares(amount, rows * top, limit, lean, False)
    places = jnp.arange(amount)

    def named(lengths, rotation):
        used = int((lengths > 0).sum())
        fixed = max(1, used // 4)
        passed = fixed + (places - fixed + rotation * (used - fixed)) % max(1, amount - fixed)
        return jnp.zeros((amount,), jnp.int32).at[sequence[jnp.where(places < fixed, places, passed)]].set(jnp.asarray(lengths, jnp.int32))

    lengths = jnp.where(number % 4 == 0, named(heavy_load, number // 4), named(ordinary, number - number // 4 - 1))
    mixed = jax.random.permutation(jax.random.fold_in(own, 3), amount)
    source_of, receiver = mixed[0:amount // 2 * 2:2], mixed[1:amount // 2 * 2:2]
    slack = jnp.minimum(lengths[source_of] - 1, limit - lengths[receiver]) // 2
    slack = jnp.where((source_of == sequence[0]) | (receiver == sequence[0]) | (lengths[receiver] == 0), 0, jnp.maximum(slack, 0))
    passed = jax.random.randint(jax.random.fold_in(own, 4), (amount // 2,), 0, 1 << 20) % (slack + 1)
    lengths = lengths.at[source_of].add(-passed).at[receiver].add(passed)
    members = jnp.searchsorted(jnp.cumsum(lengths), jnp.arange(rows * top), side="right").astype(jnp.int32)
    listing = members.reshape(top, rows).T
    listing = listing[jax.random.permutation(jax.random.fold_in(own, 1), rows)]
    rotation = jax.random.randint(jax.random.fold_in(own, 2), (rows, 1), 0, top)
    return jnp.take_along_axis(listing, (jnp.arange(top)[None, :] + rotation) % top, axis=1)


def load_shares(amount, total, limit, slope, full):
    portions = [(1 << 20) // math.isqrt(standing ** slope) + 1 for standing in range(1, amount + 1)]
    largest = limit if full else min(limit, max(-(-total // amount), total * portions[0] // sum(portions)))
    least = 1 if total - largest >= amount - 1 else 0
    counts, rest = [largest] + [least] * (amount - 1), total - largest - least * (amount - 1)
    while rest > 0:
        movable = [i for i in range(1, amount) if counts[i] < largest] or [i for i in range(1, amount) if counts[i] < limit]
        pool, remaining = sum([portions[i] for i in movable]), rest
        for i in movable:
            more = min(limit - counts[i], max(1, remaining * portions[i] // pool), rest)
            counts[i] = counts[i] + more
            rest = rest - more
    return np.array(counts)


def bell_draw(rng, dims, scale, bound, split=(), held_as=jnp.bfloat16):
    loudness = block_scale(rng, dims, split, -0.22, 0.18) if split else 1.0
    drawn = jax.random.normal(rng, dims, jnp.float32) * scale * loudness
    return jnp.minimum(jnp.maximum(drawn, -bound), bound).astype(held_as)


def setup_inputs(seed: int = 0) -> dict:
    streams_of = jax.random.split(jax.random.key(seed), 11)
    fwd_now = draw_fwd_now(jax.random.fold_in(streams_of[10], 71), 0)
    fwd_prev = draw_fwd_prev(jax.random.fold_in(streams_of[10], 71), 0)
    adj_now = draw_adj_now(jax.random.fold_in(streams_of[10], 71), 0)
    adj_prev = draw_adj_prev(jax.random.fold_in(streams_of[10], 71), 0)
    shear_mod = jnp.clip(jnp.exp(math.log(2.0) - 1.3862944 * jax.random.uniform(streams_of[4], (NODES, ELEMENTS), jnp.float32) ** block_scale(streams_of[4], (NODES, ELEMENTS), ((1, 16),), -0.2, 0.2)), 0.5, 2.0)
    density = jnp.clip(jnp.exp(math.log(2.0) - 1.3862944 * jax.random.uniform(streams_of[5], (ELEMENTS,), jnp.float32) ** block_scale(streams_of[5], (ELEMENTS,), ((0, 16),), -0.2, 0.2)), 0.5, 2.0)
    station_owner_keys = jax.random.split(jax.random.fold_in(streams_of[6], 1), STATIONS // ST_DEV)
    station_owner_turns = jax.random.permutation(jax.random.fold_in(streams_of[6], 3), STATIONS // ST_DEV)
    station_owner = jax.vmap(lambda own, number: deal_out(jax.random.fold_in(streams_of[6], 2), own, number, ST_DEV, N_SPACE, 1, CAP, 2))(station_owner_keys, station_owner_turns).reshape((STATIONS, 1))
    receiver_local = plant(jax.random.randint(streams_of[7], (STATIONS,), 0, ELEM_DEV), jax.random.fold_in(streams_of[7], 1), 0, ELEM_DEV - 1).astype(jnp.int32)
    station_weights = bell_draw(streams_of[8], (NODES, STATIONS), 1.0, 6.0, ((1, 16),), jnp.float32)
    adj_records = bell_draw(streams_of[9], (EVENTS, STEPS, STATIONS), 1.0, 6.0, ((0, 2), (2, 16)), jnp.float32)
    return {"fwd_now": fwd_now, "fwd_prev": fwd_prev, "adj_now": adj_now, "adj_prev": adj_prev, "shear_mod": shear_mod, "density": density, "station_owner": station_owner, "receiver_local": receiver_local, "station_weights": station_weights, "adj_records": adj_records}


TIME_STEP = 0.08
STEP_SQUARE = 0.0064

def element_tables():
    root = 1.0 / np.sqrt(5.0)
    points = np.array([-1.0, -root, root, 1.0])
    weights = np.array([1.0 / 6.0, 5.0 / 6.0, 5.0 / 6.0, 1.0 / 6.0])
    derivative = np.zeros((4, 4))
    for i in range(4):
        for j in range(4):
            if i == j:
                derivative[i, i] = sum((1.0 / (points[i] - points[k]) for k in range(4) if k != i))
            else:
                upper = 1.0
                for k in range(4):
                    if k != i and k != j:
                        upper = upper * (points[i] - points[k])
                lower = 1.0
                for k in range(4):
                    if k != j:
                        lower = lower * (points[j] - points[k])
                derivative[i, j] = upper / lower
    identity = np.eye(4)
    grad_a = np.kron(np.eye(16), derivative)
    grad_b = np.kron(identity, np.kron(derivative, identity))
    grad_c = np.kron(derivative, np.eye(16))
    weight3 = np.kron(weights, np.kron(weights, weights))
    return (jnp.asarray(np.stack([grad_a, grad_b, grad_c]), jnp.float32), jnp.asarray(weight3, jnp.float32))

def shifted(values, offset, keep):
    filler = jnp.zeros_like(values[..., :abs(offset)])
    if offset > 0:
        moved = jnp.concatenate([values[..., offset:], filler], axis=-1)
    else:
        moved = jnp.concatenate([filler, values[..., :offset]], axis=-1)
    return jnp.where(keep, moved, jnp.zeros_like(moved))

def assemble_axis(grid, axis, stride, first, last):
    low = jnp.take(grid, 0, axis=axis)
    high = jnp.take(grid, 3, axis=axis)
    new_low = low + shifted(high, -stride, jnp.logical_not(first))
    new_high = high + shifted(low, stride, jnp.logical_not(last))
    middle = lax.slice_in_dim(grid, 1, 3, axis=axis)
    return jnp.concatenate([jnp.expand_dims(new_low, axis), middle, jnp.expand_dims(new_high, axis)], axis=axis)

def assemble(field):
    count = field.shape[0]
    elements = field.shape[-1]
    cells = EX * EY
    depth = elements // cells
    element = jnp.arange(elements, dtype=jnp.int32)
    col_x = element % EX
    col_y = element // EX % EY
    col_z = element // cells
    grid = field.reshape(count, 4, 4, 4, elements)
    grid = assemble_axis(grid, 3, 1, col_x == 0, col_x == EX - 1)
    grid = assemble_axis(grid, 2, EX, col_y == 0, col_y == EY - 1)
    grid = assemble_axis(grid, 1, cells, col_z == 0, col_z == depth - 1)
    return grid.reshape(count, 64, elements)

def reference(fwd_now, fwd_prev, adj_now, adj_prev, shear_mod, density, station_owner, receiver_local, station_weights, adj_records):
    grad_ops, weight3 = element_tables()
    elements = fwd_now.shape[-1]
    stiff = weight3[:, None] * shear_mod
    mass = assemble((weight3[:, None] * density[None, :])[None])[0]
    global_elem = (station_owner[:, 0] * (EX * EY * LAYERS) + receiver_local).astype(jnp.int32)
    high = lax.Precision.HIGHEST

    def per_event(kern, inputs):
        fwd_a, fwd_b, adj_a, adj_b, record = inputs
        source = jnp.zeros((STEPS, 64, elements), jnp.float32).at[:, :, global_elem].add(record[:, None, :] * station_weights[None, :, :])
        now = jnp.stack([fwd_a, adj_a])
        before = jnp.stack([fwd_b, adj_b])
        for step in range(STEPS):
            grads = jnp.einsum('dnm,fme->dfne', grad_ops, now, precision=high)
            kern = kern - TIME_STEP * stiff * lax.optimization_barrier(jnp.sum(grads[:, 0] * grads[:, 1], axis=0))
            local = jnp.einsum('dnm,dfne->fme', grad_ops, grads * stiff[None, None], precision=high)
            local = local - jnp.stack([jnp.zeros_like(source[step]), source[step]])
            after = 2.0 * now - before - STEP_SQUARE * assemble(local) / mass[None]
            before = now
            now = after
        return (kern, (now[0], before[0], now[1], before[1]))
    kern, outs = lax.scan(per_event, jnp.zeros((64, elements), jnp.float32), (fwd_now, fwd_prev, adj_now, adj_prev, adj_records))
    return (outs[0], outs[1], outs[2], outs[3], kern)
```

```python
import functools

import jax
import jax.numpy as jnp
import numpy as np
from jax import lax
from jax.experimental import pallas as pl
from jax.experimental.pallas import tpu as pltpu
from jax.sharding import PartitionSpec as P

EX = 16
EY = 16
STEPS = 2
CAP = 256
NODES = 64
SUB = 8
LANE = 128
FIELD = NODES * SUB
FACE = 4 * SUB


TIME_STEP = 0.08
STEP_SQUARE = 0.0064

EDGE = np.array([1.0 / 6.0, 5.0 / 6.0, 5.0 / 6.0, 1.0 / 6.0])
WEIGHT = [float(np.float32(EDGE[n // 16] * EDGE[n // 4 % 4] * EDGE[n % 4])) for n in range(NODES)]
ROOT5 = float(np.sqrt(5.0))

LINES = (
    [[16 * c + 4 * b + i for i in range(4)] for c in range(4) for b in range(4)],
    [[16 * c + 4 * i + a for i in range(4)] for c in range(4) for a in range(4)],
    [[16 * i + 4 * b + a for i in range(4)] for b in range(4) for a in range(4)],
)


def derive(x0, x1, x2, x3):
    o0, o1 = x0 - x3, x1 - x2
    q = (x1 + x2) - (x0 + x3)
    a0, a1 = 1.25 * q, (0.25 * ROOT5) * q
    b0 = -1.75 * o0 + (1.25 * ROOT5) * o1
    b1 = -0.25 * o0 - (0.25 * ROOT5) * o1
    return b0 + a0, b1 + a1, b1 - a1, b0 - a0


def derive_transposed(h0, h1, h2, h3):
    p0, m0, p1, m1 = h0 + h3, h0 - h3, h1 + h2, h1 - h2
    q = 1.25 * m0 + (0.25 * ROOT5) * m1
    o0 = -1.75 * p0 - 0.25 * p1
    o1 = (1.25 * ROOT5) * p0 - (0.25 * ROOT5) * p1
    return o0 - q, o1 + q, q - o1, -o0 - q


def at(ref, base, node):
    if isinstance(base, int):
        return ref.at[pl.ds(base + node * SUB, SUB), :]
    return ref.at[pl.ds(pl.multiple_of(base, SUB) + node * SUB, SUB), :]


def spread(src_ref, index, dst_ref, base):
    for k in range(SUB):
        block = src_ref[:, k * LANE : (k + 1) * LANE] if index is None else src_ref[index, :, k * LANE : (k + 1) * LANE]
        dst_ref[pl.ds(base + k, NODES, stride=SUB), :] = block


def gather_back(src_ref, base, dst_ref, index):
    for k in range(SUB):
        dst_ref[index, :, k * LANE : (k + 1) * LANE] = src_ref[pl.ds(base + k, NODES, stride=SUB), :]


def places():
    lane = lax.broadcasted_iota(jnp.int32, (SUB, LANE), 1)
    sub = lax.broadcasted_iota(jnp.int32, (SUB, LANE), 0)
    return lane, sub


def assemble(ref, base):
    lane, sub = places()
    zero = jnp.zeros((SUB, LANE), jnp.float32)
    not_first = lane % EX != 0
    not_last = lane % EX != EX - 1
    odd = sub % 2 == 1
    for c in range(4):
        for b in range(4):
            n = 16 * c + 4 * b
            low_at, high_at = at(ref, base, n), at(ref, base, n + 3)
            low, high = low_at[...], high_at[...]
            low_at[...] = low + jnp.where(not_first, pltpu.roll(high, 1, 1), zero)
            high_at[...] = high + jnp.where(not_last, pltpu.roll(low, LANE - 1, 1), zero)
    for c in range(4):
        for a in range(4):
            n = 16 * c + a
            low_at, high_at = at(ref, base, n), at(ref, base, n + 12)
            low, high = low_at[...], high_at[...]
            back = pltpu.roll(high, EX, 1)
            ahead = pltpu.roll(low, LANE - EX, 1)
            back = jnp.where(lane >= EX, back, jnp.where(odd, pltpu.roll(back, 1, 0), zero))
            ahead = jnp.where(lane < LANE - EX, ahead, jnp.where(odd, zero, pltpu.roll(ahead, SUB - 1, 0)))
            low_at[...] = low + back
            high_at[...] = high + ahead
    for n in range(16):
        low_at, high_at = at(ref, base, n), at(ref, base, n + 48)
        low, high = low_at[...], high_at[...]
        low_at[...] = low + jnp.where(sub >= 2, pltpu.roll(high, 2, 0), zero)
        high_at[...] = high + jnp.where(sub < SUB - 2, pltpu.roll(low, SUB - 2, 0), zero)


def roll_sub(value, shift):
    shift = shift % SUB
    return value if shift == 0 else pltpu.roll(value, shift, 0)


def pack_faces(ref, base, low_ref, high_ref, out_base):
    _, sub = places()
    for b in range(4):
        for target, first, shift in ((low_ref, 0, 0), (high_ref, 48, 2)):
            pieces = [roll_sub(at(ref, base, first + 4 * b + a)[...], 2 * a + shift) for a in range(4)]
            tile = jnp.where(
                sub < 4,
                jnp.where(sub < 2, pieces[0], pieces[1]),
                jnp.where(sub < 6, pieces[2], pieces[3]),
            )
            at(target, out_base, b)[...] = tile


def with_rim(value, node, low_ref, high_ref, rim_base):
    _, sub = places()
    zero = jnp.zeros((SUB, LANE), jnp.float32)
    c, b, a = node // 16, node // 4 % 4, node % 4
    if c == 0:
        return value + jnp.where(sub < 2, roll_sub(at(low_ref, rim_base, b)[...], -2 * a), zero)
    if c == 3:
        return value + jnp.where(sub >= 6, roll_sub(at(high_ref, rim_base, b)[...], 6 - 2 * a), zero)
    return value


def stiffness(ins, outs, stiff_ref, kern):
    for dim, lines in enumerate(LINES):
        for line in lines:
            stiff = [at(stiff_ref, 0, n)[...] for n in line]
            grads = []
            for (src, sbase), out in zip(ins, outs):
                g = derive(*[at(src, sbase, n)[...] for n in line])
                grads.append(g)
                if out is None:
                    continue
                dst, dbase = out
                back = derive_transposed(*[x * s for x, s in zip(g, stiff)])
                for n, x in zip(line, back):
                    place = at(dst, dbase, n)
                    place[...] = x if dim == 0 else place[...] + x
            if kern is not None:
                for i, n in enumerate(line):
                    place = at(kern, 0, n)
                    place[...] = place[...] + grads[0][i] * grads[1][i]


def place_kernel(owner_ref, local_ref, weights_ref, records_ref, out_ref, rank_ref, data_ref):
    stations = weights_ref.shape[1]
    slabs, rows, _ = out_ref.shape
    blocks = stations // LANE
    owner_id = lax.broadcasted_iota(jnp.int32, (slabs, LANE), 0)
    before = lax.broadcasted_iota(jnp.int32, (LANE, LANE), 0) < lax.broadcasted_iota(jnp.int32, (LANE, LANE), 1)
    counting = jnp.concatenate(
        [jnp.where(before, 1.0, 0.0), jnp.ones((LANE, LANE), jnp.float32)], axis=1
    ).astype(jnp.bfloat16)
    named = [jnp.where(owner_ref[b : b + 1, :] == owner_id, 1.0, 0.0) for b in range(blocks)]
    counts = jnp.dot(
        jnp.concatenate(named, axis=0).astype(jnp.bfloat16), counting, preferred_element_type=jnp.float32
    )
    total = jnp.zeros((slabs, LANE), jnp.float32)
    for b in range(blocks):
        part = counts[b * slabs : (b + 1) * slabs]
        rank_ref[b : b + 1, :] = jnp.sum(named[b] * (part[:, :LANE] + total), axis=0, keepdims=True)
        total = total + part[:, LANE:]
    extra = rows - weights_ref.shape[0] - records_ref.shape[0]
    for b in range(blocks):
        cut = slice(b * LANE, (b + 1) * LANE)
        ids = jnp.broadcast_to(local_ref[b : b + 1, :].astype(jnp.float32), (extra, LANE))
        full = jnp.concatenate([weights_ref[:, cut], records_ref[:, cut], ids], axis=0)
        high = full.astype(jnp.bfloat16)
        data_ref[:rows, cut] = high
        data_ref[rows:, cut] = (full - high.astype(jnp.float32)).astype(jnp.bfloat16)
    slot = lax.broadcasted_iota(jnp.int32, (CAP, LANE), 0).astype(jnp.bfloat16)

    def one(slab, _):
        hot = []
        for b in range(blocks):
            wanted = jnp.where(owner_ref[b : b + 1, :] == slab, rank_ref[b : b + 1, :], -1.0).astype(jnp.bfloat16)
            hot.append(jnp.where(slot == wanted, jnp.bfloat16(1), jnp.bfloat16(0)))
        placed = lax.dot_general(
            data_ref[...],
            jnp.concatenate(hot, axis=1),
            (((1,), (1,)), ((), ())),
            preferred_element_type=jnp.float32,
        )
        out_ref[slab] = placed[:rows] + placed[rows:]
        return 0

    lax.fori_loop(0, slabs, one, 0)


def land(got_ref, step, events, out_ref, acc_ref):
    slabs = got_ref.shape[0]
    group = 4
    half = events * NODES
    slot = lax.broadcasted_iota(jnp.int32, (CAP, LANE), 0).astype(jnp.bfloat16)
    acc_ref[...] = jnp.zeros_like(acc_ref)

    def one(g, _):
        left, hot = [], [[] for _ in range(4)]
        for i in range(group):
            src = g * group + i
            weights = got_ref[src, :NODES, :]
            parts = []
            for event in range(events):
                row = NODES + event * STEPS + step
                parts.append(weights * got_ref[src, row : row + 1, :])
            full = jnp.concatenate(parts, axis=0)
            high = full.astype(jnp.bfloat16)
            low = (full - high.astype(jnp.float32)).astype(jnp.bfloat16)
            left.append(jnp.concatenate([high, low], axis=0))
            ids = got_ref[src, NODES + events * STEPS : NODES + events * STEPS + 1, :].astype(jnp.int32)
            for q in range(4):
                for cut in (slice(0, LANE), slice(LANE, 2 * LANE)):
                    wanted = jnp.where(ids[:, cut] // CAP == q, ids[:, cut] % CAP, -1).astype(jnp.float32).astype(jnp.bfloat16)
                    hot[q].append(jnp.where(slot == wanted, jnp.bfloat16(1), jnp.bfloat16(0)))
        left = jnp.concatenate(left, axis=1)
        for q in range(4):
            landed = lax.dot_general(
                left,
                jnp.concatenate(hot[q], axis=1),
                (((1,), (1,)), ((), ())),
                preferred_element_type=jnp.float32,
            )
            cut = slice(q * CAP, (q + 1) * CAP)
            acc_ref[:, cut] += landed[:half] + landed[half:]
        return 0

    lax.fori_loop(0, slabs // group, one, 0)
    for event in range(events):
        for k in range(SUB):
            out_ref[pl.ds(event * FIELD + k, NODES, stride=SUB), :] = acc_ref[
                event * NODES : (event + 1) * NODES, k * LANE : (k + 1) * LANE
            ]


def land_first_kernel(events, got_ref, out_ref, low_ref, high_ref, acc_ref):
    land(got_ref, 0, events, out_ref, acc_ref)
    for event in range(events):
        assemble(out_ref, event * FIELD)
        pack_faces(out_ref, event * FIELD, low_ref, high_ref, event * FACE)


def land_later_kernel(events, got_ref, out_ref, acc_ref):
    land(got_ref, 1, events, out_ref, acc_ref)


def first_kernel(events, fwd_ref, adj_ref, shear_ref, density_ref, _, fields_ref, stiff_ref, kern_ref, low_ref, high_ref, in_ref):
    spread(shear_ref, None, stiff_ref, 0)
    for n in range(NODES):
        place = at(stiff_ref, 0, n)
        place[...] = place[...] * WEIGHT[n]
        at(kern_ref, 0, n)[...] = jnp.zeros((SUB, LANE), jnp.float32)
        at(fields_ref, 2 * events * FIELD, n)[...] = density_ref[...] * WEIGHT[n]

    def one(event, _):
        u, v = event * FIELD, (events + event) * FIELD
        spread(fwd_ref, event, in_ref, 0)
        spread(adj_ref, event, in_ref, FIELD)
        stiffness([(in_ref, 0), (in_ref, FIELD)], [(fields_ref, u), (fields_ref, v)], stiff_ref, kern_ref)
        return 0

    lax.fori_loop(0, events, one, 0)

    def join(field, _):
        assemble(fields_ref, field * FIELD)
        pack_faces(fields_ref, field * FIELD, low_ref, high_ref, field * FACE)
        return 0

    lax.fori_loop(0, 2 * events + 1, join, 0)


def second_kernel(
    events, fwd_ref, fwd_prev_ref, adj_ref, adj_prev_ref, fields_ref, stiff_ref, rim_low_ref, rim_high_ref,
    fwd_out_ref, now_ref, factor_ref, next_ref, low_ref, high_ref, in_ref, prev_ref,
):
    for n in range(NODES):
        mass = with_rim(at(fields_ref, 2 * events * FIELD, n)[...], n, rim_low_ref, rim_high_ref, 2 * events * FACE)
        at(factor_ref, 0, n)[...] = STEP_SQUARE / mass

    def step(event, now_src, prev_src, field):
        spread(now_src, event, in_ref, 0)
        spread(prev_src, event, prev_ref, 0)
        for n in range(NODES):
            force = with_rim(at(fields_ref, field * FIELD, n)[...], n, rim_low_ref, rim_high_ref, field * FACE)
            at(now_ref, field * FIELD, n)[...] = (
                2.0 * at(in_ref, 0, n)[...] - at(prev_ref, 0, n)[...] - at(factor_ref, 0, n)[...] * force
            )

    def one(event, _):
        step(event, fwd_ref, fwd_prev_ref, event)
        step(event, adj_ref, adj_prev_ref, events + event)
        gather_back(now_ref, event * FIELD, fwd_out_ref, event)
        stiffness([(now_ref, event * FIELD)], [(next_ref, event * FIELD)], stiff_ref, None)
        assemble(next_ref, event * FIELD)
        pack_faces(next_ref, event * FIELD, low_ref, high_ref, event * FACE)
        return 0

    lax.fori_loop(0, events, one, 0)


def last_kernel(events, first, prev_ref, now_ref, factor_ref, next_ref, rim_low_ref, rim_high_ref, *rest):
    if first:
        out_ref, in_ref, done_ref = rest
    else:
        parts, (out_ref, kernel_ref, in_ref, done_ref) = rest[:-4], rest[-4:]
        total = parts[0][0]
        for part in parts[1:]:
            total = total + part[0]
        kernel_ref[...] = total

    def one(event, _):
        spread(prev_ref, event, in_ref, 0)
        for n in range(NODES):
            force = with_rim(at(next_ref, event * FIELD, n)[...], n, rim_low_ref, rim_high_ref, event * FACE)
            at(done_ref, 0, n)[...] = (
                2.0 * at(now_ref, event * FIELD, n)[...] - at(in_ref, 0, n)[...] - at(factor_ref, 0, n)[...] * force
            )
        gather_back(done_ref, 0, out_ref, event)
        return 0

    lax.fori_loop(0, events, one, 0)


def third_kernel(
    events, share, position_ref, now_ref, factor_ref, stiff_ref, kern_in_ref, source_ref, later_ref, rim_low_ref, rim_high_ref,
    adj_out_ref, adj_now_ref, next_ref, parts_ref, low_ref, high_ref, kern_ref,
):
    kern_ref[...] = kern_in_ref[...]

    def one(event, _):
        here = event * FIELD
        for n in range(NODES):
            source = with_rim(at(source_ref, here, n)[...], n, rim_low_ref, rim_high_ref, event * FACE)
            at(adj_now_ref, here, n)[...] = at(now_ref, (events + event) * FIELD, n)[...] + at(factor_ref, 0, n)[...] * source
        gather_back(adj_now_ref, here, adj_out_ref, event)
        stiffness([(now_ref, here), (adj_now_ref, here)], [None, (next_ref, here)], stiff_ref, kern_ref)
        for n in range(NODES):
            place = at(next_ref, here, n)
            place[...] = place[...] - at(later_ref, here, n)[...]
        assemble(next_ref, here)
        pack_faces(next_ref, here, low_ref, high_ref, event * FACE)
        return 0

    lax.fori_loop(0, events, one, 0)
    for n in range(NODES):
        place = at(kern_ref, 0, n)
        place[...] = -TIME_STEP * at(stiff_ref, 0, n)[...] * place[...]
    tiles = SUB // share
    for j in range(share):
        owner = lax.rem(position_ref[0] + j, share)
        for k in range(tiles):
            parts_ref[j, :, k * LANE : (k + 1) * LANE] = kern_ref[pl.ds(owner * tiles + k, NODES, stride=SUB), :]


def call(body, outs, scratch=(), cost=2_000_000, smem=0, count=0):
    in_specs = [pl.BlockSpec(memory_space=pltpu.SMEM)] * smem + [pl.BlockSpec(memory_space=pltpu.VMEM)] * (count - smem)
    return pl.pallas_call(
        body,
        out_shape=[jax.ShapeDtypeStruct(shape, jnp.float32) for shape in outs],
        in_specs=in_specs,
        out_specs=[pl.BlockSpec(memory_space=pltpu.VMEM)] * len(outs),
        scratch_shapes=[pltpu.VMEM(shape, dtype) for shape, dtype in scratch],
        compiler_params=pltpu.CompilerParams(vmem_limit_bytes=24 * 1024 * 1024),
        cost_estimate=pl.CostEstimate(flops=cost, bytes_accessed=cost, transcendentals=0),
    )


def beside(low, high):
    count = lax.axis_size("space")
    from_before = lax.ppermute(high, "space", [(i, i + 1) for i in range(count - 1)])
    from_after = lax.ppermute(low, "space", [(i + 1, i) for i in range(count - 1)])
    return from_before, from_after


def shards(
    fwd_now,
    fwd_prev,
    adj_now,
    adj_prev,
    shear_mod,
    density,
    station_owner,
    receiver_local,
    station_weights,
    adj_records,
):
    events = fwd_now.shape[0]
    stations = station_owner.shape[0]
    elements = fwd_now.shape[-1]
    slabs = lax.axis_size("space")
    share = lax.axis_size("event")
    f32 = jnp.float32
    rows = -(-(NODES + events * STEPS + 1) // SUB) * SUB
    blocks = stations // LANE

    send = call(
        place_kernel,
        [(slabs, rows, CAP)],
        [((blocks, LANE), f32), ((2 * rows, stations), jnp.bfloat16)],
        count=4,
    )(
        station_owner.reshape(blocks, LANE),
        receiver_local.reshape(blocks, LANE),
        station_weights,
        adj_records.reshape(events * STEPS, stations),
    )[0]
    got = lax.all_to_all(send, "space", split_axis=0, concat_axis=0, tiled=True)

    fields, stiff, kern, low, high = call(
        functools.partial(first_kernel, events),
        [
            ((2 * events + 1) * FIELD, LANE),
            (FIELD, LANE),
            (FIELD, LANE),
            ((2 * events + 1) * FACE, LANE),
            ((2 * events + 1) * FACE, LANE),
        ],
        [((2 * FIELD, LANE), f32)],
        count=5,
    )(fwd_now, adj_now, shear_mod, density.reshape(SUB, LANE), send[0, :8, :128])
    rim_low, rim_high = beside(low, high)
    fwd_before, now, factor, fwd_next, low, high = call(
        functools.partial(second_kernel, events),
        [
            fwd_now.shape,
            (2 * events * FIELD, LANE),
            (FIELD, LANE),
            (events * FIELD, LANE),
            (events * FACE, LANE),
            (events * FACE, LANE),
        ],
        [((FIELD, LANE), f32), ((FIELD, LANE), f32)],
        count=8,
    )(fwd_now, fwd_prev, adj_now, adj_prev, fields, stiff, rim_low, rim_high)
    rim_low, rim_high = beside(low, high)
    fwd_last = call(
        functools.partial(last_kernel, events, True),
        [fwd_now.shape],
        [((FIELD, LANE), f32), ((FIELD, LANE), f32)],
        count=6,
    )(fwd_now, now, factor, fwd_next, rim_low, rim_high)[0]

    source, low, high = call(
        functools.partial(land_first_kernel, events),
        [(events * FIELD, LANE), (events * FACE, LANE), (events * FACE, LANE)],
        [((events * NODES, elements), f32)],
        count=1,
    )(got)
    rim_low, rim_high = beside(low, high)
    later = call(
        functools.partial(land_later_kernel, events),
        [(events * FIELD, LANE)],
        [((events * NODES, elements), f32)],
        count=1,
    )(got)[0]
    adj_before, adj_mid, adj_next, parts, low, high = call(
        functools.partial(third_kernel, events, share),
        [
            adj_now.shape,
            (events * FIELD, LANE),
            (events * FIELD, LANE),
            (share, NODES, elements // share),
            (events * FACE, LANE),
            (events * FACE, LANE),
        ],
        [((FIELD, LANE), f32)],
        smem=1,
        count=9,
    )(
        lax.axis_index("event").reshape(1).astype(jnp.int32),
        now, factor, stiff, kern, source, later, rim_low, rim_high,
    )
    rim_low, rim_high = beside(low, high)
    pieces = [parts[0:1]] + [
        lax.ppermute(parts[j : j + 1], "event", [(i, (i + j) % share) for i in range(share)]) for j in range(1, share)
    ]
    adj_last, kernel = call(
        functools.partial(last_kernel, events, False),
        [adj_now.shape, (NODES, elements // share)],
        [((FIELD, LANE), f32), ((FIELD, LANE), f32)],
        count=6 + share,
    )(adj_now, adj_mid, factor, adj_next, rim_low, rim_high, *pieces)
    return fwd_last, fwd_before, adj_last, adj_before, kernel


def solution(mesh):
    in_specs = (
        P("event", None, "space"),
        P("event", None, "space"),
        P("event", None, "space"),
        P("event", None, "space"),
        P(None, "space"),
        P("space"),
        P("space", None),
        P("space"),
        P(None, "space"),
        P("event", None, "space"),
    )
    out_specs = (
        P("event", None, "space"),
        P("event", None, "space"),
        P("event", None, "space"),
        P("event", None, "space"),
        P(None, ("space", "event")),
    )
    return jax.shard_map(shards, mesh=mesh, in_specs=in_specs, out_specs=out_specs, check_vma=False)
```

```python
import functools

import jax
import jax.numpy as jnp
import numpy as np
from jax import lax
from jax.experimental import pallas as pl
from jax.experimental.pallas import tpu as pltpu
from jax.sharding import PartitionSpec as P

EX = 16
EY = 16
STEPS = 2
CAP = 256
NODES = 64
SUB = 8
LANE = 128
FIELD = NODES * SUB
FACE = 4 * SUB
LAND_LIMIT = 24


TIME_STEP = 0.08
STEP_SQUARE = 0.0064

EDGE = np.array([1.0 / 6.0, 5.0 / 6.0, 5.0 / 6.0, 1.0 / 6.0])
WEIGHT = [float(np.float32(EDGE[n // 16] * EDGE[n // 4 % 4] * EDGE[n % 4])) for n in range(NODES)]
ROOT5 = float(np.sqrt(5.0))

LINES = (
    [[16 * c + 4 * b + i for i in range(4)] for c in range(4) for b in range(4)],
    [[16 * c + 4 * i + a for i in range(4)] for c in range(4) for a in range(4)],
    [[16 * i + 4 * b + a for i in range(4)] for b in range(4) for a in range(4)],
)


def derive(x0, x1, x2, x3):
    o0, o1 = x0 - x3, x1 - x2
    q = (x1 + x2) - (x0 + x3)
    a0, a1 = 1.25 * q, (0.25 * ROOT5) * q
    b0 = -1.75 * o0 + (1.25 * ROOT5) * o1
    b1 = -0.25 * o0 - (0.25 * ROOT5) * o1
    return b0 + a0, b1 + a1, b1 - a1, b0 - a0


def derive_transposed(h0, h1, h2, h3):
    p0, m0, p1, m1 = h0 + h3, h0 - h3, h1 + h2, h1 - h2
    q = 1.25 * m0 + (0.25 * ROOT5) * m1
    o0 = -1.75 * p0 - 0.25 * p1
    o1 = (1.25 * ROOT5) * p0 - (0.25 * ROOT5) * p1
    return o0 - q, o1 + q, q - o1, -o0 - q


def at(ref, base, node):
    if isinstance(base, int):
        return ref.at[pl.ds(base + node * SUB, SUB), :]
    return ref.at[pl.ds(pl.multiple_of(base, SUB) + node * SUB, SUB), :]


def spread(src_ref, index, dst_ref, base):
    for k in range(SUB):
        block = src_ref[:, k * LANE : (k + 1) * LANE] if index is None else src_ref[index, :, k * LANE : (k + 1) * LANE]
        dst_ref[pl.ds(base + k, NODES, stride=SUB), :] = block


def gather_back(src_ref, base, dst_ref, index):
    for k in range(SUB):
        dst_ref[index, :, k * LANE : (k + 1) * LANE] = src_ref[pl.ds(base + k, NODES, stride=SUB), :]


def places():
    lane = lax.broadcasted_iota(jnp.int32, (SUB, LANE), 1)
    sub = lax.broadcasted_iota(jnp.int32, (SUB, LANE), 0)
    return lane, sub


def assemble(ref, base):
    lane, sub = places()
    zero = jnp.zeros((SUB, LANE), jnp.float32)
    not_first = lane % EX != 0
    not_last = lane % EX != EX - 1
    odd = sub % 2 == 1
    for c in range(4):
        for b in range(4):
            n = 16 * c + 4 * b
            low_at, high_at = at(ref, base, n), at(ref, base, n + 3)
            low, high = low_at[...], high_at[...]
            low_at[...] = low + jnp.where(not_first, pltpu.roll(high, 1, 1), zero)
            high_at[...] = high + jnp.where(not_last, pltpu.roll(low, LANE - 1, 1), zero)
    for c in range(4):
        for a in range(4):
            n = 16 * c + a
            low_at, high_at = at(ref, base, n), at(ref, base, n + 12)
            low, high = low_at[...], high_at[...]
            back = pltpu.roll(high, EX, 1)
            ahead = pltpu.roll(low, LANE - EX, 1)
            back = jnp.where(lane >= EX, back, jnp.where(odd, pltpu.roll(back, 1, 0), zero))
            ahead = jnp.where(lane < LANE - EX, ahead, jnp.where(odd, zero, pltpu.roll(ahead, SUB - 1, 0)))
            low_at[...] = low + back
            high_at[...] = high + ahead
    for n in range(16):
        low_at, high_at = at(ref, base, n), at(ref, base, n + 48)
        low, high = low_at[...], high_at[...]
        low_at[...] = low + jnp.where(sub >= 2, pltpu.roll(high, 2, 0), zero)
        high_at[...] = high + jnp.where(sub < SUB - 2, pltpu.roll(low, SUB - 2, 0), zero)


def roll_sub(value, shift):
    shift = shift % SUB
    return value if shift == 0 else pltpu.roll(value, shift, 0)


def is_even():
    return lax.rem(lax.axis_index("space"), 2) == 0


def pack_faces(ref, base, near_ref, far_ref, out_base):
    _, sub = places()
    even = is_even()
    for b in range(4):
        tiles = []
        for first, shift in ((0, 0), (48, 2)):
            pieces = [roll_sub(at(ref, base, first + 4 * b + a)[...], 2 * a + shift) for a in range(4)]
            tiles.append(
                jnp.where(
                    sub < 4,
                    jnp.where(sub < 2, pieces[0], pieces[1]),
                    jnp.where(sub < 6, pieces[2], pieces[3]),
                )
            )
        low, high = tiles
        at(near_ref, out_base, b)[...] = jnp.where(even, high, low)
        at(far_ref, out_base, b)[...] = jnp.where(even, low, high)


def with_rim(value, node, near_ref, far_ref, rim_base):
    _, sub = places()
    zero = jnp.zeros((SUB, LANE), jnp.float32)
    c, b, a = node // 16, node // 4 % 4, node % 4
    if c not in (0, 3):
        return value
    near, far = at(near_ref, rim_base, b)[...], at(far_ref, rim_base, b)[...]
    if c == 0:
        return value + jnp.where(sub < 2, roll_sub(jnp.where(is_even(), far, near), -2 * a), zero)
    return value + jnp.where(sub >= 6, roll_sub(jnp.where(is_even(), near, far), 6 - 2 * a), zero)


def stiffness(ins, outs, stiff_ref, kern):
    for dim, lines in enumerate(LINES):
        for line in lines:
            stiff = [at(stiff_ref, 0, n)[...] for n in line]
            grads = []
            for (src, sbase), out in zip(ins, outs):
                g = derive(*[at(src, sbase, n)[...] for n in line])
                grads.append(g)
                if out is None:
                    continue
                dst, dbase = out
                back = derive_transposed(*[x * s for x, s in zip(g, stiff)])
                for n, x in zip(line, back):
                    place = at(dst, dbase, n)
                    place[...] = x if dim == 0 else place[...] + x
            if kern is not None:
                for i, n in enumerate(line):
                    place = at(kern, 0, n)
                    place[...] = place[...] + grads[0][i] * grads[1][i]


def place_kernel(
    owner_hbm, local_hbm, weights_hbm, records_hbm, out_ref, token_ref,
    owner_ref, local_ref, weights_ref, records_ref, spot_ref, data_ref, sorted_ref, sems,
):
    copies = [
        pltpu.make_async_copy(src, dst, sems.at[i])
        for i, (src, dst) in enumerate(
            (
                (owner_hbm, owner_ref),
                (local_hbm, local_ref),
                (weights_hbm, weights_ref),
                (records_hbm, records_ref),
            )
        )
    ]
    for copy in copies:
        copy.start()
    token_ref[...] = jnp.zeros_like(token_ref)
    stations = weights_ref.shape[1]
    slabs, rows, _ = out_ref.shape
    events = records_ref.shape[0]
    blocks = stations // LANE
    chunks = stations // CAP
    owner_id = lax.broadcasted_iota(jnp.int32, (slabs, LANE), 0)
    before = lax.broadcasted_iota(jnp.int32, (LANE, LANE), 0) < lax.broadcasted_iota(jnp.int32, (LANE, LANE), 1)
    counting = jnp.concatenate(
        [jnp.where(before, 1.0, 0.0), jnp.ones((LANE, LANE), jnp.float32)], axis=1
    ).astype(jnp.bfloat16)
    copies[0].wait()
    named = [jnp.where(owner_ref[b : b + 1, :] == owner_id, 1.0, 0.0) for b in range(blocks)]
    counts = jnp.dot(
        jnp.concatenate(named, axis=0).astype(jnp.bfloat16), counting, preferred_element_type=jnp.float32
    )
    total = jnp.zeros((slabs, LANE), jnp.float32)
    earlier = []
    for b in range(blocks):
        part = counts[b * slabs : (b + 1) * slabs]
        earlier.append(part[:, :LANE] + total)
        total = total + part[:, LANE:]
    start = jnp.zeros((1, LANE), jnp.float32)
    starts = []
    for slab in range(slabs):
        starts.append(start)
        start = start + total[slab : slab + 1]
    starts = jnp.concatenate(starts, axis=0)
    for b in range(blocks):
        spot_ref[b : b + 1, :] = jnp.sum(named[b] * (earlier[b] + starts), axis=0, keepdims=True)
    first, count = starts.astype(jnp.int32), total.astype(jnp.int32)
    begins = [first[slab, 0] for slab in range(slabs)]
    sizes = [count[slab, 0] for slab in range(slabs)]
    for copy in copies[1:]:
        copy.wait()
    extra = rows - NODES - events * STEPS
    for b in range(blocks):
        cut = slice(b * LANE, (b + 1) * LANE)
        ids = jnp.broadcast_to(local_ref[b : b + 1, :].astype(jnp.float32), (extra, LANE))
        full = jnp.concatenate(
            [weights_ref[:, cut]] + [records_ref[event, :, cut] for event in range(events)] + [ids], axis=0
        )
        high = full.astype(jnp.bfloat16)
        data_ref[:rows, cut] = high
        data_ref[rows:, cut] = (full - high.astype(jnp.float32)).astype(jnp.bfloat16)
    slot = lax.broadcasted_iota(jnp.int32, (CAP, LANE), 0).astype(jnp.bfloat16)
    lane = lax.broadcasted_iota(jnp.int32, (rows, LANE), 1)

    def cut_block(slab):
        begin, size = begins[slab], sizes[slab]
        shift = lax.rem(begin, LANE)
        base = begin - shift
        turn = lax.rem(LANE - shift, LANE)
        turned = [
            pltpu.roll(sorted_ref[:, pl.ds(pl.multiple_of(base + j * LANE, LANE), LANE)], turn, 1) for j in range(3)
        ]
        for j in range(2):
            piece = jnp.where(lane < LANE - shift, turned[j], turned[j + 1])
            out_ref[slab, :, j * LANE : (j + 1) * LANE] = jnp.where(lane + j * LANE < size, piece, 0.0)

    for chunk in range(chunks):
        spots = spot_ref[...] - float(chunk * CAP)
        wanted = jnp.where((spots >= 0.0) & (spots < CAP), spots, -1.0)
        hot = [
            jnp.where(slot == wanted[b : b + 1, :].astype(jnp.bfloat16), jnp.bfloat16(1), jnp.bfloat16(0))
            for b in range(blocks)
        ]
        placed = lax.dot_general(
            data_ref[...],
            jnp.concatenate(hot, axis=1),
            (((1,), (1,)), ((), ())),
            preferred_element_type=jnp.float32,
        )
        sorted_ref[:, chunk * CAP : (chunk + 1) * CAP] = placed[:rows] + placed[rows:]
        cut_block(chunk)
    for slab in range(chunks, slabs):
        cut_block(slab)


def land(got_ref, step, events, out_ref, acc_ref):
    slabs = got_ref.shape[0]
    group = 4
    half = events * NODES
    slot = lax.broadcasted_iota(jnp.int32, (CAP, LANE), 0).astype(jnp.bfloat16)
    acc_ref[...] = jnp.zeros_like(acc_ref)

    def one(g, _):
        left, hot = [], [[] for _ in range(4)]
        for i in range(group):
            src = g * group + i
            weights = got_ref[src, :NODES, :]
            parts = []
            for event in range(events):
                row = NODES + event * STEPS + step
                parts.append(weights * got_ref[src, row : row + 1, :])
            full = jnp.concatenate(parts, axis=0)
            high = full.astype(jnp.bfloat16)
            low = (full - high.astype(jnp.float32)).astype(jnp.bfloat16)
            left.append(jnp.concatenate([high, low], axis=0))
            ids = got_ref[src, NODES + events * STEPS : NODES + events * STEPS + 1, :].astype(jnp.int32)
            for q in range(4):
                for cut in (slice(0, LANE), slice(LANE, 2 * LANE)):
                    wanted = jnp.where(ids[:, cut] // CAP == q, ids[:, cut] % CAP, -1).astype(jnp.float32).astype(jnp.bfloat16)
                    hot[q].append(jnp.where(slot == wanted, jnp.bfloat16(1), jnp.bfloat16(0)))
        left = jnp.concatenate(left, axis=1)
        for q in range(4):
            landed = lax.dot_general(
                left,
                jnp.concatenate(hot[q], axis=1),
                (((1,), (1,)), ((), ())),
                preferred_element_type=jnp.float32,
            )
            cut = slice(q * CAP, (q + 1) * CAP)
            acc_ref[:, cut] += landed[:half] + landed[half:]
        return 0

    lax.fori_loop(0, slabs // group, one, 0)
    for event in range(events):
        for k in range(SUB):
            out_ref[pl.ds(event * FIELD + k, NODES, stride=SUB), :] = acc_ref[
                event * NODES : (event + 1) * NODES, k * LANE : (k + 1) * LANE
            ]


def land_first_kernel(
    events, got_ref, fields_hbm, force_ref, near_ref, far_ref, acc_ref, fields_ref, sem
):
    copy = pltpu.make_async_copy(fields_hbm, fields_ref, sem)
    copy.start()
    land(got_ref, 0, events, force_ref, acc_ref)
    copy.wait()
    for event in range(events):
        for n in range(NODES):
            place = at(force_ref, event * FIELD, n)
            place[...] = at(fields_ref, (events + event) * FIELD, n)[...] - place[...]
        assemble(force_ref, event * FIELD)
        pack_faces(force_ref, event * FIELD, near_ref, far_ref, (events + event) * FACE)
        pack_faces(fields_ref, event * FIELD, near_ref, far_ref, event * FACE)
    pack_faces(fields_ref, 2 * events * FIELD, near_ref, far_ref, 2 * events * FACE)


def land_later_kernel(events, got_ref, out_ref, acc_ref):
    land(got_ref, 1, events, out_ref, acc_ref)


def first_kernel(
    events, fwd_ref, fwd_prev_ref, adj_ref, adj_prev_ref, shear_ref, density_ref, _,
    fields_ref, now_ref, base_ref, stiff_ref, kern_ref, prev_ref,
):
    spread(shear_ref, None, stiff_ref, 0)
    mass = 2 * events * FIELD
    for n in range(NODES):
        place = at(stiff_ref, 0, n)
        place[...] = place[...] * WEIGHT[n]
        at(kern_ref, 0, n)[...] = jnp.zeros((SUB, LANE), jnp.float32)
        at(fields_ref, mass, n)[...] = density_ref[...] * WEIGHT[n]
    assemble(fields_ref, mass)

    def one(event, _):
        u, v = event * FIELD, (events + event) * FIELD
        for now_src, prev_src, base in ((fwd_ref, fwd_prev_ref, u), (adj_ref, adj_prev_ref, v)):
            spread(now_src, event, now_ref, base)
            spread(prev_src, event, prev_ref, 0)
            for n in range(NODES):
                at(base_ref, base, n)[...] = 2.0 * at(now_ref, base, n)[...] - at(prev_ref, 0, n)[...]
        stiffness([(now_ref, u), (now_ref, v)], [(fields_ref, u), (fields_ref, v)], stiff_ref, kern_ref)
        assemble(fields_ref, u)
        return 0

    lax.fori_loop(0, events, one, 0)


def second_kernel(
    events, share, position_ref, fields_ref, force_ref, base_ref, stiff_ref, kern_in_ref, later_ref, near_rim_ref, far_rim_ref,
    new_ref, factor_ref, next_ref, parts_ref, near_ref, far_ref, kern_ref,
):
    kern_ref[...] = kern_in_ref[...]
    mass = 2 * events
    for n in range(NODES):
        at(factor_ref, 0, n)[...] = STEP_SQUARE / with_rim(
            at(fields_ref, mass * FIELD, n)[...], n, near_rim_ref, far_rim_ref, mass * FACE
        )

    def one(event, _):
        u, v = event * FIELD, (events + event) * FIELD
        for base, src_ref, src, rim in ((u, fields_ref, u, event), (v, force_ref, u, events + event)):
            for n in range(NODES):
                force = with_rim(at(src_ref, src, n)[...], n, near_rim_ref, far_rim_ref, rim * FACE)
                at(new_ref, base, n)[...] = at(base_ref, base, n)[...] - at(factor_ref, 0, n)[...] * force
        stiffness([(new_ref, u), (new_ref, v)], [(next_ref, u), (next_ref, v)], stiff_ref, kern_ref)
        for n in range(NODES):
            place = at(next_ref, v, n)
            place[...] = place[...] - at(later_ref, u, n)[...]
        assemble(next_ref, u)
        assemble(next_ref, v)
        pack_faces(next_ref, u, near_ref, far_ref, event * FACE)
        pack_faces(next_ref, v, near_ref, far_ref, (events + event) * FACE)
        return 0

    lax.fori_loop(0, events, one, 0)
    for n in range(NODES):
        place = at(kern_ref, 0, n)
        place[...] = -TIME_STEP * at(stiff_ref, 0, n)[...] * place[...]
    tiles = SUB // share
    for j in range(share):
        owner = lax.rem(position_ref[0] + j, share)
        for k in range(tiles):
            parts_ref[j, :, k * LANE : (k + 1) * LANE] = kern_ref[pl.ds(owner * tiles + k, NODES, stride=SUB), :]


def emit_kernel(events, new_ref, now_ref, fwd_out_ref, adj_out_ref, base_ref):
    def one(event, _):
        u, v = event * FIELD, (events + event) * FIELD
        gather_back(new_ref, u, fwd_out_ref, event)
        gather_back(new_ref, v, adj_out_ref, event)
        for base in (u, v):
            for n in range(NODES):
                at(base_ref, base, n)[...] = 2.0 * at(new_ref, base, n)[...] - at(now_ref, base, n)[...]
        return 0

    lax.fori_loop(0, events, one, 0)


def last_kernel(events, share, base_ref, factor_ref, next_ref, near_rim_ref, far_rim_ref, *rest):
    fwd_out_ref, adj_out_ref, kernel_ref, done_ref = rest[share:]
    total = rest[0][0]
    for part in rest[1:share]:
        total = total + part[0]
    kernel_ref[...] = total

    def one(event, _):
        for field, out_ref in ((event, fwd_out_ref), (events + event, adj_out_ref)):
            for n in range(NODES):
                force = with_rim(at(next_ref, field * FIELD, n)[...], n, near_rim_ref, far_rim_ref, field * FACE)
                at(done_ref, 0, n)[...] = at(base_ref, field * FIELD, n)[...] - at(factor_ref, 0, n)[...] * force
            gather_back(done_ref, 0, out_ref, event)
        return 0

    lax.fori_loop(0, events, one, 0)


def call(body, outs, scratch=(), cost=2_000_000, smem=0, count=0, outside=0, limit=24):
    in_specs = [pl.BlockSpec(memory_space=pltpu.SMEM)] * smem
    in_specs += [pl.BlockSpec(memory_space=pltpu.VMEM)] * (count - smem - outside)
    in_specs += [pl.BlockSpec(memory_space=pl.ANY)] * outside
    return pl.pallas_call(
        body,
        out_shape=[jax.ShapeDtypeStruct(shape, jnp.float32) for shape in outs],
        in_specs=in_specs,
        out_specs=[pl.BlockSpec(memory_space=pltpu.VMEM)] * len(outs),
        scratch_shapes=[x if isinstance(x, pltpu.SemaphoreType) or not isinstance(x, tuple) else pltpu.VMEM(*x) for x in scratch],
        compiler_params=pltpu.CompilerParams(vmem_limit_bytes=limit * 1024 * 1024),
        cost_estimate=pl.CostEstimate(flops=cost, bytes_accessed=cost, transcendentals=0),
    )


def beside(near, far):
    count = lax.axis_size("space")
    inner = [pair for i in range(1, count - 1, 2) for pair in ((i, i + 1), (i + 1, i))]
    from_far = lax.ppermute(far, "space", inner)
    from_near = lax.ppermute(near, "space", [(i, i + 1 - 2 * (i % 2)) for i in range(count)])
    return from_near, from_far


def shards(
    fwd_now,
    fwd_prev,
    adj_now,
    adj_prev,
    shear_mod,
    density,
    station_owner,
    receiver_local,
    station_weights,
    adj_records,
):
    events = fwd_now.shape[0]
    stations = station_owner.shape[0]
    elements = fwd_now.shape[-1]
    slabs = lax.axis_size("space")
    share = lax.axis_size("event")
    f32 = jnp.float32
    rows = -(-(NODES + events * STEPS + 1) // SUB) * SUB
    blocks = stations // LANE

    send, token = call(
        place_kernel,
        [(slabs, rows, CAP), (SUB, LANE)],
        [
            ((blocks, LANE), jnp.int32),
            ((blocks, LANE), jnp.int32),
            ((NODES, stations), f32),
            ((events, STEPS, stations), f32),
            ((blocks, LANE), f32),
            ((2 * rows, stations), jnp.bfloat16),
            ((rows, stations + 3 * LANE), f32),
            pltpu.SemaphoreType.DMA((4,)),
        ],
        count=4,
        outside=4,
        limit=63,
    )(
        station_owner.reshape(blocks, LANE),
        receiver_local.reshape(blocks, LANE),
        station_weights,
        adj_records,
    )
    got = lax.all_to_all(send, "space", split_axis=0, concat_axis=0, tiled=True)

    fields, now, base, stiff, kern = call(
        functools.partial(first_kernel, events),
        [
            ((2 * events + 1) * FIELD, LANE),
            (2 * events * FIELD, LANE),
            (2 * events * FIELD, LANE),
            (FIELD, LANE),
            (FIELD, LANE),
        ],
        [((FIELD, LANE), f32)],
        count=7,
    )(fwd_now, fwd_prev, adj_now, adj_prev, shear_mod, density.reshape(SUB, LANE), token)
    force, near, far = call(
        functools.partial(land_first_kernel, events),
        [(events * FIELD, LANE), ((2 * events + 1) * FACE, LANE), ((2 * events + 1) * FACE, LANE)],
        [
            ((events * NODES, elements), f32),
            (((2 * events + 1) * FIELD, LANE), f32),
            pltpu.SemaphoreType.DMA(()),
        ],
        count=2,
        outside=1,
        limit=LAND_LIMIT,
    )(got, fields)
    near_rim, far_rim = beside(near, far)
    later = call(
        functools.partial(land_later_kernel, events),
        [(events * FIELD, LANE)],
        [((events * NODES, elements), f32)],
        count=1,
    )(got)[0]
    new, factor, after, parts, near, far = call(
        functools.partial(second_kernel, events, share),
        [
            (2 * events * FIELD, LANE),
            (FIELD, LANE),
            (2 * events * FIELD, LANE),
            (share, NODES, elements // share),
            (2 * events * FACE, LANE),
            (2 * events * FACE, LANE),
        ],
        [((FIELD, LANE), f32)],
        smem=1,
        count=9,
    )(
        lax.axis_index("event").reshape(1).astype(jnp.int32),
        fields, force, base, stiff, kern, later, near_rim, far_rim,
    )
    near_rim, far_rim = beside(near, far)
    pieces = [parts[0:1]] + [
        lax.ppermute(parts[j : j + 1], "event", [(i, (i + j) % share) for i in range(share)]) for j in range(1, share)
    ]
    fwd_before, adj_before, base = call(
        functools.partial(emit_kernel, events),
        [fwd_now.shape, adj_now.shape, (2 * events * FIELD, LANE)],
        count=2,
    )(new, now)
    fwd_last, adj_last, kernel = call(
        functools.partial(last_kernel, events, share),
        [fwd_now.shape, adj_now.shape, (NODES, elements // share)],
        [((FIELD, LANE), f32)],
        count=5 + share,
    )(base, factor, after, near_rim, far_rim, *pieces)
    return fwd_last, fwd_before, adj_last, adj_before, kernel


def solution(mesh):
    in_specs = (
        P("event", None, "space"),
        P("event", None, "space"),
        P("event", None, "space"),
        P("event", None, "space"),
        P(None, "space"),
        P("space"),
        P("space", None),
        P("space"),
        P(None, "space"),
        P("event", None, "space"),
    )
    out_specs = (
        P("event", None, "space"),
        P("event", None, "space"),
        P("event", None, "space"),
        P("event", None, "space"),
        P(None, ("space", "event")),
    )
    return jax.shard_map(shards, mesh=mesh, in_specs=in_specs, out_specs=out_specs, check_vma=False)
```

```python
import functools

import jax
import jax.numpy as jnp
import numpy as np
from jax import lax
from jax.experimental import pallas as pl
from jax.experimental.pallas import tpu as pltpu
from jax.sharding import PartitionSpec as P

EX = 16
EY = 16
STEPS = 2
CAP = 256
NODES = 64
SUB = 8
LANE = 128
FIELD = NODES * SUB
FACE = 4 * SUB


TIME_STEP = 0.08
STEP_SQUARE = 0.0064

EDGE = np.array([1.0 / 6.0, 5.0 / 6.0, 5.0 / 6.0, 1.0 / 6.0])
WEIGHT = [float(np.float32(EDGE[n // 16] * EDGE[n // 4 % 4] * EDGE[n % 4])) for n in range(NODES)]
ROOT5 = float(np.sqrt(5.0))

LINES = (
    [[16 * c + 4 * b + i for i in range(4)] for c in range(4) for b in range(4)],
    [[16 * c + 4 * i + a for i in range(4)] for c in range(4) for a in range(4)],
    [[16 * i + 4 * b + a for i in range(4)] for b in range(4) for a in range(4)],
)


def derive(x0, x1, x2, x3):
    o0, o1 = x0 - x3, x1 - x2
    q = (x1 + x2) - (x0 + x3)
    a0, a1 = 1.25 * q, (0.25 * ROOT5) * q
    b0 = -1.75 * o0 + (1.25 * ROOT5) * o1
    b1 = -0.25 * o0 - (0.25 * ROOT5) * o1
    return b0 + a0, b1 + a1, b1 - a1, b0 - a0


def derive_transposed(h0, h1, h2, h3):
    p0, m0, p1, m1 = h0 + h3, h0 - h3, h1 + h2, h1 - h2
    q = 1.25 * m0 + (0.25 * ROOT5) * m1
    o0 = -1.75 * p0 - 0.25 * p1
    o1 = (1.25 * ROOT5) * p0 - (0.25 * ROOT5) * p1
    return o0 - q, o1 + q, q - o1, -o0 - q


def at(ref, base, node):
    if isinstance(base, int):
        return ref.at[pl.ds(base + node * SUB, SUB), :]
    return ref.at[pl.ds(pl.multiple_of(base, SUB) + node * SUB, SUB), :]


def spread(src_ref, index, dst_ref, base):
    for k in range(SUB):
        block = src_ref[:, k * LANE : (k + 1) * LANE] if index is None else src_ref[index, :, k * LANE : (k + 1) * LANE]
        dst_ref[pl.ds(base + k, NODES, stride=SUB), :] = block


def gather_back(src_ref, base, dst_ref, index):
    for k in range(SUB):
        dst_ref[index, :, k * LANE : (k + 1) * LANE] = src_ref[pl.ds(base + k, NODES, stride=SUB), :]


def places():
    lane = lax.broadcasted_iota(jnp.int32, (SUB, LANE), 1)
    sub = lax.broadcasted_iota(jnp.int32, (SUB, LANE), 0)
    return lane, sub


def assemble_layers(ref, base, planes):
    lane, sub = places()
    zero = jnp.zeros((SUB, LANE), jnp.float32)
    not_first = lane % EX != 0
    not_last = lane % EX != EX - 1
    odd = sub % 2 == 1
    for c in range(planes):
        for b in range(4):
            n = 16 * c + 4 * b
            low_at, high_at = at(ref, base, n), at(ref, base, n + 3)
            low, high = low_at[...], high_at[...]
            low_at[...] = low + jnp.where(not_first, pltpu.roll(high, 1, 1), zero)
            high_at[...] = high + jnp.where(not_last, pltpu.roll(low, LANE - 1, 1), zero)
    for c in range(planes):
        for a in range(4):
            n = 16 * c + a
            low_at, high_at = at(ref, base, n), at(ref, base, n + 12)
            low, high = low_at[...], high_at[...]
            back = pltpu.roll(high, EX, 1)
            ahead = pltpu.roll(low, LANE - EX, 1)
            back = jnp.where(lane >= EX, back, jnp.where(odd, pltpu.roll(back, 1, 0), zero))
            ahead = jnp.where(lane < LANE - EX, ahead, jnp.where(odd, zero, pltpu.roll(ahead, SUB - 1, 0)))
            low_at[...] = low + back
            high_at[...] = high + ahead


def assemble(ref, base):
    _, sub = places()
    zero = jnp.zeros((SUB, LANE), jnp.float32)
    assemble_layers(ref, base, 4)
    for n in range(16):
        low_at, high_at = at(ref, base, n), at(ref, base, n + 48)
        low, high = low_at[...], high_at[...]
        low_at[...] = low + jnp.where(sub >= 2, pltpu.roll(high, 2, 0), zero)
        high_at[...] = high + jnp.where(sub < SUB - 2, pltpu.roll(low, SUB - 2, 0), zero)


def roll_sub(value, shift):
    shift = shift % SUB
    return value if shift == 0 else pltpu.roll(value, shift, 0)


def is_even():
    return lax.rem(lax.axis_index("space"), 2) == 0


def face_tiles(ref, base, b, low_first, high_first):
    _, sub = places()
    tiles = []
    for first, shift in ((low_first, 0), (high_first, 2)):
        pieces = [roll_sub(at(ref, base, first + 4 * b + a)[...], 2 * a + shift) for a in range(4)]
        tiles.append(
            jnp.where(
                sub < 4, jnp.where(sub < 2, pieces[0], pieces[1]), jnp.where(sub < 6, pieces[2], pieces[3])
            )
        )
    return tiles


def with_rim(value, node, near_ref, far_ref, rim_base):
    _, sub = places()
    zero = jnp.zeros((SUB, LANE), jnp.float32)
    c, b, a = node // 16, node // 4 % 4, node % 4
    if c not in (0, 3):
        return value
    near, far = at(near_ref, rim_base, b)[...], at(far_ref, rim_base, b)[...]
    if c == 0:
        return value + jnp.where(sub < 2, roll_sub(jnp.where(is_even(), far, near), -2 * a), zero)
    return value + jnp.where(sub >= 6, roll_sub(jnp.where(is_even(), near, far), 6 - 2 * a), zero)


def stiffness(ins, outs, stiff_ref, kern):
    for dim, lines in enumerate(LINES):
        for line in lines:
            stiff = [at(stiff_ref, 0, n)[...] for n in line]
            grads = []
            for (src, sbase), out in zip(ins, outs):
                g = derive(*[at(src, sbase, n)[...] for n in line])
                grads.append(g)
                if out is None:
                    continue
                dst, dbase = out
                back = derive_transposed(*[x * s for x, s in zip(g, stiff)])
                for n, x in zip(line, back):
                    place = at(dst, dbase, n)
                    place[...] = x if dim == 0 else place[...] + x
            if kern is not None:
                for i, n in enumerate(line):
                    place = at(kern, 0, n)
                    place[...] = place[...] + grads[0][i] * grads[1][i]


def place_kernel(
    owner_hbm, local_hbm, weights_hbm, records_hbm, out_ref, token_ref,
    owner_ref, local_ref, weights_ref, records_ref, spot_ref, data_ref, sorted_ref, sems,
):
    copies = [
        pltpu.make_async_copy(src, dst, sems.at[i])
        for i, (src, dst) in enumerate(
            (
                (owner_hbm, owner_ref),
                (local_hbm, local_ref),
                (weights_hbm, weights_ref),
                (records_hbm, records_ref),
            )
        )
    ]
    for copy in copies:
        copy.start()
    token_ref[...] = jnp.zeros_like(token_ref)
    stations = weights_ref.shape[1]
    slabs, rows, _ = out_ref.shape
    events = records_ref.shape[0]
    blocks = stations // LANE
    chunks = stations // CAP
    owner_id = lax.broadcasted_iota(jnp.int32, (slabs, LANE), 0)
    before = lax.broadcasted_iota(jnp.int32, (LANE, LANE), 0) < lax.broadcasted_iota(jnp.int32, (LANE, LANE), 1)
    counting = jnp.concatenate(
        [jnp.where(before, 1.0, 0.0), jnp.ones((LANE, LANE), jnp.float32)], axis=1
    ).astype(jnp.bfloat16)
    copies[0].wait()
    named = [jnp.where(owner_ref[b : b + 1, :] == owner_id, 1.0, 0.0) for b in range(blocks)]
    counts = jnp.dot(
        jnp.concatenate(named, axis=0).astype(jnp.bfloat16), counting, preferred_element_type=jnp.float32
    )
    total = jnp.zeros((slabs, LANE), jnp.float32)
    earlier = []
    for b in range(blocks):
        part = counts[b * slabs : (b + 1) * slabs]
        earlier.append(part[:, :LANE] + total)
        total = total + part[:, LANE:]
    start = jnp.zeros((1, LANE), jnp.float32)
    starts = []
    for slab in range(slabs):
        starts.append(start)
        start = start + total[slab : slab + 1]
    starts = jnp.concatenate(starts, axis=0)
    for b in range(blocks):
        spot_ref[b : b + 1, :] = jnp.sum(named[b] * (earlier[b] + starts), axis=0, keepdims=True)
    first, count = starts.astype(jnp.int32), total.astype(jnp.int32)
    begins = [first[slab, 0] for slab in range(slabs)]
    sizes = [count[slab, 0] for slab in range(slabs)]
    for copy in copies[1:]:
        copy.wait()
    extra = rows - NODES - events * STEPS
    for b in range(blocks):
        cut = slice(b * LANE, (b + 1) * LANE)
        ids = jnp.broadcast_to(local_ref[b : b + 1, :].astype(jnp.float32), (extra, LANE))
        full = jnp.concatenate(
            [weights_ref[:, cut]] + [records_ref[event, :, cut] for event in range(events)] + [ids], axis=0
        )
        high = full.astype(jnp.bfloat16)
        data_ref[:rows, cut] = high
        data_ref[rows:, cut] = (full - high.astype(jnp.float32)).astype(jnp.bfloat16)
    slot = lax.broadcasted_iota(jnp.int32, (CAP, LANE), 0).astype(jnp.bfloat16)
    lane = lax.broadcasted_iota(jnp.int32, (rows, LANE), 1)

    def cut_block(slab):
        begin, size = begins[slab], sizes[slab]
        shift = lax.rem(begin, LANE)
        base = begin - shift
        turn = lax.rem(LANE - shift, LANE)
        turned = [
            pltpu.roll(sorted_ref[:, pl.ds(pl.multiple_of(base + j * LANE, LANE), LANE)], turn, 1) for j in range(3)
        ]
        for j in range(2):
            piece = jnp.where(lane < LANE - shift, turned[j], turned[j + 1])
            out_ref[slab, :, j * LANE : (j + 1) * LANE] = jnp.where(lane + j * LANE < size, piece, 0.0)

    for chunk in range(chunks):
        spots = spot_ref[...] - float(chunk * CAP)
        wanted = jnp.where((spots >= 0.0) & (spots < CAP), spots, -1.0)
        hot = [
            jnp.where(slot == wanted[b : b + 1, :].astype(jnp.bfloat16), jnp.bfloat16(1), jnp.bfloat16(0))
            for b in range(blocks)
        ]
        placed = lax.dot_general(
            data_ref[...],
            jnp.concatenate(hot, axis=1),
            (((1,), (1,)), ((), ())),
            preferred_element_type=jnp.float32,
        )
        sorted_ref[:, chunk * CAP : (chunk + 1) * CAP] = placed[:rows] + placed[rows:]
        cut_block(chunk)
    for slab in range(chunks, slabs):
        cut_block(slab)


def split(full):
    high = full.astype(jnp.bfloat16)
    return jnp.concatenate([high, (full - high.astype(jnp.float32)).astype(jnp.bfloat16)], axis=0)


def land(got_ref, events, wants, acc_refs):
    slabs = got_ref.shape[0]
    group = min(slabs, 16)
    slot = lax.broadcasted_iota(jnp.int32, (CAP, LANE), 0).astype(jnp.bfloat16)
    if slabs > group:
        for acc_ref in acc_refs:
            acc_ref[...] = jnp.zeros_like(acc_ref)

    def one(g, _):
        items = {item: [] for _, chosen in wants for item in chosen}
        hot = [[] for _ in wants]
        for i in range(group):
            src = g * group + i
            for (first, last, step), found in items.items():
                weights = got_ref[src, first:last, :]
                rows = [NODES + event * STEPS + step for event in range(events)]
                found.append(
                    split(jnp.concatenate([weights * got_ref[src, row : row + 1, :] for row in rows], axis=0))
                )
            ids = got_ref[src, NODES + events * STEPS : NODES + events * STEPS + 1, :].astype(jnp.int32)
            for at_hot, (quarter, _) in zip(hot, wants):
                wanted = jnp.where(ids // CAP == quarter, ids % CAP, -1).astype(jnp.float32).astype(jnp.bfloat16)
                for cut in (slice(0, LANE), slice(LANE, 2 * LANE)):
                    at_hot.append(jnp.where(slot == wanted[:, cut], jnp.bfloat16(1), jnp.bfloat16(0)))
        left = {item: jnp.concatenate(found, axis=1) for item, found in items.items()}
        for at_hot, (_, chosen), acc_ref in zip(hot, wants, acc_refs):
            landed = lax.dot_general(
                jnp.concatenate([left[item] for item in chosen], axis=0),
                jnp.concatenate(at_hot, axis=1),
                (((1,), (1,)), ((), ())),
                preferred_element_type=jnp.float32,
            )
            at_in, at_out = 0, 0
            for first, last, _ in chosen:
                count = events * (last - first)
                rows = slice(at_out, at_out + count)
                both = landed[at_in : at_in + count] + landed[at_in + count : at_in + 2 * count]
                acc_ref[rows, :] = acc_ref[rows, :] + both if slabs > group else both
                at_in, at_out = at_in + 2 * count, at_out + count
        return 0

    if slabs > group:
        lax.fori_loop(0, slabs // group, one, 0)
    else:
        one(0, 0)


FACE_WANTS = ((0, ((0, 16, 0),)), (3, ((48, 64, 0),)))
FIRST_WANTS = (
    (0, ((0, NODES, 0), (0, 16, 1))),
    (1, ((0, NODES, 0),)),
    (2, ((0, NODES, 0),)),
    (3, ((0, NODES, 0), (48, 64, 1))),
)
LATER_WANTS = tuple((q, ((0, NODES, 1),)) for q in range(4))


def sums(events, wants):
    return [
        ((sum(events * (last - first) for first, last, _ in chosen), CAP), jnp.float32) for _, chosen in wants
    ]


def spread_source(events, acc_refs, out_ref):
    for event in range(events):
        for k in range(SUB):
            cut = slice(k % 2 * LANE, (k % 2 + 1) * LANE)
            out_ref[pl.ds(event * FIELD + k, NODES, stride=SUB), :] = acc_refs[k // 2][event * NODES : (event + 1) * NODES, cut]
        assemble(out_ref, event * FIELD)


def spread_faces(events, low_ref, high_ref, skip, out_ref):
    out_ref[...] = jnp.zeros_like(out_ref)
    for event in range(events):
        rows = slice(skip + event * 16, skip + (event + 1) * 16)
        for j in range(2):
            cut = slice(j * LANE, (j + 1) * LANE)
            out_ref[pl.ds(event * 16 * SUB + j, 16, stride=SUB), :] = low_ref[rows, cut]
            out_ref[pl.ds(event * 16 * SUB + SUB - 2 + j, 16, stride=SUB), :] = high_ref[rows, cut]
        assemble_layers(out_ref, event * 16 * SUB, 1)


def land_faces_kernel(events, got_ref, faces_hbm, near_ref, far_ref, faces_ref, source_ref, low_ref, high_ref, sem):
    copy = pltpu.make_async_copy(faces_hbm, faces_ref, sem)
    copy.start()
    land(got_ref, events, FACE_WANTS, (low_ref, high_ref))
    spread_faces(events, low_ref, high_ref, 0, source_ref)
    copy.wait()
    even = is_even()
    fields = 2 * events + 1
    for field in range(fields):
        for b in range(4):
            low = at(faces_ref, field * FACE, b)[...]
            high = at(faces_ref, (fields + field) * FACE, b)[...]
            if events <= field < 2 * events:
                source_low, source_high = face_tiles(source_ref, (field - events) * 16 * SUB, b, 0, 0)
                low, high = low - source_low, high - source_high
            at(near_ref, field * FACE, b)[...] = jnp.where(even, high, low)
            at(far_ref, field * FACE, b)[...] = jnp.where(even, low, high)


def state_rows(events):
    counts = {"force": 2 * events, "mass": 1, "base": 2 * events, "stiff": 1, "kern": 1}
    rows, total = {}, 0
    for name, count in counts.items():
        rows[name] = total * FIELD
        total += count
    return rows, total * FIELD


def land_first_kernel(
    events, got_ref, state_hbm, now_hbm, state_ref, now_ref, later_ref, source_ref, acc0, acc1, acc2, acc3, sems
):
    copies = [
        pltpu.make_async_copy(state_hbm, state_ref, sems.at[0]),
        pltpu.make_async_copy(now_hbm, now_ref, sems.at[1]),
    ]
    for copy in copies:
        copy.start()
    land(got_ref, events, FIRST_WANTS, (acc0, acc1, acc2, acc3))
    spread_source(events, (acc0, acc1, acc2, acc3), source_ref)
    spread_faces(events, acc0, acc3, events * NODES, later_ref)
    for copy in copies:
        copy.wait()
    rows, _ = state_rows(events)
    for event in range(events):
        for n in range(NODES):
            place = at(state_ref, rows["force"] + (events + event) * FIELD, n)
            place[...] = place[...] - at(source_ref, event * FIELD, n)[...]


def land_later_kernel(
    events, got_ref, new_ref, fwd_hbm, adj_hbm, source_ref, out_ref, acc0, acc1, acc2, acc3, sems
):
    copies = []
    for event in range(events):
        for field, out_hbm in ((event, fwd_hbm), (events + event, adj_hbm)):
            gather_back(new_ref, field * FIELD, out_ref, field)
            copies.append(pltpu.make_async_copy(out_ref.at[field], out_hbm.at[event], sems.at[field]))
            copies[-1].start()
    land(got_ref, events, LATER_WANTS, (acc0, acc1, acc2, acc3))
    spread_source(events, (acc0, acc1, acc2, acc3), source_ref)
    for copy in copies:
        copy.wait()


def first_kernel(
    events, fwd_ref, fwd_prev_ref, adj_ref, adj_prev_ref, shear_ref, density_ref, _, state_ref, now_ref, faces_ref, prev_ref
):
    rows, _ = state_rows(events)
    stiff_ref, kern_ref = (state_ref.at[pl.ds(rows[name], FIELD), :] for name in ("stiff", "kern"))
    spread(shear_ref, None, state_ref, rows["stiff"])
    for n in range(NODES):
        place = at(stiff_ref, 0, n)
        place[...] = place[...] * WEIGHT[n]
        at(kern_ref, 0, n)[...] = jnp.zeros((SUB, LANE), jnp.float32)
        at(state_ref, rows["mass"], n)[...] = density_ref[...] * WEIGHT[n]

    def one(event, _):
        u, v = event * FIELD, (events + event) * FIELD
        for now_src, prev_src, field in ((fwd_ref, fwd_prev_ref, u), (adj_ref, adj_prev_ref, v)):
            spread(now_src, event, now_ref, field)
            spread(prev_src, event, prev_ref, 0)
            for n in range(NODES):
                at(state_ref, rows["base"] + field, n)[...] = 2.0 * at(now_ref, field, n)[...] - at(prev_ref, 0, n)[...]
        stiffness(
            [(now_ref, u), (now_ref, v)],
            [(state_ref, rows["force"] + u), (state_ref, rows["force"] + v)],
            stiff_ref,
            kern_ref,
        )
        return 0

    lax.fori_loop(0, events, one, 0)
    fields = 2 * events + 1

    def join(field, _):
        assemble(state_ref, rows["force"] + field * FIELD)
        for b in range(4):
            low, high = face_tiles(state_ref, rows["force"] + field * FIELD, b, 0, 48)
            at(faces_ref, field * FACE, b)[...] = low
            at(faces_ref, (fields + field) * FACE, b)[...] = high
        return 0

    lax.fori_loop(0, fields, join, 0)


def second_kernel(
    events, share, position_ref, state_ref, now_ref, later_ref, near_rim_ref, far_rim_ref,
    new_ref, base_ref, factor_ref, next_ref, parts_ref, near_ref, far_ref, kern_ref,
):
    rows, _ = state_rows(events)
    stiff_ref = state_ref.at[pl.ds(rows["stiff"], FIELD), :]
    kern_ref[...] = state_ref[pl.ds(rows["kern"], FIELD), :]
    mass = 2 * events
    even = is_even()
    for n in range(NODES):
        at(factor_ref, 0, n)[...] = STEP_SQUARE / with_rim(
            at(state_ref, rows["mass"], n)[...], n, near_rim_ref, far_rim_ref, mass * FACE
        )

    def one(event, _):
        u, v = event * FIELD, (events + event) * FIELD
        for field, rim in ((u, event), (v, events + event)):
            for n in range(NODES):
                force = with_rim(at(state_ref, rows["force"] + field, n)[...], n, near_rim_ref, far_rim_ref, rim * FACE)
                new = at(state_ref, rows["base"] + field, n)[...] - at(factor_ref, 0, n)[...] * force
                at(new_ref, field, n)[...] = new
                at(base_ref, field, n)[...] = 2.0 * new - at(now_ref, field, n)[...]
        stiffness([(new_ref, u), (new_ref, v)], [(next_ref, u), (next_ref, v)], stiff_ref, kern_ref)
        assemble(next_ref, u)
        assemble(next_ref, v)
        for b in range(4):
            low, high = face_tiles(next_ref, u, b, 0, 48)
            at(near_ref, event * FACE, b)[...] = jnp.where(even, high, low)
            at(far_ref, event * FACE, b)[...] = jnp.where(even, low, high)
            low, high = face_tiles(next_ref, v, b, 0, 48)
            source_low, source_high = face_tiles(later_ref, event * 16 * SUB, b, 0, 0)
            low, high = low - source_low, high - source_high
            at(near_ref, (events + event) * FACE, b)[...] = jnp.where(even, high, low)
            at(far_ref, (events + event) * FACE, b)[...] = jnp.where(even, low, high)
        return 0

    lax.fori_loop(0, events, one, 0)
    for n in range(NODES):
        place = at(kern_ref, 0, n)
        place[...] = -TIME_STEP * at(stiff_ref, 0, n)[...] * place[...]
    tiles = SUB // share
    for j in range(share):
        owner = lax.rem(position_ref[0] + j, share)
        for k in range(tiles):
            parts_ref[j, :, k * LANE : (k + 1) * LANE] = kern_ref[pl.ds(owner * tiles + k, NODES, stride=SUB), :]


def last_kernel(events, share, base_ref, factor_ref, next_ref, source_ref, near_rim_ref, far_rim_ref, *rest):
    fwd_hbm, adj_hbm, kernel_ref, done_ref, out_ref, sems = rest[share:]
    copies = []
    for event in range(events):
        for field, out_hbm in ((event, fwd_hbm), (events + event, adj_hbm)):
            for n in range(NODES):
                force = with_rim(at(next_ref, field * FIELD, n)[...], n, near_rim_ref, far_rim_ref, field * FACE)
                if field >= events:
                    force = force - at(source_ref, event * FIELD, n)[...]
                at(done_ref, 0, n)[...] = at(base_ref, field * FIELD, n)[...] - at(factor_ref, 0, n)[...] * force
            gather_back(done_ref, 0, out_ref, field)
            copies.append(pltpu.make_async_copy(out_ref.at[field], out_hbm.at[event], sems.at[field]))
            copies[-1].start()
    total = rest[0][0]
    for part in rest[1:share]:
        total = total + part[0]
    kernel_ref[...] = total
    for copy in copies:
        copy.wait()


def call(body, outs, scratch=(), cost=2_000_000, smem=0, count=0, outside=0, limit=24, written=0):
    in_specs = [pl.BlockSpec(memory_space=pltpu.SMEM)] * smem
    in_specs += [pl.BlockSpec(memory_space=pltpu.VMEM)] * (count - smem - outside)
    in_specs += [pl.BlockSpec(memory_space=pl.ANY)] * outside
    return pl.pallas_call(
        body,
        out_shape=[out if not isinstance(out, tuple) else jax.ShapeDtypeStruct(out, jnp.float32) for out in outs],
        in_specs=in_specs,
        out_specs=[pl.BlockSpec(memory_space=pl.ANY)] * written
        + [pl.BlockSpec(memory_space=pltpu.VMEM)] * (len(outs) - written),
        scratch_shapes=[pltpu.VMEM(*x) if isinstance(x, tuple) else x for x in scratch],
        compiler_params=pltpu.CompilerParams(vmem_limit_bytes=limit * 1024 * 1024),
        cost_estimate=pl.CostEstimate(flops=cost, bytes_accessed=cost, transcendentals=0),
    )


def near_core(shape):
    return pltpu.VMEM(shape, jnp.float32)


def off_core(shape):
    return pltpu.HBM(shape, jnp.float32)


def kept(*arrays):
    return [pltpu.with_memory_space_constraint(x, pltpu.VMEM) for x in arrays]


def far_off(*arrays):
    return [pltpu.with_memory_space_constraint(x, pltpu.HBM) for x in arrays]


def beside(near, far):
    count = lax.axis_size("space")
    inner = [pair for i in range(1, count - 1, 2) for pair in ((i, i + 1), (i + 1, i))]
    from_far = lax.ppermute(far, "space", inner)
    from_near = lax.ppermute(near, "space", [(i, i + 1 - 2 * (i % 2)) for i in range(count)])
    return from_near, from_far


def shards(
    fwd_now,
    fwd_prev,
    adj_now,
    adj_prev,
    shear_mod,
    density,
    station_owner,
    receiver_local,
    station_weights,
    adj_records,
):
    events = fwd_now.shape[0]
    stations = station_owner.shape[0]
    elements = fwd_now.shape[-1]
    slabs = lax.axis_size("space")
    share = lax.axis_size("event")
    f32 = jnp.float32
    rows = -(-(NODES + events * STEPS + 1) // SUB) * SUB
    blocks = stations // LANE

    send, token = call(
        place_kernel,
        [(slabs, rows, CAP), near_core((SUB, LANE))],
        [
            ((blocks, LANE), jnp.int32),
            ((blocks, LANE), jnp.int32),
            ((NODES, stations), f32),
            ((events, STEPS, stations), f32),
            ((blocks, LANE), f32),
            ((2 * rows, stations), jnp.bfloat16),
            ((rows, stations + 3 * LANE), f32),
            pltpu.SemaphoreType.DMA((4,)),
        ],
        count=4,
        outside=4,
        limit=48,
    )(
        *far_off(
            station_owner.reshape(blocks, LANE), receiver_local.reshape(blocks, LANE), station_weights, adj_records
        )
    )
    got = lax.all_to_all(send, "space", split_axis=0, concat_axis=0, tiled=True)

    fields = 2 * events + 1
    state, now, faces = call(
        functools.partial(first_kernel, events),
        [
            off_core((state_rows(events)[1], LANE)),
            off_core((2 * events * FIELD, LANE)),
            off_core((2 * fields * FACE, LANE)),
        ],
        [((FIELD, LANE), f32)],
        count=7,
    )(*far_off(fwd_now, fwd_prev, adj_now, adj_prev, shear_mod, density.reshape(SUB, LANE)), *kept(token))
    near, far = call(
        functools.partial(land_faces_kernel, events),
        [(fields * FACE, LANE), (fields * FACE, LANE)],
        [((2 * fields * FACE, LANE), f32), ((events * 16 * SUB, LANE), f32)]
        + sums(events, FACE_WANTS)
        + [pltpu.SemaphoreType.DMA(())],
        count=2,
        outside=1,
    )(got, *far_off(faces))
    near_rim, far_rim = beside(near, far)
    state, now, later = call(
        functools.partial(land_first_kernel, events),
        [near_core(state.shape), near_core(now.shape), near_core((events * 16 * SUB, LANE))],
        [((events * FIELD, LANE), f32)] + sums(events, FIRST_WANTS) + [pltpu.SemaphoreType.DMA((2,))],
        count=3,
        outside=2,
        limit=40,
    )(got, *far_off(state, now))
    new, base, factor, after, parts, near, far = call(
        functools.partial(second_kernel, events, share),
        [
            near_core((2 * events * FIELD, LANE)),
            near_core((2 * events * FIELD, LANE)),
            near_core((FIELD, LANE)),
            near_core((2 * events * FIELD, LANE)),
            (share, NODES, elements // share),
            (2 * events * FACE, LANE),
            (2 * events * FACE, LANE),
        ],
        [((FIELD, LANE), f32)],
        smem=1,
        count=6,
    )(lax.axis_index("event").reshape(1).astype(jnp.int32), *kept(state, now, later), near_rim, far_rim)
    near_rim, far_rim = beside(near, far)
    pieces = [parts[0:1]] + [
        lax.ppermute(parts[j : j + 1], "event", [(i, (i + j) % share) for i in range(share)]) for j in range(1, share)
    ]
    fwd_before, adj_before, source = call(
        functools.partial(land_later_kernel, events),
        [fwd_now.shape, adj_now.shape, near_core((events * FIELD, LANE))],
        [((2 * events, NODES, elements), f32)]
        + sums(events, LATER_WANTS)
        + [pltpu.SemaphoreType.DMA((2 * events,))],
        count=2,
        limit=40,
        written=2,
    )(got, *kept(new))
    fwd_last, adj_last, kernel = call(
        functools.partial(last_kernel, events, share),
        [fwd_now.shape, adj_now.shape, (NODES, elements // share)],
        [((FIELD, LANE), f32), ((2 * events, NODES, elements), f32), pltpu.SemaphoreType.DMA((2 * events,))],
        count=6 + share,
        written=2,
    )(*kept(base, factor, after, source), near_rim, far_rim, *pieces)
    return fwd_last, fwd_before, adj_last, adj_before, kernel


def solution(mesh):
    in_specs = (
        P("event", None, "space"),
        P("event", None, "space"),
        P("event", None, "space"),
        P("event", None, "space"),
        P(None, "space"),
        P("space"),
        P("space", None),
        P("space"),
        P(None, "space"),
        P("event", None, "space"),
    )
    out_specs = (
        P("event", None, "space"),
        P("event", None, "space"),
        P("event", None, "space"),
        P("event", None, "space"),
        P(None, ("space", "event")),
    )
    return jax.shard_map(shards, mesh=mesh, in_specs=in_specs, out_specs=out_specs, check_vma=False)
```

```python
import functools

import jax
import jax.numpy as jnp
import numpy as np
from jax import lax
from jax.experimental import pallas as pl
from jax.experimental.pallas import tpu as pltpu
from jax.sharding import PartitionSpec as P

EX = 16
EY = 16
STEPS = 2
CAP = 256
NODES = 64
SUB = 8
LANE = 128
FIELD = NODES * SUB
FACE = 4 * SUB


TIME_STEP = 0.08
STEP_SQUARE = 0.0064

EDGE = np.array([1.0 / 6.0, 5.0 / 6.0, 5.0 / 6.0, 1.0 / 6.0])
WEIGHT = [float(np.float32(EDGE[n // 16] * EDGE[n // 4 % 4] * EDGE[n % 4])) for n in range(NODES)]
ROOT5 = float(np.sqrt(5.0))

LINES = (
    [[16 * c + 4 * b + i for i in range(4)] for c in range(4) for b in range(4)],
    [[16 * c + 4 * i + a for i in range(4)] for c in range(4) for a in range(4)],
    [[16 * i + 4 * b + a for i in range(4)] for b in range(4) for a in range(4)],
)


def derive(x0, x1, x2, x3):
    o0, o1 = x0 - x3, x1 - x2
    q = (x1 + x2) - (x0 + x3)
    a0, a1 = 1.25 * q, (0.25 * ROOT5) * q
    b0 = -1.75 * o0 + (1.25 * ROOT5) * o1
    b1 = -0.25 * o0 - (0.25 * ROOT5) * o1
    return b0 + a0, b1 + a1, b1 - a1, b0 - a0


def derive_transposed(h0, h1, h2, h3):
    p0, m0, p1, m1 = h0 + h3, h0 - h3, h1 + h2, h1 - h2
    q = 1.25 * m0 + (0.25 * ROOT5) * m1
    o0 = -1.75 * p0 - 0.25 * p1
    o1 = (1.25 * ROOT5) * p0 - (0.25 * ROOT5) * p1
    return o0 - q, o1 + q, q - o1, -o0 - q


def at(ref, base, node):
    if isinstance(base, int):
        return ref.at[pl.ds(base + node * SUB, SUB), :]
    return ref.at[pl.ds(pl.multiple_of(base, SUB) + node * SUB, SUB), :]


def spread(src_ref, index, dst_ref, base):
    for k in range(SUB):
        block = src_ref[:, k * LANE : (k + 1) * LANE] if index is None else src_ref[index, :, k * LANE : (k + 1) * LANE]
        dst_ref[pl.ds(base + k, NODES, stride=SUB), :] = block


def gather_back(src_ref, base, dst_ref, index):
    for k in range(SUB):
        dst_ref[index, :, k * LANE : (k + 1) * LANE] = src_ref[pl.ds(base + k, NODES, stride=SUB), :]


def places():
    lane = lax.broadcasted_iota(jnp.int32, (SUB, LANE), 1)
    sub = lax.broadcasted_iota(jnp.int32, (SUB, LANE), 0)
    return lane, sub


def assemble_layers(ref, base, planes):
    lane, sub = places()
    zero = jnp.zeros((SUB, LANE), jnp.float32)
    not_first = lane % EX != 0
    not_last = lane % EX != EX - 1
    odd = sub % 2 == 1
    for c in range(planes):
        for b in range(4):
            n = 16 * c + 4 * b
            low_at, high_at = at(ref, base, n), at(ref, base, n + 3)
            low, high = low_at[...], high_at[...]
            low_at[...] = low + jnp.where(not_first, pltpu.roll(high, 1, 1), zero)
            high_at[...] = high + jnp.where(not_last, pltpu.roll(low, LANE - 1, 1), zero)
    for c in range(planes):
        for a in range(4):
            n = 16 * c + a
            low_at, high_at = at(ref, base, n), at(ref, base, n + 12)
            low, high = low_at[...], high_at[...]
            back = pltpu.roll(high, EX, 1)
            ahead = pltpu.roll(low, LANE - EX, 1)
            back = jnp.where(lane >= EX, back, jnp.where(odd, pltpu.roll(back, 1, 0), zero))
            ahead = jnp.where(lane < LANE - EX, ahead, jnp.where(odd, zero, pltpu.roll(ahead, SUB - 1, 0)))
            low_at[...] = low + back
            high_at[...] = high + ahead


def assemble(ref, base):
    _, sub = places()
    zero = jnp.zeros((SUB, LANE), jnp.float32)
    assemble_layers(ref, base, 4)
    for n in range(16):
        low_at, high_at = at(ref, base, n), at(ref, base, n + 48)
        low, high = low_at[...], high_at[...]
        low_at[...] = low + jnp.where(sub >= 2, pltpu.roll(high, 2, 0), zero)
        high_at[...] = high + jnp.where(sub < SUB - 2, pltpu.roll(low, SUB - 2, 0), zero)


def roll_sub(value, shift):
    shift = shift % SUB
    return value if shift == 0 else pltpu.roll(value, shift, 0)


def is_even():
    return lax.rem(lax.axis_index("space"), 2) == 0


def face_tiles(ref, base, b, low_first, high_first):
    _, sub = places()
    tiles = []
    for first, shift in ((low_first, 0), (high_first, 2)):
        pieces = [roll_sub(at(ref, base, first + 4 * b + a)[...], 2 * a + shift) for a in range(4)]
        tiles.append(
            jnp.where(
                sub < 4, jnp.where(sub < 2, pieces[0], pieces[1]), jnp.where(sub < 6, pieces[2], pieces[3])
            )
        )
    return tiles


def with_rim(value, node, near_ref, far_ref, rim_base):
    _, sub = places()
    zero = jnp.zeros((SUB, LANE), jnp.float32)
    c, b, a = node // 16, node // 4 % 4, node % 4
    if c not in (0, 3):
        return value
    near, far = at(near_ref, rim_base, b)[...], at(far_ref, rim_base, b)[...]
    if c == 0:
        return value + jnp.where(sub < 2, roll_sub(jnp.where(is_even(), far, near), -2 * a), zero)
    return value + jnp.where(sub >= 6, roll_sub(jnp.where(is_even(), near, far), 6 - 2 * a), zero)


def stiffness(ins, outs, stiff_ref, kern):
    for dim, lines in enumerate(LINES):
        for line in lines:
            stiff = [at(stiff_ref, 0, n)[...] for n in line]
            grads = []
            for (src, sbase), out in zip(ins, outs):
                g = derive(*[at(src, sbase, n)[...] for n in line])
                grads.append(g)
                if out is None:
                    continue
                dst, dbase = out
                back = derive_transposed(*[x * s for x, s in zip(g, stiff)])
                for n, x in zip(line, back):
                    place = at(dst, dbase, n)
                    place[...] = x if dim == 0 else place[...] + x
            if kern is not None:
                for i, n in enumerate(line):
                    place = at(kern, 0, n)
                    place[...] = place[...] + grads[0][i] * grads[1][i]


def place_kernel(
    owner_hbm, local_hbm, weights_hbm, records_hbm, out_ref, token_ref,
    owner_ref, local_ref, weights_ref, records_ref, spot_ref, data_ref, sorted_ref, sems,
):
    copies = [
        pltpu.make_async_copy(src, dst, sems.at[i])
        for i, (src, dst) in enumerate(
            (
                (owner_hbm, owner_ref),
                (local_hbm, local_ref),
                (weights_hbm, weights_ref),
                (records_hbm, records_ref),
            )
        )
    ]
    for copy in copies:
        copy.start()
    token_ref[...] = jnp.zeros_like(token_ref)
    stations = weights_ref.shape[1]
    rows = sorted_ref.shape[0]
    events = records_ref.shape[0]
    few = events * STEPS + 1
    packed = 2 * (NODES + few)
    slabs = out_ref.shape[0] // packed
    blocks = stations // LANE
    chunks = stations // CAP
    owner_id = lax.broadcasted_iota(jnp.int32, (slabs, LANE), 0)
    before = lax.broadcasted_iota(jnp.int32, (LANE, LANE), 0) < lax.broadcasted_iota(jnp.int32, (LANE, LANE), 1)
    counting = jnp.concatenate(
        [jnp.where(before, 1.0, 0.0), jnp.ones((LANE, LANE), jnp.float32)], axis=1
    ).astype(jnp.bfloat16)
    copies[0].wait()
    named = [jnp.where(owner_ref[b : b + 1, :] == owner_id, 1.0, 0.0) for b in range(blocks)]
    counts = jnp.dot(
        jnp.concatenate(named, axis=0).astype(jnp.bfloat16), counting, preferred_element_type=jnp.float32
    )
    total = jnp.zeros((slabs, LANE), jnp.float32)
    earlier = []
    for b in range(blocks):
        part = counts[b * slabs : (b + 1) * slabs]
        earlier.append(part[:, :LANE] + total)
        total = total + part[:, LANE:]
    start = jnp.zeros((1, LANE), jnp.float32)
    starts = []
    for slab in range(slabs):
        starts.append(start)
        start = start + total[slab : slab + 1]
    starts = jnp.concatenate(starts, axis=0)
    for b in range(blocks):
        spot_ref[b : b + 1, :] = jnp.sum(named[b] * (earlier[b] + starts), axis=0, keepdims=True)
    first, count = starts.astype(jnp.int32), total.astype(jnp.int32)
    begins = [first[slab, 0] for slab in range(slabs)]
    sizes = [count[slab, 0] for slab in range(slabs)]
    for copy in copies[1:]:
        copy.wait()
    extra = rows - NODES - events * STEPS
    for b in range(blocks):
        cut = slice(b * LANE, (b + 1) * LANE)
        ids = jnp.broadcast_to(local_ref[b : b + 1, :].astype(jnp.float32), (extra, LANE))
        full = jnp.concatenate(
            [weights_ref[:, cut]] + [records_ref[event, :, cut] for event in range(events)] + [ids], axis=0
        )
        high = full.astype(jnp.bfloat16)
        data_ref[:rows, cut] = high
        data_ref[rows:, cut] = (full - high.astype(jnp.float32)).astype(jnp.bfloat16)
    slot = lax.broadcasted_iota(jnp.int32, (CAP, LANE), 0).astype(jnp.bfloat16)
    lane = lax.broadcasted_iota(jnp.int32, (SUB, LANE), 1)
    sorted_ref[:, stations:] = jnp.zeros((rows, 3 * LANE), jnp.float32)

    def cut_block(slab):
        begin, size = begins[slab], sizes[slab]
        shift = lax.rem(begin, LANE)
        base = begin - shift
        turn = lax.rem(LANE - shift, LANE)
        kept_lanes = lane >= shift
        for first in range(0, rows, SUB):
            tiles = [
                sorted_ref[first : first + SUB, pl.ds(pl.multiple_of(base + j * LANE, LANE), LANE)] for j in range(3)
            ]
            for j in range(2):
                piece = pltpu.roll(jnp.where(kept_lanes, tiles[j], tiles[j + 1]), turn, 1)
                if first < NODES:
                    out_ref[pl.ds(slab * packed + j * NODES + first, SUB), :] = piece
                else:
                    piece = jnp.where(lane + j * LANE < size, piece, 0.0)
                    out_ref[pl.ds(slab * packed + 2 * NODES + j * few, few), :] = piece[:few]

    for chunk in range(chunks):
        spots = spot_ref[...] - float(chunk * CAP)
        wanted = jnp.where((spots >= 0.0) & (spots < CAP), spots, -1.0)
        hot = [
            jnp.where(slot == wanted[b : b + 1, :].astype(jnp.bfloat16), jnp.bfloat16(1), jnp.bfloat16(0))
            for b in range(blocks)
        ]
        placed = lax.dot_general(
            data_ref[...],
            jnp.concatenate(hot, axis=1),
            (((1,), (1,)), ((), ())),
            preferred_element_type=jnp.float32,
        )
        sorted_ref[:, chunk * CAP : (chunk + 1) * CAP] = placed[:rows] + placed[rows:]
        cut_block(chunk)
    for slab in range(chunks, slabs):
        cut_block(slab)


def split(full):
    high = full.astype(jnp.bfloat16)
    return jnp.concatenate([high, (full - high.astype(jnp.float32)).astype(jnp.bfloat16)], axis=0)


def land(got_ref, events, wants, acc_refs):
    few = events * STEPS + 1
    packed = 2 * (NODES + few)
    slabs = got_ref.shape[0] // packed
    group = min(slabs, 16)
    slot = lax.broadcasted_iota(jnp.int32, (CAP, LANE), 0).astype(jnp.bfloat16)
    if slabs > group:
        for acc_ref in acc_refs:
            acc_ref[...] = jnp.zeros_like(acc_ref)

    def one(g, _):
        items = {item: [] for _, chosen in wants for item in chosen}
        hot = [[] for _ in wants]
        for i in range(group):
            src = g * group + i
            for (first, last, step), found in items.items():
                for j in range(2):
                    weights = got_ref[pl.ds(src * packed + j * NODES + first, last - first), :]
                    samples = [
                        got_ref[pl.ds(src * packed + 2 * NODES + j * few + event * STEPS + step, 1), :]
                        for event in range(events)
                    ]
                    found.append(split(jnp.concatenate([weights * sample for sample in samples], axis=0)))
            ids = [
                got_ref[pl.ds(src * packed + 2 * NODES + (j + 1) * few - 1, 1), :].astype(jnp.int32) for j in range(2)
            ]
            for at_hot, (quarter, _) in zip(hot, wants):
                for half in ids:
                    wanted = jnp.where(half // CAP == quarter, half % CAP, -1).astype(jnp.float32).astype(jnp.bfloat16)
                    at_hot.append(jnp.where(slot == wanted, jnp.bfloat16(1), jnp.bfloat16(0)))
        left = {item: jnp.concatenate(found, axis=1) for item, found in items.items()}
        for at_hot, (_, chosen), acc_ref in zip(hot, wants, acc_refs):
            landed = lax.dot_general(
                jnp.concatenate([left[item] for item in chosen], axis=0),
                jnp.concatenate(at_hot, axis=1),
                (((1,), (1,)), ((), ())),
                preferred_element_type=jnp.float32,
            )
            at_in, at_out = 0, 0
            for first, last, _ in chosen:
                count = events * (last - first)
                rows = slice(at_out, at_out + count)
                both = landed[at_in : at_in + count] + landed[at_in + count : at_in + 2 * count]
                acc_ref[rows, :] = acc_ref[rows, :] + both if slabs > group else both
                at_in, at_out = at_in + 2 * count, at_out + count
        return 0

    if slabs > group:
        lax.fori_loop(0, slabs // group, one, 0)
    else:
        one(0, 0)


FACE_WANTS = ((0, ((0, 16, 0), (0, 16, 1))), (3, ((48, 64, 0), (48, 64, 1))))
FIRST_WANTS = ((0, ((0, NODES, 0), (0, NODES, 1))),) + tuple((q, ((0, NODES, 0),)) for q in range(1, 4))
LATER_WANTS = tuple((q, ((0, NODES, 1),)) for q in range(1, 4))


def sums(events, wants):
    return [
        ((sum(events * (last - first) for first, last, _ in chosen), CAP), jnp.float32) for _, chosen in wants
    ]


def spread_source(events, acc_refs, skip, out_ref):
    for event in range(events):
        for k in range(SUB):
            cut = slice(k % 2 * LANE, (k % 2 + 1) * LANE)
            first = event * NODES + (skip if k < 2 else 0)
            rows = slice(first, first + NODES)
            out_ref[pl.ds(event * FIELD + k, NODES, stride=SUB), :] = acc_refs[k // 2][rows, cut]
        assemble(out_ref, event * FIELD)


def land_faces_kernel(events, got_ref, faces_hbm, near_ref, far_ref, faces_ref, source_ref, low_ref, high_ref, sem):
    copy = pltpu.make_async_copy(faces_hbm, faces_ref, sem)
    copy.start()
    land(got_ref, events, FACE_WANTS, (low_ref, high_ref))
    source_ref[...] = jnp.zeros_like(source_ref)
    for each in range(STEPS * events):
        rows = slice(each * 16, (each + 1) * 16)
        for j in range(2):
            cut = slice(j * LANE, (j + 1) * LANE)
            source_ref[pl.ds(each * 16 * SUB + j, 16, stride=SUB), :] = low_ref[rows, cut]
            source_ref[pl.ds(each * 16 * SUB + SUB - 2 + j, 16, stride=SUB), :] = high_ref[rows, cut]
        assemble_layers(source_ref, each * 16 * SUB, 1)
    copy.wait()
    even = is_even()
    fields = 2 * events + 1
    for field in range(fields + events):
        for b in range(4):
            if field < fields:
                low = at(faces_ref, field * FACE, b)[...]
                high = at(faces_ref, (fields + field) * FACE, b)[...]
            if events <= field < 2 * events:
                source_low, source_high = face_tiles(source_ref, (field - events) * 16 * SUB, b, 0, 0)
                low, high = low - source_low, high - source_high
            if field >= fields:
                low, high = face_tiles(source_ref, (events + field - fields) * 16 * SUB, b, 0, 0)
            at(near_ref, field * FACE, b)[...] = jnp.where(even, high, low)
            at(far_ref, field * FACE, b)[...] = jnp.where(even, low, high)


def state_rows(events):
    counts = {"force": 2 * events, "mass": 1, "base": 2 * events, "stiff": 1, "kern": 1}
    rows, total = {}, 0
    for name, count in counts.items():
        rows[name] = total * FIELD
        total += count
    return rows, total * FIELD


def land_first_kernel(
    events, got_ref, state_hbm, now_hbm, state_ref, now_ref, acc0, source_ref, acc1, acc2, acc3, sems
):
    copies = [
        pltpu.make_async_copy(state_hbm, state_ref, sems.at[0]),
        pltpu.make_async_copy(now_hbm, now_ref, sems.at[1]),
    ]
    for copy in copies:
        copy.start()
    land(got_ref, events, FIRST_WANTS, (acc0, acc1, acc2, acc3))
    spread_source(events, (acc0, acc1, acc2, acc3), 0, source_ref)
    for copy in copies:
        copy.wait()
    rows, _ = state_rows(events)
    for event in range(events):
        for n in range(NODES):
            place = at(state_ref, rows["force"] + (events + event) * FIELD, n)
            place[...] = place[...] - at(source_ref, event * FIELD, n)[...]


def land_later_kernel(
    events, got_ref, new_ref, acc0, fwd_hbm, adj_hbm, source_ref, out_ref, acc1, acc2, acc3, sems
):
    copies = []
    for event in range(events):
        for field, out_hbm in ((event, fwd_hbm), (events + event, adj_hbm)):
            gather_back(new_ref, field * FIELD, out_ref, field)
            copies.append(pltpu.make_async_copy(out_ref.at[field], out_hbm.at[event], sems.at[field]))
            copies[-1].start()
    land(got_ref, events, LATER_WANTS, (acc1, acc2, acc3))
    spread_source(events, (acc0, acc1, acc2, acc3), events * NODES, source_ref)
    for copy in copies:
        copy.wait()


def first_kernel(
    events, fwd_ref, fwd_prev_ref, adj_ref, adj_prev_ref, shear_ref, density_ref, _, state_ref, now_ref, faces_ref, prev_ref
):
    rows, _ = state_rows(events)
    stiff_ref, kern_ref = (state_ref.at[pl.ds(rows[name], FIELD), :] for name in ("stiff", "kern"))
    spread(shear_ref, None, state_ref, rows["stiff"])
    for n in range(NODES):
        place = at(stiff_ref, 0, n)
        place[...] = place[...] * WEIGHT[n]
        at(kern_ref, 0, n)[...] = jnp.zeros((SUB, LANE), jnp.float32)
        at(state_ref, rows["mass"], n)[...] = density_ref[...] * WEIGHT[n]

    def one(event, _):
        u, v = event * FIELD, (events + event) * FIELD
        for now_src, prev_src, field in ((fwd_ref, fwd_prev_ref, u), (adj_ref, adj_prev_ref, v)):
            spread(now_src, event, now_ref, field)
            spread(prev_src, event, prev_ref, 0)
            for n in range(NODES):
                at(state_ref, rows["base"] + field, n)[...] = 2.0 * at(now_ref, field, n)[...] - at(prev_ref, 0, n)[...]
        stiffness(
            [(now_ref, u), (now_ref, v)],
            [(state_ref, rows["force"] + u), (state_ref, rows["force"] + v)],
            stiff_ref,
            kern_ref,
        )
        return 0

    lax.fori_loop(0, events, one, 0)
    fields = 2 * events + 1

    def join(field, _):
        assemble(state_ref, rows["force"] + field * FIELD)
        for b in range(4):
            low, high = face_tiles(state_ref, rows["force"] + field * FIELD, b, 0, 48)
            at(faces_ref, field * FACE, b)[...] = low
            at(faces_ref, (fields + field) * FACE, b)[...] = high
        return 0

    lax.fori_loop(0, fields, join, 0)


def second_kernel(
    events, share, position_ref, state_ref, now_ref, near_rim_ref, far_rim_ref,
    new_ref, base_ref, factor_ref, next_ref, parts_ref, near_ref, far_ref, later_ref, kern_ref,
):
    rows, _ = state_rows(events)
    stiff_ref = state_ref.at[pl.ds(rows["stiff"], FIELD), :]
    kern_ref[...] = state_ref[pl.ds(rows["kern"], FIELD), :]
    mass = 2 * events
    for side, rim_ref in enumerate((near_rim_ref, far_rim_ref)):
        for row in range(0, events * FACE, SUB):
            later_ref[side, row : row + SUB, :] = rim_ref[(mass + 1) * FACE + row : (mass + 1) * FACE + row + SUB, :]
    even = is_even()
    for n in range(NODES):
        at(factor_ref, 0, n)[...] = STEP_SQUARE / with_rim(
            at(state_ref, rows["mass"], n)[...], n, near_rim_ref, far_rim_ref, mass * FACE
        )

    def one(event, _):
        u, v = event * FIELD, (events + event) * FIELD
        for field, rim in ((u, event), (v, events + event)):
            for n in range(NODES):
                force = with_rim(at(state_ref, rows["force"] + field, n)[...], n, near_rim_ref, far_rim_ref, rim * FACE)
                new = at(state_ref, rows["base"] + field, n)[...] - at(factor_ref, 0, n)[...] * force
                at(new_ref, field, n)[...] = new
                at(base_ref, field, n)[...] = 2.0 * new - at(now_ref, field, n)[...]
        stiffness([(new_ref, u), (new_ref, v)], [(next_ref, u), (next_ref, v)], stiff_ref, kern_ref)
        assemble(next_ref, u)
        assemble(next_ref, v)
        for field in (u, v):
            for b in range(4):
                low, high = face_tiles(next_ref, field, b, 0, 48)
                at(near_ref, field // NODES * 4, b)[...] = jnp.where(even, high, low)
                at(far_ref, field // NODES * 4, b)[...] = jnp.where(even, low, high)
        return 0

    lax.fori_loop(0, events, one, 0)
    for n in range(NODES):
        place = at(kern_ref, 0, n)
        place[...] = -TIME_STEP * at(stiff_ref, 0, n)[...] * place[...]
    tiles = SUB // share
    for j in range(share):
        owner = lax.rem(position_ref[0] + j, share)
        for k in range(tiles):
            parts_ref[j, :, k * LANE : (k + 1) * LANE] = kern_ref[pl.ds(owner * tiles + k, NODES, stride=SUB), :]


def last_kernel(events, share, base_ref, factor_ref, next_ref, source_ref, later_ref, near_rim_ref, far_rim_ref, *rest):
    fwd_hbm, adj_hbm, kernel_ref, done_ref, out_ref, sems = rest[share:]
    copies = []
    for event in range(events):
        for field, out_hbm in ((event, fwd_hbm), (events + event, adj_hbm)):
            for n in range(NODES):
                force = with_rim(at(next_ref, field * FIELD, n)[...], n, near_rim_ref, far_rim_ref, field * FACE)
                if field >= events:
                    source = at(source_ref, event * FIELD, n)[...]
                    force = force - with_rim(source, n, later_ref.at[0], later_ref.at[1], event * FACE)
                at(done_ref, 0, n)[...] = at(base_ref, field * FIELD, n)[...] - at(factor_ref, 0, n)[...] * force
            gather_back(done_ref, 0, out_ref, field)
            copies.append(pltpu.make_async_copy(out_ref.at[field], out_hbm.at[event], sems.at[field]))
            copies[-1].start()
    total = rest[0][0]
    for part in rest[1:share]:
        total = total + part[0]
    kernel_ref[...] = total
    for copy in copies:
        copy.wait()


def call(body, outs, scratch=(), cost=2_000_000, smem=0, count=0, outside=0, limit=24, written=0):
    in_specs = [pl.BlockSpec(memory_space=pltpu.SMEM)] * smem
    in_specs += [pl.BlockSpec(memory_space=pltpu.VMEM)] * (count - smem - outside)
    in_specs += [pl.BlockSpec(memory_space=pl.ANY)] * outside
    return pl.pallas_call(
        body,
        out_shape=[out if not isinstance(out, tuple) else jax.ShapeDtypeStruct(out, jnp.float32) for out in outs],
        in_specs=in_specs,
        out_specs=[pl.BlockSpec(memory_space=pl.ANY)] * written
        + [pl.BlockSpec(memory_space=pltpu.VMEM)] * (len(outs) - written),
        scratch_shapes=[pltpu.VMEM(*x) if isinstance(x, tuple) else x for x in scratch],
        compiler_params=pltpu.CompilerParams(vmem_limit_bytes=limit * 1024 * 1024),
        cost_estimate=pl.CostEstimate(flops=cost, bytes_accessed=cost, transcendentals=0),
    )


def near_core(shape):
    return pltpu.VMEM(shape, jnp.float32)


def off_core(shape):
    return pltpu.HBM(shape, jnp.float32)


def kept(*arrays):
    return [pltpu.with_memory_space_constraint(x, pltpu.VMEM) for x in arrays]


def far_off(*arrays):
    return [pltpu.with_memory_space_constraint(x, pltpu.HBM) for x in arrays]


def beside(near, far):
    count = lax.axis_size("space")
    inner = [pair for i in range(1, count - 1, 2) for pair in ((i, i + 1), (i + 1, i))]
    from_far = lax.ppermute(far, "space", inner)
    from_near = lax.ppermute(near, "space", [(i, i + 1 - 2 * (i % 2)) for i in range(count)])
    return from_near, from_far


def shards(
    fwd_now,
    fwd_prev,
    adj_now,
    adj_prev,
    shear_mod,
    density,
    station_owner,
    receiver_local,
    station_weights,
    adj_records,
):
    events = fwd_now.shape[0]
    stations = station_owner.shape[0]
    elements = fwd_now.shape[-1]
    slabs = lax.axis_size("space")
    share = lax.axis_size("event")
    f32 = jnp.float32
    rows = -(-(NODES + events * STEPS + 1) // SUB) * SUB
    packed = 2 * (NODES + events * STEPS + 1)
    blocks = stations // LANE

    send, token = call(
        place_kernel,
        [(slabs * packed, LANE), near_core((SUB, LANE))],
        [
            ((blocks, LANE), jnp.int32),
            ((blocks, LANE), jnp.int32),
            ((NODES, stations), f32),
            ((events, STEPS, stations), f32),
            ((blocks, LANE), f32),
            ((2 * rows, stations), jnp.bfloat16),
            ((rows, stations + 3 * LANE), f32),
            pltpu.SemaphoreType.DMA((4,)),
        ],
        count=4,
        outside=4,
        limit=48,
    )(
        *far_off(
            station_owner.reshape(blocks, LANE), receiver_local.reshape(blocks, LANE), station_weights, adj_records
        )
    )
    send = send.reshape(slabs, packed // 2, 2, LANE)
    got = lax.all_to_all(send, "space", split_axis=0, concat_axis=0, tiled=True).reshape(slabs * packed, LANE)

    fields = 2 * events + 1
    state, now, faces = call(
        functools.partial(first_kernel, events),
        [
            off_core((state_rows(events)[1], LANE)),
            off_core((2 * events * FIELD, LANE)),
            off_core((2 * fields * FACE, LANE)),
        ],
        [((FIELD, LANE), f32)],
        count=7,
    )(*far_off(fwd_now, fwd_prev, adj_now, adj_prev, shear_mod, density.reshape(SUB, LANE)), *kept(token))
    near, far = call(
        functools.partial(land_faces_kernel, events),
        [((fields + events) * FACE, LANE)] * 2,
        [((2 * fields * FACE, LANE), f32), ((STEPS * events * 16 * SUB, LANE), f32)]
        + sums(events, FACE_WANTS)
        + [pltpu.SemaphoreType.DMA(())],
        count=2,
        outside=1,
    )(got, *far_off(faces))
    near_rim, far_rim = beside(near, far)
    state, now, quarter = call(
        functools.partial(land_first_kernel, events),
        [near_core(state.shape), near_core(now.shape), near_core((STEPS * events * NODES, CAP))],
        [((events * FIELD, LANE), f32)] + sums(events, FIRST_WANTS[1:]) + [pltpu.SemaphoreType.DMA((2,))],
        count=3,
        outside=2,
        limit=40,
    )(got, *far_off(state, now))
    new, base, factor, after, parts, near, far, later = call(
        functools.partial(second_kernel, events, share),
        [
            near_core((2 * events * FIELD, LANE)),
            near_core((2 * events * FIELD, LANE)),
            near_core((FIELD, LANE)),
            near_core((2 * events * FIELD, LANE)),
            (share, NODES, elements // share),
            (2 * events * FACE, LANE),
            (2 * events * FACE, LANE),
            near_core((2, events * FACE, LANE)),
        ],
        [((FIELD, LANE), f32)],
        smem=1,
        count=5,
    )(lax.axis_index("event").reshape(1).astype(jnp.int32), *kept(state, now), near_rim, far_rim)
    near_rim, far_rim = beside(near, far)
    pieces = [parts[0:1]] + [
        lax.ppermute(parts[j : j + 1], "event", [(i, (i + j) % share) for i in range(share)]) for j in range(1, share)
    ]
    fwd_before, adj_before, source = call(
        functools.partial(land_later_kernel, events),
        [fwd_now.shape, adj_now.shape, near_core((events * FIELD, LANE))],
        [((2 * events, NODES, elements), f32)]
        + sums(events, LATER_WANTS)
        + [pltpu.SemaphoreType.DMA((2 * events,))],
        count=3,
        limit=40,
        written=2,
    )(got, *kept(new, quarter))
    fwd_last, adj_last, kernel = call(
        functools.partial(last_kernel, events, share),
        [fwd_now.shape, adj_now.shape, (NODES, elements // share)],
        [((FIELD, LANE), f32), ((2 * events, NODES, elements), f32), pltpu.SemaphoreType.DMA((2 * events,))],
        count=7 + share,
        written=2,
    )(*kept(base, factor, after, source, later), near_rim, far_rim, *pieces)
    return fwd_last, fwd_before, adj_last, adj_before, kernel


def solution(mesh):
    in_specs = (
        P("event", None, "space"),
        P("event", None, "space"),
        P("event", None, "space"),
        P("event", None, "space"),
        P(None, "space"),
        P("space"),
        P("space", None),
        P("space"),
        P(None, "space"),
        P("event", None, "space"),
    )
    out_specs = (
        P("event", None, "space"),
        P("event", None, "space"),
        P("event", None, "space"),
        P("event", None, "space"),
        P(None, ("space", "event")),
    )
    return jax.shard_map(shards, mesh=mesh, in_specs=in_specs, out_specs=out_specs, check_vma=False)
```

```python
import functools

import jax
import jax.numpy as jnp
import numpy as np
from jax import lax
from jax.experimental import pallas as pl
from jax.experimental.pallas import tpu as pltpu
from jax.sharding import PartitionSpec as P

EX = 16
EY = 16
STEPS = 2
CAP = 256
NODES = 64
SUB = 8
LANE = 128
FIELD = NODES * SUB
FACE = 4 * SUB


TIME_STEP = 0.08
STEP_SQUARE = 0.0064

EDGE = np.array([1.0 / 6.0, 5.0 / 6.0, 5.0 / 6.0, 1.0 / 6.0])
WEIGHT = [float(np.float32(EDGE[n // 16] * EDGE[n // 4 % 4] * EDGE[n % 4])) for n in range(NODES)]
ROOT5 = float(np.sqrt(5.0))

LINES = (
    [[16 * c + 4 * b + i for i in range(4)] for c in range(4) for b in range(4)],
    [[16 * c + 4 * i + a for i in range(4)] for c in range(4) for a in range(4)],
    [[16 * i + 4 * b + a for i in range(4)] for b in range(4) for a in range(4)],
)


def derive(x0, x1, x2, x3):
    o0, o1 = x0 - x3, x1 - x2
    q = (x1 + x2) - (x0 + x3)
    a0, a1 = 1.25 * q, (0.25 * ROOT5) * q
    b0 = -1.75 * o0 + (1.25 * ROOT5) * o1
    b1 = -0.25 * o0 - (0.25 * ROOT5) * o1
    return b0 + a0, b1 + a1, b1 - a1, b0 - a0


def derive_transposed(h0, h1, h2, h3):
    p0, m0, p1, m1 = h0 + h3, h0 - h3, h1 + h2, h1 - h2
    q = 1.25 * m0 + (0.25 * ROOT5) * m1
    o0 = -1.75 * p0 - 0.25 * p1
    o1 = (1.25 * ROOT5) * p0 - (0.25 * ROOT5) * p1
    return o0 - q, o1 + q, q - o1, -o0 - q


def at(ref, base, node):
    if isinstance(base, int):
        return ref.at[pl.ds(base + node * SUB, SUB), :]
    return ref.at[pl.ds(pl.multiple_of(base, SUB) + node * SUB, SUB), :]


def spread(src_ref, index, dst_ref, base):
    for k in range(SUB):
        block = src_ref[:, k * LANE : (k + 1) * LANE] if index is None else src_ref[index, :, k * LANE : (k + 1) * LANE]
        dst_ref[pl.ds(base + k, NODES, stride=SUB), :] = block


def gather_back(src_ref, base, dst_ref, index):
    for k in range(SUB):
        dst_ref[index, :, k * LANE : (k + 1) * LANE] = src_ref[pl.ds(base + k, NODES, stride=SUB), :]


def places():
    lane = lax.broadcasted_iota(jnp.int32, (SUB, LANE), 1)
    sub = lax.broadcasted_iota(jnp.int32, (SUB, LANE), 0)
    return lane, sub


def assemble_layers(ref, base, planes):
    lane, sub = places()
    zero = jnp.zeros((SUB, LANE), jnp.float32)
    not_first = lane % EX != 0
    not_last = lane % EX != EX - 1
    odd = sub % 2 == 1
    for c in range(planes):
        for b in range(4):
            n = 16 * c + 4 * b
            low_at, high_at = at(ref, base, n), at(ref, base, n + 3)
            low, high = low_at[...], high_at[...]
            low_at[...] = low + jnp.where(not_first, pltpu.roll(high, 1, 1), zero)
            high_at[...] = high + jnp.where(not_last, pltpu.roll(low, LANE - 1, 1), zero)
    for c in range(planes):
        for a in range(4):
            n = 16 * c + a
            low_at, high_at = at(ref, base, n), at(ref, base, n + 12)
            low, high = low_at[...], high_at[...]
            back = pltpu.roll(high, EX, 1)
            ahead = pltpu.roll(low, LANE - EX, 1)
            back = jnp.where(lane >= EX, back, jnp.where(odd, pltpu.roll(back, 1, 0), zero))
            ahead = jnp.where(lane < LANE - EX, ahead, jnp.where(odd, zero, pltpu.roll(ahead, SUB - 1, 0)))
            low_at[...] = low + back
            high_at[...] = high + ahead


def assemble(ref, base):
    _, sub = places()
    zero = jnp.zeros((SUB, LANE), jnp.float32)
    assemble_layers(ref, base, 4)
    for n in range(16):
        low_at, high_at = at(ref, base, n), at(ref, base, n + 48)
        low, high = low_at[...], high_at[...]
        low_at[...] = low + jnp.where(sub >= 2, pltpu.roll(high, 2, 0), zero)
        high_at[...] = high + jnp.where(sub < SUB - 2, pltpu.roll(low, SUB - 2, 0), zero)


def roll_sub(value, shift):
    shift = shift % SUB
    return value if shift == 0 else pltpu.roll(value, shift, 0)


def is_even():
    return lax.rem(lax.axis_index("space"), 2) == 0


def face_tiles(ref, base, b, low_first, high_first):
    _, sub = places()
    tiles = []
    for first, shift in ((low_first, 0), (high_first, 2)):
        pieces = [roll_sub(at(ref, base, first + 4 * b + a)[...], 2 * a + shift) for a in range(4)]
        tiles.append(
            jnp.where(
                sub < 4, jnp.where(sub < 2, pieces[0], pieces[1]), jnp.where(sub < 6, pieces[2], pieces[3])
            )
        )
    return tiles


def with_rim(value, node, near_ref, far_ref, rim_base):
    _, sub = places()
    zero = jnp.zeros((SUB, LANE), jnp.float32)
    c, b, a = node // 16, node // 4 % 4, node % 4
    if c not in (0, 3):
        return value
    near, far = at(near_ref, rim_base, b)[...], at(far_ref, rim_base, b)[...]
    if c == 0:
        return value + jnp.where(sub < 2, roll_sub(jnp.where(is_even(), far, near), -2 * a), zero)
    return value + jnp.where(sub >= 6, roll_sub(jnp.where(is_even(), near, far), 6 - 2 * a), zero)


def stiffness(ins, outs, stiff_ref, kern):
    for dim, lines in enumerate(LINES):
        for line in lines:
            stiff = [at(stiff_ref, 0, n)[...] for n in line]
            grads = []
            for (src, sbase), out in zip(ins, outs):
                g = derive(*[at(src, sbase, n)[...] for n in line])
                grads.append(g)
                if out is None:
                    continue
                dst, dbase = out
                back = derive_transposed(*[x * s for x, s in zip(g, stiff)])
                for n, x in zip(line, back):
                    place = at(dst, dbase, n)
                    place[...] = x if dim == 0 else place[...] + x
            if kern is not None:
                for i, n in enumerate(line):
                    place = at(kern, 0, n)
                    place[...] = place[...] + grads[0][i] * grads[1][i]


def place_kernel(
    owner_hbm, local_hbm, weights_hbm, records_hbm, out_hbm, token_ref,
    owner_ref, local_ref, weights_ref, records_ref, spot_ref, data_ref, sorted_ref, out_ref, sems, out_sems,
):
    copies = [
        pltpu.make_async_copy(src, dst, sems.at[i])
        for i, (src, dst) in enumerate(
            (
                (owner_hbm, owner_ref),
                (local_hbm, local_ref),
                (weights_hbm, weights_ref),
                (records_hbm, records_ref),
            )
        )
    ]
    for copy in copies:
        copy.start()
    token_ref[...] = jnp.zeros_like(token_ref)
    stations = weights_ref.shape[1]
    rows = sorted_ref.shape[0]
    events = records_ref.shape[0]
    few = events * STEPS + 1
    packed = 2 * (NODES + few)
    slabs = out_ref.shape[0] // packed
    blocks = stations // LANE
    chunks = stations // CAP
    owner_id = lax.broadcasted_iota(jnp.int32, (slabs, LANE), 0)
    before = lax.broadcasted_iota(jnp.int32, (LANE, LANE), 0) < lax.broadcasted_iota(jnp.int32, (LANE, LANE), 1)
    counting = jnp.concatenate(
        [jnp.where(before, 1.0, 0.0), jnp.ones((LANE, LANE), jnp.float32)], axis=1
    ).astype(jnp.bfloat16)
    copies[0].wait()
    named = [jnp.where(owner_ref[b : b + 1, :] == owner_id, 1.0, 0.0) for b in range(blocks)]
    counts = jnp.dot(
        jnp.concatenate(named, axis=0).astype(jnp.bfloat16), counting, preferred_element_type=jnp.float32
    )
    total = jnp.zeros((slabs, LANE), jnp.float32)
    earlier = []
    for b in range(blocks):
        part = counts[b * slabs : (b + 1) * slabs]
        earlier.append(part[:, :LANE] + total)
        total = total + part[:, LANE:]
    start = jnp.zeros((1, LANE), jnp.float32)
    starts = []
    for slab in range(slabs):
        starts.append(start)
        start = start + total[slab : slab + 1]
    starts = jnp.concatenate(starts, axis=0)
    for b in range(blocks):
        spot_ref[b : b + 1, :] = jnp.sum(named[b] * (earlier[b] + starts), axis=0, keepdims=True)
    first, count = starts.astype(jnp.int32), total.astype(jnp.int32)
    begins = [first[slab, 0] for slab in range(slabs)]
    sizes = [count[slab, 0] for slab in range(slabs)]
    for copy in copies[1:]:
        copy.wait()
    extra = rows - NODES - events * STEPS
    for b in range(blocks):
        cut = slice(b * LANE, (b + 1) * LANE)
        ids = jnp.broadcast_to(local_ref[b : b + 1, :].astype(jnp.float32), (extra, LANE))
        full = jnp.concatenate(
            [weights_ref[:, cut]] + [records_ref[event, :, cut] for event in range(events)] + [ids], axis=0
        )
        high = full.astype(jnp.bfloat16)
        data_ref[:rows, cut] = high
        data_ref[rows:, cut] = (full - high.astype(jnp.float32)).astype(jnp.bfloat16)
    slot = lax.broadcasted_iota(jnp.int32, (CAP, LANE), 0).astype(jnp.bfloat16)
    lane = lax.broadcasted_iota(jnp.int32, (SUB, LANE), 1)
    sorted_ref[:, stations:] = jnp.zeros((rows, 3 * LANE), jnp.float32)

    leaving = []

    def cut_block(slab):
        begin, size = begins[slab], sizes[slab]
        shift = lax.rem(begin, LANE)
        base = begin - shift
        turn = lax.rem(LANE - shift, LANE)
        kept_lanes = lane >= shift
        for first in range(0, rows, SUB):
            tiles = [
                sorted_ref[first : first + SUB, pl.ds(pl.multiple_of(base + j * LANE, LANE), LANE)] for j in range(3)
            ]
            for j in range(2):
                piece = pltpu.roll(jnp.where(kept_lanes, tiles[j], tiles[j + 1]), turn, 1)
                if first < NODES:
                    out_ref[pl.ds(slab * packed + j * NODES + first, SUB), :] = piece
                else:
                    piece = jnp.where(lane + j * LANE < size, piece, 0.0)
                    out_ref[pl.ds(slab * packed + 2 * NODES + j * few, few), :] = piece[:few]
        if slab % 4 == 3:
            part = pl.ds((slab - 3) * packed, 4 * packed)
            leaving.append(pltpu.make_async_copy(out_ref.at[part], out_hbm.at[part], out_sems.at[slab // 4]))
            leaving[-1].start()

    for chunk in range(chunks):
        spots = spot_ref[...] - float(chunk * CAP)
        wanted = jnp.where((spots >= 0.0) & (spots < CAP), spots, -1.0)
        hot = [
            jnp.where(slot == wanted[b : b + 1, :].astype(jnp.bfloat16), jnp.bfloat16(1), jnp.bfloat16(0))
            for b in range(blocks)
        ]
        placed = lax.dot_general(
            data_ref[...],
            jnp.concatenate(hot, axis=1),
            (((1,), (1,)), ((), ())),
            preferred_element_type=jnp.float32,
        )
        sorted_ref[:, chunk * CAP : (chunk + 1) * CAP] = placed[:rows] + placed[rows:]
        cut_block(chunk)
    for slab in range(chunks, slabs):
        cut_block(slab)
    for copy in leaving:
        copy.wait()


def split(full):
    high = full.astype(jnp.bfloat16)
    return jnp.concatenate([high, (full - high.astype(jnp.float32)).astype(jnp.bfloat16)], axis=0)


def land(got_ref, events, wants, acc_refs):
    few = events * STEPS + 1
    packed = 2 * (NODES + few)
    slabs = got_ref.shape[0] // packed
    group = min(slabs, 16)
    slot = lax.broadcasted_iota(jnp.int32, (CAP, LANE), 0).astype(jnp.bfloat16)
    if slabs > group:
        for acc_ref in acc_refs:
            acc_ref[...] = jnp.zeros_like(acc_ref)

    def one(g, _):
        items = {item: [] for _, chosen in wants for item in chosen}
        hot = [[] for _ in wants]
        for i in range(group):
            src = g * group + i
            for (first, last, step), found in items.items():
                for j in range(2):
                    weights = got_ref[pl.ds(src * packed + j * NODES + first, last - first), :]
                    samples = [
                        got_ref[pl.ds(src * packed + 2 * NODES + j * few + event * STEPS + step, 1), :]
                        for event in range(events)
                    ]
                    found.append(split(jnp.concatenate([weights * sample for sample in samples], axis=0)))
            ids = [
                got_ref[pl.ds(src * packed + 2 * NODES + (j + 1) * few - 1, 1), :].astype(jnp.int32) for j in range(2)
            ]
            for at_hot, (quarter, _) in zip(hot, wants):
                for half in ids:
                    wanted = jnp.where(half // CAP == quarter, half % CAP, -1).astype(jnp.float32).astype(jnp.bfloat16)
                    at_hot.append(jnp.where(slot == wanted, jnp.bfloat16(1), jnp.bfloat16(0)))
        left = {item: jnp.concatenate(found, axis=1) for item, found in items.items()}
        for at_hot, (_, chosen), acc_ref in zip(hot, wants, acc_refs):
            landed = lax.dot_general(
                jnp.concatenate([left[item] for item in chosen], axis=0),
                jnp.concatenate(at_hot, axis=1),
                (((1,), (1,)), ((), ())),
                preferred_element_type=jnp.float32,
            )
            at_in, at_out = 0, 0
            for first, last, _ in chosen:
                count = events * (last - first)
                rows = slice(at_out, at_out + count)
                both = landed[at_in : at_in + count] + landed[at_in + count : at_in + 2 * count]
                acc_ref[rows, :] = acc_ref[rows, :] + both if slabs > group else both
                at_in, at_out = at_in + 2 * count, at_out + count
        return 0

    if slabs > group:
        lax.fori_loop(0, slabs // group, one, 0)
    else:
        one(0, 0)


FACE_WANTS = ((0, ((0, 16, 0), (0, 16, 1))), (3, ((48, 64, 0), (48, 64, 1))))
FIRST_WANTS = ((0, ((0, NODES, 0), (0, NODES, 1))),) + tuple((q, ((0, NODES, 0),)) for q in range(1, 4))
LATER_WANTS = tuple((q, ((0, NODES, 1),)) for q in range(1, 4))


def sums(events, wants):
    return [
        ((sum(events * (last - first) for first, last, _ in chosen), CAP), jnp.float32) for _, chosen in wants
    ]


def spread_source(events, acc_refs, skip, out_ref):
    for event in range(events):
        for k in range(SUB):
            cut = slice(k % 2 * LANE, (k % 2 + 1) * LANE)
            first = event * NODES + (skip if k < 2 else 0)
            rows = slice(first, first + NODES)
            out_ref[pl.ds(event * FIELD + k, NODES, stride=SUB), :] = acc_refs[k // 2][rows, cut]
        assemble(out_ref, event * FIELD)


def land_faces_kernel(events, got_ref, faces_hbm, near_ref, far_ref, faces_ref, source_ref, low_ref, high_ref, sem):
    copy = pltpu.make_async_copy(faces_hbm, faces_ref, sem)
    copy.start()
    land(got_ref, events, FACE_WANTS, (low_ref, high_ref))
    source_ref[...] = jnp.zeros_like(source_ref)
    for each in range(STEPS * events):
        rows = slice(each * 16, (each + 1) * 16)
        for j in range(2):
            cut = slice(j * LANE, (j + 1) * LANE)
            source_ref[pl.ds(each * 16 * SUB + j, 16, stride=SUB), :] = low_ref[rows, cut]
            source_ref[pl.ds(each * 16 * SUB + SUB - 2 + j, 16, stride=SUB), :] = high_ref[rows, cut]
        assemble_layers(source_ref, each * 16 * SUB, 1)
    copy.wait()
    even = is_even()
    fields = 2 * events + 1
    for field in range(fields + events):
        for b in range(4):
            if field < fields:
                low = at(faces_ref, field * FACE, b)[...]
                high = at(faces_ref, (fields + field) * FACE, b)[...]
            if events <= field < 2 * events:
                source_low, source_high = face_tiles(source_ref, (field - events) * 16 * SUB, b, 0, 0)
                low, high = low - source_low, high - source_high
            if field >= fields:
                low, high = face_tiles(source_ref, (events + field - fields) * 16 * SUB, b, 0, 0)
            at(near_ref, field * FACE, b)[...] = jnp.where(even, high, low)
            at(far_ref, field * FACE, b)[...] = jnp.where(even, low, high)


def state_rows(events):
    counts = {"force": 2 * events, "mass": 1, "base": 2 * events, "stiff": 1, "kern": 1}
    rows, total = {}, 0
    for name, count in counts.items():
        rows[name] = total * FIELD
        total += count
    return rows, total * FIELD


def land_first_kernel(
    events, got_ref, state_hbm, now_hbm, state_ref, now_ref, acc0, source_ref, acc1, acc2, acc3, sems
):
    copies = [
        pltpu.make_async_copy(state_hbm, state_ref, sems.at[0]),
        pltpu.make_async_copy(now_hbm, now_ref, sems.at[1]),
    ]
    for copy in copies:
        copy.start()
    land(got_ref, events, FIRST_WANTS, (acc0, acc1, acc2, acc3))
    spread_source(events, (acc0, acc1, acc2, acc3), 0, source_ref)
    for copy in copies:
        copy.wait()
    rows, _ = state_rows(events)
    for event in range(events):
        for n in range(NODES):
            place = at(state_ref, rows["force"] + (events + event) * FIELD, n)
            place[...] = place[...] - at(source_ref, event * FIELD, n)[...]


def land_later_kernel(
    events, got_ref, new_ref, acc0, fwd_hbm, adj_hbm, source_ref, out_ref, acc1, acc2, acc3, sems
):
    copies = []
    for event in range(events):
        for field, out_hbm in ((event, fwd_hbm), (events + event, adj_hbm)):
            gather_back(new_ref, field * FIELD, out_ref, field)
            copies.append(pltpu.make_async_copy(out_ref.at[field], out_hbm.at[event], sems.at[field]))
            copies[-1].start()
    land(got_ref, events, LATER_WANTS, (acc1, acc2, acc3))
    spread_source(events, (acc0, acc1, acc2, acc3), events * NODES, source_ref)
    for copy in copies:
        copy.wait()


def first_kernel(
    events, fwd_ref, fwd_prev_ref, adj_ref, adj_prev_ref, shear_ref, density_ref, _, state_ref, now_ref, faces_ref, prev_ref
):
    rows, _ = state_rows(events)
    stiff_ref, kern_ref = (state_ref.at[pl.ds(rows[name], FIELD), :] for name in ("stiff", "kern"))
    spread(shear_ref, None, state_ref, rows["stiff"])
    for n in range(NODES):
        place = at(stiff_ref, 0, n)
        place[...] = place[...] * WEIGHT[n]
        at(kern_ref, 0, n)[...] = jnp.zeros((SUB, LANE), jnp.float32)
        at(state_ref, rows["mass"], n)[...] = density_ref[...] * WEIGHT[n]

    def one(event, _):
        u, v = event * FIELD, (events + event) * FIELD
        for now_src, prev_src, field in ((fwd_ref, fwd_prev_ref, u), (adj_ref, adj_prev_ref, v)):
            spread(now_src, event, now_ref, field)
            spread(prev_src, event, prev_ref, 0)
            for n in range(NODES):
                at(state_ref, rows["base"] + field, n)[...] = 2.0 * at(now_ref, field, n)[...] - at(prev_ref, 0, n)[...]
        stiffness(
            [(now_ref, u), (now_ref, v)],
            [(state_ref, rows["force"] + u), (state_ref, rows["force"] + v)],
            stiff_ref,
            kern_ref,
        )
        return 0

    lax.fori_loop(0, events, one, 0)
    fields = 2 * events + 1

    def join(field, _):
        assemble(state_ref, rows["force"] + field * FIELD)
        for b in range(4):
            low, high = face_tiles(state_ref, rows["force"] + field * FIELD, b, 0, 48)
            at(faces_ref, field * FACE, b)[...] = low
            at(faces_ref, (fields + field) * FACE, b)[...] = high
        return 0

    lax.fori_loop(0, fields, join, 0)


def second_kernel(
    events, share, position_ref, state_ref, now_ref, far_rim_ref, near_rim_ref,
    new_ref, base_ref, factor_ref, next_ref, parts_ref, near_ref, far_ref, later_ref, kern_ref,
):
    rows, _ = state_rows(events)
    stiff_ref = state_ref.at[pl.ds(rows["stiff"], FIELD), :]
    kern_ref[...] = state_ref[pl.ds(rows["kern"], FIELD), :]
    mass = 2 * events
    for side, rim_ref in enumerate((near_rim_ref, far_rim_ref)):
        for row in range(0, events * FACE, SUB):
            later_ref[side, row : row + SUB, :] = rim_ref[(mass + 1) * FACE + row : (mass + 1) * FACE + row + SUB, :]
    even = is_even()
    for n in range(NODES):
        at(factor_ref, 0, n)[...] = STEP_SQUARE / with_rim(
            at(state_ref, rows["mass"], n)[...], n, near_rim_ref, far_rim_ref, mass * FACE
        )

    def one(event, _):
        u, v = event * FIELD, (events + event) * FIELD
        for field, rim in ((u, event), (v, events + event)):
            for n in range(NODES):
                force = with_rim(at(state_ref, rows["force"] + field, n)[...], n, near_rim_ref, far_rim_ref, rim * FACE)
                new = at(state_ref, rows["base"] + field, n)[...] - at(factor_ref, 0, n)[...] * force
                at(new_ref, field, n)[...] = new
                at(base_ref, field, n)[...] = 2.0 * new - at(now_ref, field, n)[...]
        stiffness([(new_ref, u), (new_ref, v)], [(next_ref, u), (next_ref, v)], stiff_ref, kern_ref)
        assemble(next_ref, u)
        assemble(next_ref, v)
        for field in (u, v):
            for b in range(4):
                low, high = face_tiles(next_ref, field, b, 0, 48)
                at(near_ref, field // NODES * 4, b)[...] = jnp.where(even, high, low)
                at(far_ref, field // NODES * 4, b)[...] = jnp.where(even, low, high)
        return 0

    lax.fori_loop(0, events, one, 0)
    for n in range(NODES):
        place = at(kern_ref, 0, n)
        place[...] = -TIME_STEP * at(stiff_ref, 0, n)[...] * place[...]
    tiles = SUB // share
    for j in range(share):
        owner = lax.rem(position_ref[0] + j, share)
        for k in range(tiles):
            parts_ref[j, :, k * LANE : (k + 1) * LANE] = kern_ref[pl.ds(owner * tiles + k, NODES, stride=SUB), :]


def last_kernel(events, share, base_ref, factor_ref, next_ref, source_ref, later_ref, *rest):
    far_rim_ref, near_rim_ref, fwd_hbm, adj_hbm, kernel_hbm, done_ref, out_ref, kernel_ref, sems = rest[share:]
    total = rest[0][0]
    for part in rest[1:share]:
        total = total + part[0]
    kernel_ref[...] = total
    copies = [pltpu.make_async_copy(kernel_ref, kernel_hbm, sems.at[2 * events])]
    copies[0].start()
    for event in range(events):
        for field, out_hbm in ((event, fwd_hbm), (events + event, adj_hbm)):
            for n in range(NODES):
                force = with_rim(at(next_ref, field * FIELD, n)[...], n, near_rim_ref, far_rim_ref, field * FACE)
                if field >= events:
                    source = at(source_ref, event * FIELD, n)[...]
                    force = force - with_rim(source, n, later_ref.at[0], later_ref.at[1], event * FACE)
                at(done_ref, 0, n)[...] = at(base_ref, field * FIELD, n)[...] - at(factor_ref, 0, n)[...] * force
            gather_back(done_ref, 0, out_ref, field)
            copies.append(pltpu.make_async_copy(out_ref.at[field], out_hbm.at[event], sems.at[field]))
            copies[-1].start()
    for copy in copies:
        copy.wait()


def call(body, outs, scratch=(), cost=2_000_000, smem=0, count=0, outside=0, limit=24, written=0):
    in_specs = [pl.BlockSpec(memory_space=pltpu.SMEM)] * smem
    in_specs += [pl.BlockSpec(memory_space=pltpu.VMEM)] * (count - smem - outside)
    in_specs += [pl.BlockSpec(memory_space=pl.ANY)] * outside
    return pl.pallas_call(
        body,
        out_shape=[out if not isinstance(out, tuple) else jax.ShapeDtypeStruct(out, jnp.float32) for out in outs],
        in_specs=in_specs,
        out_specs=[pl.BlockSpec(memory_space=pl.ANY)] * written
        + [pl.BlockSpec(memory_space=pltpu.VMEM)] * (len(outs) - written),
        scratch_shapes=[pltpu.VMEM(*x) if isinstance(x, tuple) else x for x in scratch],
        compiler_params=pltpu.CompilerParams(vmem_limit_bytes=limit * 1024 * 1024),
        cost_estimate=pl.CostEstimate(flops=cost, bytes_accessed=cost, transcendentals=0),
    )


def near_core(shape):
    return pltpu.VMEM(shape, jnp.float32)


def off_core(shape):
    return pltpu.HBM(shape, jnp.float32)


def kept(*arrays):
    return [pltpu.with_memory_space_constraint(x, pltpu.VMEM) for x in arrays]


def far_off(*arrays):
    return [pltpu.with_memory_space_constraint(x, pltpu.HBM) for x in arrays]


def beside(near, far):
    count = lax.axis_size("space")
    inner = [pair for i in range(1, count - 1, 2) for pair in ((i, i + 1), (i + 1, i))]
    from_far = lax.ppermute(far, "space", inner)
    from_near = lax.ppermute(near, "space", [(i, i + 1 - 2 * (i % 2)) for i in range(count)])
    return from_near, from_far


def shards(
    fwd_now,
    fwd_prev,
    adj_now,
    adj_prev,
    shear_mod,
    density,
    station_owner,
    receiver_local,
    station_weights,
    adj_records,
):
    events = fwd_now.shape[0]
    stations = station_owner.shape[0]
    elements = fwd_now.shape[-1]
    slabs = lax.axis_size("space")
    share = lax.axis_size("event")
    f32 = jnp.float32
    rows = -(-(NODES + events * STEPS + 1) // SUB) * SUB
    packed = 2 * (NODES + events * STEPS + 1)
    blocks = stations // LANE

    send, token = call(
        place_kernel,
        [(slabs * packed, LANE), near_core((SUB, LANE))],
        [
            ((blocks, LANE), jnp.int32),
            ((blocks, LANE), jnp.int32),
            ((NODES, stations), f32),
            ((events, STEPS, stations), f32),
            ((blocks, LANE), f32),
            ((2 * rows, stations), jnp.bfloat16),
            ((rows, stations + 3 * LANE), f32),
            ((slabs * packed, LANE), f32),
            pltpu.SemaphoreType.DMA((4,)),
            pltpu.SemaphoreType.DMA((slabs // 4,)),
        ],
        written=1,
        count=4,
        outside=4,
        limit=48,
    )(
        *far_off(
            station_owner.reshape(blocks, LANE), receiver_local.reshape(blocks, LANE), station_weights, adj_records
        )
    )
    send = send.reshape(slabs, packed // 2, 2, LANE)
    got = lax.all_to_all(send, "space", split_axis=0, concat_axis=0, tiled=True).reshape(slabs * packed, LANE)

    fields = 2 * events + 1
    state, now, faces = call(
        functools.partial(first_kernel, events),
        [
            off_core((state_rows(events)[1], LANE)),
            off_core((2 * events * FIELD, LANE)),
            off_core((2 * fields * FACE, LANE)),
        ],
        [((FIELD, LANE), f32)],
        count=7,
    )(*far_off(fwd_now, fwd_prev, adj_now, adj_prev, shear_mod, density.reshape(SUB, LANE)), *kept(token))
    near, far = call(
        functools.partial(land_faces_kernel, events),
        [((fields + events) * FACE, LANE)] * 2,
        [((2 * fields * FACE, LANE), f32), ((STEPS * events * 16 * SUB, LANE), f32)]
        + sums(events, FACE_WANTS)
        + [pltpu.SemaphoreType.DMA(())],
        count=2,
        outside=1,
    )(got, *far_off(faces))
    near_rim, far_rim = beside(near, far)
    state, now, quarter = call(
        functools.partial(land_first_kernel, events),
        [near_core(state.shape), near_core(now.shape), near_core((STEPS * events * NODES, CAP))],
        [((events * FIELD, LANE), f32)] + sums(events, FIRST_WANTS[1:]) + [pltpu.SemaphoreType.DMA((2,))],
        count=3,
        outside=2,
        limit=40,
    )(got, *far_off(state, now))
    new, base, factor, after, parts, near, far, later = call(
        functools.partial(second_kernel, events, share),
        [
            near_core((2 * events * FIELD, LANE)),
            near_core((2 * events * FIELD, LANE)),
            near_core((FIELD, LANE)),
            near_core((2 * events * FIELD, LANE)),
            (share, NODES, elements // share),
            (2 * events * FACE, LANE),
            (2 * events * FACE, LANE),
            near_core((2, events * FACE, LANE)),
        ],
        [((FIELD, LANE), f32)],
        smem=1,
        count=5,
    )(lax.axis_index("event").reshape(1).astype(jnp.int32), *kept(state, now), far_rim, near_rim)
    near_rim, far_rim = beside(near, far)
    pieces = [parts[0:1]] + [
        lax.ppermute(parts[j : j + 1], "event", [(i, (i + j) % share) for i in range(share)]) for j in range(1, share)
    ]
    fwd_before, adj_before, source = call(
        functools.partial(land_later_kernel, events),
        [fwd_now.shape, adj_now.shape, near_core((events * FIELD, LANE))],
        [((2 * events, NODES, elements), f32)]
        + sums(events, LATER_WANTS)
        + [pltpu.SemaphoreType.DMA((2 * events,))],
        count=3,
        limit=40,
        written=2,
    )(got, *kept(new, quarter))
    fwd_last, adj_last, kernel = call(
        functools.partial(last_kernel, events, share),
        [fwd_now.shape, adj_now.shape, (NODES, elements // share)],
        [
            ((FIELD, LANE), f32),
            ((2 * events, NODES, elements), f32),
            ((NODES, elements // share), f32),
            pltpu.SemaphoreType.DMA((2 * events + 1,)),
        ],
        count=7 + share,
        written=3,
    )(*kept(base, factor, after, source, later), *pieces, far_rim, near_rim)
    return fwd_last, fwd_before, adj_last, adj_before, kernel


def solution(mesh):
    in_specs = (
        P("event", None, "space"),
        P("event", None, "space"),
        P("event", None, "space"),
        P("event", None, "space"),
        P(None, "space"),
        P("space"),
        P("space", None),
        P("space"),
        P(None, "space"),
        P("event", None, "space"),
    )
    out_specs = (
        P("event", None, "space"),
        P("event", None, "space"),
        P("event", None, "space"),
        P("event", None, "space"),
        P(None, ("space", "event")),
    )
    return jax.shard_map(shards, mesh=mesh, in_specs=in_specs, out_specs=out_specs, check_vma=False)
```

```python
import functools

import jax
import jax.numpy as jnp
import numpy as np
from jax import lax
from jax.experimental import pallas as pl
from jax.experimental.pallas import tpu as pltpu
from jax.sharding import PartitionSpec as P

EX = 16
EY = 16
STEPS = 2
CAP = 256
NODES = 64
SUB = 8
LANE = 128
FIELD = NODES * SUB
FACE = 4 * SUB


TIME_STEP = 0.08
STEP_SQUARE = 0.0064

EDGE = np.array([1.0 / 6.0, 5.0 / 6.0, 5.0 / 6.0, 1.0 / 6.0])
WEIGHT = [float(np.float32(EDGE[n // 16] * EDGE[n // 4 % 4] * EDGE[n % 4])) for n in range(NODES)]
ROOT5 = float(np.sqrt(5.0))

LINES = (
    [[16 * c + 4 * b + i for i in range(4)] for c in range(4) for b in range(4)],
    [[16 * c + 4 * i + a for i in range(4)] for c in range(4) for a in range(4)],
    [[16 * i + 4 * b + a for i in range(4)] for b in range(4) for a in range(4)],
)


def derive(x0, x1, x2, x3):
    o0, o1 = x0 - x3, x1 - x2
    q = (x1 + x2) - (x0 + x3)
    a0, a1 = 1.25 * q, (0.25 * ROOT5) * q
    b0 = -1.75 * o0 + (1.25 * ROOT5) * o1
    b1 = -0.25 * o0 - (0.25 * ROOT5) * o1
    return b0 + a0, b1 + a1, b1 - a1, b0 - a0


def derive_transposed(h0, h1, h2, h3):
    p0, m0, p1, m1 = h0 + h3, h0 - h3, h1 + h2, h1 - h2
    q = 1.25 * m0 + (0.25 * ROOT5) * m1
    o0 = -1.75 * p0 - 0.25 * p1
    o1 = (1.25 * ROOT5) * p0 - (0.25 * ROOT5) * p1
    return o0 - q, o1 + q, q - o1, -o0 - q


def at(ref, base, node):
    if isinstance(base, int):
        return ref.at[pl.ds(base + node * SUB, SUB), :]
    return ref.at[pl.ds(pl.multiple_of(base, SUB) + node * SUB, SUB), :]


def spread(src_ref, index, dst_ref, base):
    for k in range(SUB):
        block = src_ref[:, k * LANE : (k + 1) * LANE] if index is None else src_ref[index, :, k * LANE : (k + 1) * LANE]
        dst_ref[pl.ds(base + k, NODES, stride=SUB), :] = block


def gather_back(src_ref, base, dst_ref, index):
    for k in range(SUB):
        dst_ref[index, :, k * LANE : (k + 1) * LANE] = src_ref[pl.ds(base + k, NODES, stride=SUB), :]


def places():
    lane = lax.broadcasted_iota(jnp.int32, (SUB, LANE), 1)
    sub = lax.broadcasted_iota(jnp.int32, (SUB, LANE), 0)
    return lane, sub


def assemble_layers(ref, base, planes):
    lane, sub = places()
    zero = jnp.zeros((SUB, LANE), jnp.float32)
    not_first = lane % EX != 0
    not_last = lane % EX != EX - 1
    odd = sub % 2 == 1
    for c in range(planes):
        for b in range(4):
            n = 16 * c + 4 * b
            low_at, high_at = at(ref, base, n), at(ref, base, n + 3)
            low, high = low_at[...], high_at[...]
            low_at[...] = low + jnp.where(not_first, pltpu.roll(high, 1, 1), zero)
            high_at[...] = high + jnp.where(not_last, pltpu.roll(low, LANE - 1, 1), zero)
    for c in range(planes):
        for a in range(4):
            n = 16 * c + a
            low_at, high_at = at(ref, base, n), at(ref, base, n + 12)
            low, high = low_at[...], high_at[...]
            back = pltpu.roll(high, EX, 1)
            ahead = pltpu.roll(low, LANE - EX, 1)
            back = jnp.where(lane >= EX, back, jnp.where(odd, pltpu.roll(back, 1, 0), zero))
            ahead = jnp.where(lane < LANE - EX, ahead, jnp.where(odd, zero, pltpu.roll(ahead, SUB - 1, 0)))
            low_at[...] = low + back
            high_at[...] = high + ahead


def assemble(ref, base):
    _, sub = places()
    zero = jnp.zeros((SUB, LANE), jnp.float32)
    assemble_layers(ref, base, 4)
    for n in range(16):
        low_at, high_at = at(ref, base, n), at(ref, base, n + 48)
        low, high = low_at[...], high_at[...]
        low_at[...] = low + jnp.where(sub >= 2, pltpu.roll(high, 2, 0), zero)
        high_at[...] = high + jnp.where(sub < SUB - 2, pltpu.roll(low, SUB - 2, 0), zero)


def roll_sub(value, shift):
    shift = shift % SUB
    return value if shift == 0 else pltpu.roll(value, shift, 0)


def is_even():
    return lax.rem(lax.axis_index("space"), 2) == 0


def face_tiles(ref, base, b, low_first, high_first):
    _, sub = places()
    tiles = []
    for first, shift in ((low_first, 0), (high_first, 2)):
        pieces = [roll_sub(at(ref, base, first + 4 * b + a)[...], 2 * a + shift) for a in range(4)]
        tiles.append(
            jnp.where(
                sub < 4, jnp.where(sub < 2, pieces[0], pieces[1]), jnp.where(sub < 6, pieces[2], pieces[3])
            )
        )
    return tiles


def with_rim(value, node, near_ref, far_ref, rim_base):
    _, sub = places()
    zero = jnp.zeros((SUB, LANE), jnp.float32)
    c, b, a = node // 16, node // 4 % 4, node % 4
    if c not in (0, 3):
        return value
    near, far = at(near_ref, rim_base, b)[...], at(far_ref, rim_base, b)[...]
    if c == 0:
        return value + jnp.where(sub < 2, roll_sub(jnp.where(is_even(), far, near), -2 * a), zero)
    return value + jnp.where(sub >= 6, roll_sub(jnp.where(is_even(), near, far), 6 - 2 * a), zero)


def stiffness(ins, outs, stiff_ref, kern):
    for dim, lines in enumerate(LINES):
        for line in lines:
            stiff = [at(stiff_ref, 0, n)[...] for n in line]
            grads = []
            for (src, sbase), out in zip(ins, outs):
                g = derive(*[at(src, sbase, n)[...] for n in line])
                grads.append(g)
                if out is None:
                    continue
                dst, dbase = out
                back = derive_transposed(*[x * s for x, s in zip(g, stiff)])
                for n, x in zip(line, back):
                    place = at(dst, dbase, n)
                    place[...] = x if dim == 0 else place[...] + x
            if kern is not None:
                for i, n in enumerate(line):
                    place = at(kern, 0, n)
                    place[...] = place[...] + grads[0][i] * grads[1][i]


def place_kernel(
    owner_hbm, local_hbm, weights_hbm, records_hbm, out_ref, token_ref,
    owner_ref, local_ref, weights_ref, records_ref, spot_ref, data_ref, sorted_ref, sems,
):
    copies = [
        pltpu.make_async_copy(src, dst, sems.at[i])
        for i, (src, dst) in enumerate(
            (
                (owner_hbm, owner_ref),
                (local_hbm, local_ref),
                (weights_hbm, weights_ref),
                (records_hbm, records_ref),
            )
        )
    ]
    for copy in copies:
        copy.start()
    token_ref[...] = jnp.zeros_like(token_ref)
    stations = weights_ref.shape[1]
    rows = sorted_ref.shape[0]
    events = records_ref.shape[0]
    few = events * STEPS + 1
    packed = 2 * (NODES + few)
    slabs = out_ref.shape[0] // packed
    blocks = stations // LANE
    chunks = stations // CAP
    owner_id = lax.broadcasted_iota(jnp.int32, (slabs, LANE), 0)
    before = lax.broadcasted_iota(jnp.int32, (LANE, LANE), 0) < lax.broadcasted_iota(jnp.int32, (LANE, LANE), 1)
    counting = jnp.concatenate(
        [jnp.where(before, 1.0, 0.0), jnp.ones((LANE, LANE), jnp.float32)], axis=1
    ).astype(jnp.bfloat16)
    copies[0].wait()
    named = [jnp.where(owner_ref[b : b + 1, :] == owner_id, 1.0, 0.0) for b in range(blocks)]
    counts = jnp.dot(
        jnp.concatenate(named, axis=0).astype(jnp.bfloat16), counting, preferred_element_type=jnp.float32
    )
    total = jnp.zeros((slabs, LANE), jnp.float32)
    earlier = []
    for b in range(blocks):
        part = counts[b * slabs : (b + 1) * slabs]
        earlier.append(part[:, :LANE] + total)
        total = total + part[:, LANE:]
    start = jnp.zeros((1, LANE), jnp.float32)
    starts = []
    for slab in range(slabs):
        starts.append(start)
        start = start + total[slab : slab + 1]
    starts = jnp.concatenate(starts, axis=0)
    for b in range(blocks):
        spot_ref[b : b + 1, :] = jnp.sum(named[b] * (earlier[b] + starts), axis=0, keepdims=True)
    first, count = starts.astype(jnp.int32), total.astype(jnp.int32)
    begins = [first[slab, 0] for slab in range(slabs)]
    sizes = [count[slab, 0] for slab in range(slabs)]
    for copy in copies[1:]:
        copy.wait()
    extra = rows - NODES - events * STEPS
    for b in range(blocks):
        cut = slice(b * LANE, (b + 1) * LANE)
        ids = jnp.broadcast_to(local_ref[b : b + 1, :].astype(jnp.float32), (extra, LANE))
        full = jnp.concatenate(
            [weights_ref[:, cut]] + [records_ref[event, :, cut] for event in range(events)] + [ids], axis=0
        )
        high = full.astype(jnp.bfloat16)
        data_ref[:rows, cut] = high
        data_ref[rows:, cut] = (full - high.astype(jnp.float32)).astype(jnp.bfloat16)
    slot = lax.broadcasted_iota(jnp.int32, (CAP, LANE), 0).astype(jnp.bfloat16)
    lane = lax.broadcasted_iota(jnp.int32, (SUB, LANE), 1)
    sorted_ref[:, stations:] = jnp.zeros((rows, 3 * LANE), jnp.float32)

    def cut_block(slab):
        begin, size = begins[slab], sizes[slab]
        shift = lax.rem(begin, LANE)
        base = begin - shift
        late = lane >= shift
        slots = (jnp.where(late, lane - shift, lane + 2 * LANE - shift), lane + LANE - shift)
        for first in range(0, rows, SUB):
            tiles = [
                sorted_ref[first : first + SUB, pl.ds(pl.multiple_of(base + j * LANE, LANE), LANE)] for j in range(3)
            ]
            for j, piece in enumerate((jnp.where(late, tiles[0], tiles[2]), tiles[1])):
                if first < NODES:
                    out_ref[pl.ds(slab * packed + j * NODES + first, SUB), :] = piece
                else:
                    piece = jnp.where(slots[j] < size, piece, 0.0)
                    out_ref[pl.ds(slab * packed + 2 * NODES + j * few, few), :] = piece[:few]

    for chunk in range(chunks):
        spots = spot_ref[...] - float(chunk * CAP)
        wanted = jnp.where((spots >= 0.0) & (spots < CAP), spots, -1.0)
        hot = [
            jnp.where(slot == wanted[b : b + 1, :].astype(jnp.bfloat16), jnp.bfloat16(1), jnp.bfloat16(0))
            for b in range(blocks)
        ]
        placed = lax.dot_general(
            data_ref[...],
            jnp.concatenate(hot, axis=1),
            (((1,), (1,)), ((), ())),
            preferred_element_type=jnp.float32,
        )
        sorted_ref[:, chunk * CAP : (chunk + 1) * CAP] = placed[:rows] + placed[rows:]
        cut_block(chunk)
    for slab in range(chunks, slabs):
        cut_block(slab)


def split(full):
    high = full.astype(jnp.bfloat16)
    return jnp.concatenate([high, (full - high.astype(jnp.float32)).astype(jnp.bfloat16)], axis=0)


def land(got_ref, events, wants, acc_refs):
    few = events * STEPS + 1
    packed = 2 * (NODES + few)
    slabs = got_ref.shape[0] // packed
    group = min(slabs, 16)
    slot = lax.broadcasted_iota(jnp.int32, (CAP, LANE), 0).astype(jnp.bfloat16)
    if slabs > group:
        for acc_ref in acc_refs:
            acc_ref[...] = jnp.zeros_like(acc_ref)

    def one(g, _):
        items = {item: [] for _, chosen in wants for item in chosen}
        hot = [[] for _ in wants]
        for i in range(group):
            src = g * group + i
            for (first, last, step), found in items.items():
                for j in range(2):
                    weights = got_ref[pl.ds(src * packed + j * NODES + first, last - first), :]
                    samples = [
                        got_ref[pl.ds(src * packed + 2 * NODES + j * few + event * STEPS + step, 1), :]
                        for event in range(events)
                    ]
                    found.append(split(jnp.concatenate([weights * sample for sample in samples], axis=0)))
            ids = [
                got_ref[pl.ds(src * packed + 2 * NODES + (j + 1) * few - 1, 1), :].astype(jnp.int32) for j in range(2)
            ]
            for at_hot, (quarter, _) in zip(hot, wants):
                for half in ids:
                    wanted = jnp.where(half // CAP == quarter, half % CAP, -1).astype(jnp.float32).astype(jnp.bfloat16)
                    at_hot.append(jnp.where(slot == wanted, jnp.bfloat16(1), jnp.bfloat16(0)))
        left = {item: jnp.concatenate(found, axis=1) for item, found in items.items()}
        for at_hot, (_, chosen), acc_ref in zip(hot, wants, acc_refs):
            landed = lax.dot_general(
                jnp.concatenate([left[item] for item in chosen], axis=0),
                jnp.concatenate(at_hot, axis=1),
                (((1,), (1,)), ((), ())),
                preferred_element_type=jnp.float32,
            )
            at_in, at_out = 0, 0
            for first, last, _ in chosen:
                count = events * (last - first)
                rows = slice(at_out, at_out + count)
                both = landed[at_in : at_in + count] + landed[at_in + count : at_in + 2 * count]
                acc_ref[rows, :] = acc_ref[rows, :] + both if slabs > group else both
                at_in, at_out = at_in + 2 * count, at_out + count
        return 0

    if slabs > group:
        lax.fori_loop(0, slabs // group, one, 0)
    else:
        one(0, 0)


FACE_WANTS = ((0, ((0, 16, 0), (0, 16, 1))), (3, ((48, 64, 0), (48, 64, 1))))
FIRST_WANTS = ((0, ((0, NODES, 0), (0, NODES, 1))),) + tuple((q, ((0, NODES, 0),)) for q in range(1, 4))
LATER_WANTS = tuple((q, ((0, NODES, 1),)) for q in range(1, 4))


def sums(events, wants):
    return [
        ((sum(events * (last - first) for first, last, _ in chosen), CAP), jnp.float32) for _, chosen in wants
    ]


def spread_source(events, acc_refs, skip, out_ref):
    for event in range(events):
        for k in range(SUB):
            cut = slice(k % 2 * LANE, (k % 2 + 1) * LANE)
            first = event * NODES + (skip if k < 2 else 0)
            rows = slice(first, first + NODES)
            out_ref[pl.ds(event * FIELD + k, NODES, stride=SUB), :] = acc_refs[k // 2][rows, cut]
        assemble(out_ref, event * FIELD)


def land_faces_kernel(events, got_ref, faces_hbm, near_ref, far_ref, faces_ref, source_ref, low_ref, high_ref, sem):
    copy = pltpu.make_async_copy(faces_hbm, faces_ref, sem)
    copy.start()
    land(got_ref, events, FACE_WANTS, (low_ref, high_ref))
    source_ref[...] = jnp.zeros_like(source_ref)
    for each in range(STEPS * events):
        rows = slice(each * 16, (each + 1) * 16)
        for j in range(2):
            cut = slice(j * LANE, (j + 1) * LANE)
            source_ref[pl.ds(each * 16 * SUB + j, 16, stride=SUB), :] = low_ref[rows, cut]
            source_ref[pl.ds(each * 16 * SUB + SUB - 2 + j, 16, stride=SUB), :] = high_ref[rows, cut]
        assemble_layers(source_ref, each * 16 * SUB, 1)
    copy.wait()
    even = is_even()
    fields = 2 * events + 1
    for field in range(fields + events):
        for b in range(4):
            if field < fields:
                low = at(faces_ref, field * FACE, b)[...]
                high = at(faces_ref, (fields + field) * FACE, b)[...]
            if events <= field < 2 * events:
                source_low, source_high = face_tiles(source_ref, (field - events) * 16 * SUB, b, 0, 0)
                low, high = low - source_low, high - source_high
            if field >= fields:
                low, high = face_tiles(source_ref, (events + field - fields) * 16 * SUB, b, 0, 0)
            at(near_ref, field * FACE, b)[...] = jnp.where(even, high, low)
            at(far_ref, field * FACE, b)[...] = jnp.where(even, low, high)


def state_rows(events):
    counts = {"force": 2 * events, "mass": 1, "base": 2 * events, "stiff": 1, "kern": 1}
    rows, total = {}, 0
    for name, count in counts.items():
        rows[name] = total * FIELD
        total += count
    return rows, total * FIELD


def land_first_kernel(
    events, got_ref, state_hbm, now_hbm, state_ref, now_ref, acc0, source_ref, acc1, acc2, acc3, sems
):
    copies = [
        pltpu.make_async_copy(state_hbm, state_ref, sems.at[0]),
        pltpu.make_async_copy(now_hbm, now_ref, sems.at[1]),
    ]
    for copy in copies:
        copy.start()
    land(got_ref, events, FIRST_WANTS, (acc0, acc1, acc2, acc3))
    spread_source(events, (acc0, acc1, acc2, acc3), 0, source_ref)
    for copy in copies:
        copy.wait()
    rows, _ = state_rows(events)
    for event in range(events):
        for n in range(NODES):
            place = at(state_ref, rows["force"] + (events + event) * FIELD, n)
            place[...] = place[...] - at(source_ref, event * FIELD, n)[...]


def land_later_kernel(
    events, got_ref, new_ref, acc0, fwd_hbm, adj_hbm, source_ref, out_ref, acc1, acc2, acc3, sems
):
    copies = []
    for event in range(events):
        for field, out_hbm in ((event, fwd_hbm), (events + event, adj_hbm)):
            gather_back(new_ref, field * FIELD, out_ref, field)
            copies.append(pltpu.make_async_copy(out_ref.at[field], out_hbm.at[event], sems.at[field]))
            copies[-1].start()
    land(got_ref, events, LATER_WANTS, (acc1, acc2, acc3))
    spread_source(events, (acc0, acc1, acc2, acc3), events * NODES, source_ref)
    for copy in copies:
        copy.wait()


def first_kernel(
    events, fwd_ref, fwd_prev_ref, adj_ref, adj_prev_ref, shear_ref, density_ref, _, state_ref, now_ref, faces_ref, prev_ref
):
    rows, _ = state_rows(events)
    stiff_ref, kern_ref = (state_ref.at[pl.ds(rows[name], FIELD), :] for name in ("stiff", "kern"))
    spread(shear_ref, None, state_ref, rows["stiff"])
    for n in range(NODES):
        place = at(stiff_ref, 0, n)
        place[...] = place[...] * WEIGHT[n]
        at(kern_ref, 0, n)[...] = jnp.zeros((SUB, LANE), jnp.float32)
        at(state_ref, rows["mass"], n)[...] = density_ref[...] * WEIGHT[n]

    def one(event, _):
        u, v = event * FIELD, (events + event) * FIELD
        for now_src, prev_src, field in ((fwd_ref, fwd_prev_ref, u), (adj_ref, adj_prev_ref, v)):
            spread(now_src, event, now_ref, field)
            spread(prev_src, event, prev_ref, 0)
            for n in range(NODES):
                at(state_ref, rows["base"] + field, n)[...] = 2.0 * at(now_ref, field, n)[...] - at(prev_ref, 0, n)[...]
        stiffness(
            [(now_ref, u), (now_ref, v)],
            [(state_ref, rows["force"] + u), (state_ref, rows["force"] + v)],
            stiff_ref,
            kern_ref,
        )
        return 0

    lax.fori_loop(0, events, one, 0)
    fields = 2 * events + 1

    def join(field, _):
        assemble(state_ref, rows["force"] + field * FIELD)
        for b in range(4):
            low, high = face_tiles(state_ref, rows["force"] + field * FIELD, b, 0, 48)
            at(faces_ref, field * FACE, b)[...] = low
            at(faces_ref, (fields + field) * FACE, b)[...] = high
        return 0

    lax.fori_loop(0, fields, join, 0)


def second_kernel(
    events, share, position_ref, state_ref, now_ref, far_rim_ref, near_rim_ref,
    new_ref, base_ref, factor_ref, next_ref, parts_ref, near_ref, far_ref, later_ref, kern_ref,
):
    rows, _ = state_rows(events)
    stiff_ref = state_ref.at[pl.ds(rows["stiff"], FIELD), :]
    kern_ref[...] = state_ref[pl.ds(rows["kern"], FIELD), :]
    mass = 2 * events
    for side, rim_ref in enumerate((near_rim_ref, far_rim_ref)):
        for row in range(0, events * FACE, SUB):
            later_ref[side, row : row + SUB, :] = rim_ref[(mass + 1) * FACE + row : (mass + 1) * FACE + row + SUB, :]
    even = is_even()
    for n in range(NODES):
        at(factor_ref, 0, n)[...] = STEP_SQUARE / with_rim(
            at(state_ref, rows["mass"], n)[...], n, near_rim_ref, far_rim_ref, mass * FACE
        )

    def one(event, _):
        u, v = event * FIELD, (events + event) * FIELD
        for field, rim in ((u, event), (v, events + event)):
            for n in range(NODES):
                force = with_rim(at(state_ref, rows["force"] + field, n)[...], n, near_rim_ref, far_rim_ref, rim * FACE)
                new = at(state_ref, rows["base"] + field, n)[...] - at(factor_ref, 0, n)[...] * force
                at(new_ref, field, n)[...] = new
                at(base_ref, field, n)[...] = 2.0 * new - at(now_ref, field, n)[...]
        stiffness([(new_ref, u), (new_ref, v)], [(next_ref, u), (next_ref, v)], stiff_ref, kern_ref)
        assemble(next_ref, u)
        assemble(next_ref, v)
        for field in (u, v):
            for b in range(4):
                low, high = face_tiles(next_ref, field, b, 0, 48)
                at(near_ref, field // NODES * 4, b)[...] = jnp.where(even, high, low)
                at(far_ref, field // NODES * 4, b)[...] = jnp.where(even, low, high)
        return 0

    lax.fori_loop(0, events, one, 0)
    for n in range(NODES):
        place = at(kern_ref, 0, n)
        place[...] = -TIME_STEP * at(stiff_ref, 0, n)[...] * place[...]
    tiles = SUB // share
    for j in range(share):
        owner = lax.rem(position_ref[0] + j, share)
        for k in range(tiles):
            parts_ref[j, :, k * LANE : (k + 1) * LANE] = kern_ref[pl.ds(owner * tiles + k, NODES, stride=SUB), :]


def last_kernel(events, share, base_ref, factor_ref, next_ref, source_ref, later_ref, *rest):
    far_rim_ref, near_rim_ref, fwd_hbm, adj_hbm, kernel_hbm, done_ref, out_ref, kernel_ref, sems = rest[share:]
    total = rest[0][0]
    for part in rest[1:share]:
        total = total + part[0]
    kernel_ref[...] = total
    copies = [pltpu.make_async_copy(kernel_ref, kernel_hbm, sems.at[2 * events])]
    copies[0].start()
    for event in range(events):
        for field, out_hbm in ((event, fwd_hbm), (events + event, adj_hbm)):
            for n in range(NODES):
                force = with_rim(at(next_ref, field * FIELD, n)[...], n, near_rim_ref, far_rim_ref, field * FACE)
                if field >= events:
                    source = at(source_ref, event * FIELD, n)[...]
                    force = force - with_rim(source, n, later_ref.at[0], later_ref.at[1], event * FACE)
                at(done_ref, 0, n)[...] = at(base_ref, field * FIELD, n)[...] - at(factor_ref, 0, n)[...] * force
            gather_back(done_ref, 0, out_ref, field)
            copies.append(pltpu.make_async_copy(out_ref.at[field], out_hbm.at[event], sems.at[field]))
            copies[-1].start()
    for copy in copies:
        copy.wait()


def call(body, outs, scratch=(), cost=2_000_000, smem=0, count=0, outside=0, limit=24, written=0):
    in_specs = [pl.BlockSpec(memory_space=pltpu.SMEM)] * smem
    in_specs += [pl.BlockSpec(memory_space=pltpu.VMEM)] * (count - smem - outside)
    in_specs += [pl.BlockSpec(memory_space=pl.ANY)] * outside
    return pl.pallas_call(
        body,
        out_shape=[out if not isinstance(out, tuple) else jax.ShapeDtypeStruct(out, jnp.float32) for out in outs],
        in_specs=in_specs,
        out_specs=[pl.BlockSpec(memory_space=pl.ANY)] * written
        + [pl.BlockSpec(memory_space=pltpu.VMEM)] * (len(outs) - written),
        scratch_shapes=[pltpu.VMEM(*x) if isinstance(x, tuple) else x for x in scratch],
        compiler_params=pltpu.CompilerParams(vmem_limit_bytes=limit * 1024 * 1024),
        cost_estimate=pl.CostEstimate(flops=cost, bytes_accessed=cost, transcendentals=0),
    )


def near_core(shape):
    return pltpu.VMEM(shape, jnp.float32)


def off_core(shape):
    return pltpu.HBM(shape, jnp.float32)


def kept(*arrays):
    return [pltpu.with_memory_space_constraint(x, pltpu.VMEM) for x in arrays]


def far_off(*arrays):
    return [pltpu.with_memory_space_constraint(x, pltpu.HBM) for x in arrays]


def beside(near, far):
    count = lax.axis_size("space")
    inner = [pair for i in range(1, count - 1, 2) for pair in ((i, i + 1), (i + 1, i))]
    from_far = lax.ppermute(far, "space", inner)
    from_near = lax.ppermute(near, "space", [(i, i + 1 - 2 * (i % 2)) for i in range(count)])
    return from_near, from_far


def shards(
    fwd_now,
    fwd_prev,
    adj_now,
    adj_prev,
    shear_mod,
    density,
    station_owner,
    receiver_local,
    station_weights,
    adj_records,
):
    events = fwd_now.shape[0]
    stations = station_owner.shape[0]
    elements = fwd_now.shape[-1]
    slabs = lax.axis_size("space")
    share = lax.axis_size("event")
    f32 = jnp.float32
    rows = -(-(NODES + events * STEPS + 1) // SUB) * SUB
    packed = 2 * (NODES + events * STEPS + 1)
    blocks = stations // LANE

    send, token = call(
        place_kernel,
        [near_core((slabs * packed, LANE)), near_core((SUB, LANE))],
        [
            ((blocks, LANE), jnp.int32),
            ((blocks, LANE), jnp.int32),
            ((NODES, stations), f32),
            ((events, STEPS, stations), f32),
            ((blocks, LANE), f32),
            ((2 * rows, stations), jnp.bfloat16),
            ((rows, stations + 3 * LANE), f32),
            pltpu.SemaphoreType.DMA((4,)),
        ],
        count=4,
        outside=4,
        limit=48,
    )(
        *far_off(
            station_owner.reshape(blocks, LANE), receiver_local.reshape(blocks, LANE), station_weights, adj_records
        )
    )
    send = send.reshape(slabs, packed // 2, 2, LANE)
    got = lax.all_to_all(send, "space", split_axis=0, concat_axis=0, tiled=True).reshape(slabs * packed, LANE)

    fields = 2 * events + 1
    state, now, faces = call(
        functools.partial(first_kernel, events),
        [
            off_core((state_rows(events)[1], LANE)),
            off_core((2 * events * FIELD, LANE)),
            off_core((2 * fields * FACE, LANE)),
        ],
        [((FIELD, LANE), f32)],
        count=7,
    )(*far_off(fwd_now, fwd_prev, adj_now, adj_prev, shear_mod, density.reshape(SUB, LANE)), *kept(token))
    near, far = call(
        functools.partial(land_faces_kernel, events),
        [((fields + events) * FACE, LANE)] * 2,
        [((2 * fields * FACE, LANE), f32), ((STEPS * events * 16 * SUB, LANE), f32)]
        + sums(events, FACE_WANTS)
        + [pltpu.SemaphoreType.DMA(())],
        count=2,
        outside=1,
    )(got, *far_off(faces))
    near_rim, far_rim = beside(near, far)
    state, now, quarter = call(
        functools.partial(land_first_kernel, events),
        [near_core(state.shape), near_core(now.shape), near_core((STEPS * events * NODES, CAP))],
        [((events * FIELD, LANE), f32)] + sums(events, FIRST_WANTS[1:]) + [pltpu.SemaphoreType.DMA((2,))],
        count=3,
        outside=2,
        limit=40,
    )(got, *far_off(state, now))
    new, base, factor, after, parts, near, far, later = call(
        functools.partial(second_kernel, events, share),
        [
            near_core((2 * events * FIELD, LANE)),
            near_core((2 * events * FIELD, LANE)),
            near_core((FIELD, LANE)),
            near_core((2 * events * FIELD, LANE)),
            (share, NODES, elements // share),
            (2 * events * FACE, LANE),
            (2 * events * FACE, LANE),
            near_core((2, events * FACE, LANE)),
        ],
        [((FIELD, LANE), f32)],
        smem=1,
        count=5,
    )(lax.axis_index("event").reshape(1).astype(jnp.int32), *kept(state, now), far_rim, near_rim)
    near_rim, far_rim = beside(near, far)
    pieces = [parts[0:1]] + [
        lax.ppermute(parts[j : j + 1], "event", [(i, (i + j) % share) for i in range(share)]) for j in range(1, share)
    ]
    fwd_before, adj_before, source = call(
        functools.partial(land_later_kernel, events),
        [fwd_now.shape, adj_now.shape, near_core((events * FIELD, LANE))],
        [((2 * events, NODES, elements), f32)]
        + sums(events, LATER_WANTS)
        + [pltpu.SemaphoreType.DMA((2 * events,))],
        count=3,
        limit=40,
        written=2,
    )(got, *kept(new, quarter))
    fwd_last, adj_last, kernel = call(
        functools.partial(last_kernel, events, share),
        [fwd_now.shape, adj_now.shape, (NODES, elements // share)],
        [
            ((FIELD, LANE), f32),
            ((2 * events, NODES, elements), f32),
            ((NODES, elements // share), f32),
            pltpu.SemaphoreType.DMA((2 * events + 1,)),
        ],
        count=7 + share,
        written=3,
    )(*kept(base, factor, after, source, later), *pieces, far_rim, near_rim)
    return fwd_last, fwd_before, adj_last, adj_before, kernel


def solution(mesh):
    in_specs = (
        P("event", None, "space"),
        P("event", None, "space"),
        P("event", None, "space"),
        P("event", None, "space"),
        P(None, "space"),
        P("space"),
        P("space", None),
        P("space"),
        P(None, "space"),
        P("event", None, "space"),
    )
    out_specs = (
        P("event", None, "space"),
        P("event", None, "space"),
        P("event", None, "space"),
        P("event", None, "space"),
        P(None, ("space", "event")),
    )
    return jax.shard_map(shards, mesh=mesh, in_specs=in_specs, out_specs=out_specs, check_vma=False)
```

```python
import functools

import jax
import jax.numpy as jnp
import numpy as np
from jax import lax
from jax.experimental import pallas as pl
from jax.experimental.pallas import tpu as pltpu
from jax.sharding import PartitionSpec as P

EX = 16
EY = 16
STEPS = 2
CAP = 256
NODES = 64
SUB = 8
LANE = 128
FIELD = NODES * SUB
FACE = 4 * SUB


TIME_STEP = 0.08
STEP_SQUARE = 0.0064

EDGE = np.array([1.0 / 6.0, 5.0 / 6.0, 5.0 / 6.0, 1.0 / 6.0])
WEIGHT = [float(np.float32(EDGE[n // 16] * EDGE[n // 4 % 4] * EDGE[n % 4])) for n in range(NODES)]
ROOT5 = float(np.sqrt(5.0))

LINES = (
    [[16 * c + 4 * b + i for i in range(4)] for c in range(4) for b in range(4)],
    [[16 * c + 4 * i + a for i in range(4)] for c in range(4) for a in range(4)],
    [[16 * i + 4 * b + a for i in range(4)] for b in range(4) for a in range(4)],
)


def derive(x0, x1, x2, x3):
    o0, o1 = x0 - x3, x1 - x2
    q = (x1 + x2) - (x0 + x3)
    a0, a1 = 1.25 * q, (0.25 * ROOT5) * q
    b0 = -1.75 * o0 + (1.25 * ROOT5) * o1
    b1 = -0.25 * o0 - (0.25 * ROOT5) * o1
    return b0 + a0, b1 + a1, b1 - a1, b0 - a0


def derive_transposed(h0, h1, h2, h3):
    p0, m0, p1, m1 = h0 + h3, h0 - h3, h1 + h2, h1 - h2
    q = 1.25 * m0 + (0.25 * ROOT5) * m1
    o0 = -1.75 * p0 - 0.25 * p1
    o1 = (1.25 * ROOT5) * p0 - (0.25 * ROOT5) * p1
    return o0 - q, o1 + q, q - o1, -o0 - q


def at(ref, base, node):
    if isinstance(base, int):
        return ref.at[pl.ds(base + node * SUB, SUB), :]
    return ref.at[pl.ds(pl.multiple_of(base, SUB) + node * SUB, SUB), :]


def spread(src_ref, index, dst_ref, base):
    for k in range(SUB):
        block = src_ref[:, k * LANE : (k + 1) * LANE] if index is None else src_ref[index, :, k * LANE : (k + 1) * LANE]
        dst_ref[pl.ds(base + k, NODES, stride=SUB), :] = block


def gather_back(src_ref, base, dst_ref, index):
    for k in range(SUB):
        dst_ref[index, :, k * LANE : (k + 1) * LANE] = src_ref[pl.ds(base + k, NODES, stride=SUB), :]


def places():
    lane = lax.broadcasted_iota(jnp.int32, (SUB, LANE), 1)
    sub = lax.broadcasted_iota(jnp.int32, (SUB, LANE), 0)
    return lane, sub


def assemble_layers(ref, base, planes):
    lane, sub = places()
    zero = jnp.zeros((SUB, LANE), jnp.float32)
    not_first = lane % EX != 0
    not_last = lane % EX != EX - 1
    odd = sub % 2 == 1
    for c in range(planes):
        for b in range(4):
            n = 16 * c + 4 * b
            low_at, high_at = at(ref, base, n), at(ref, base, n + 3)
            low, high = low_at[...], high_at[...]
            low_at[...] = low + jnp.where(not_first, pltpu.roll(high, 1, 1), zero)
            high_at[...] = high + jnp.where(not_last, pltpu.roll(low, LANE - 1, 1), zero)
    for c in range(planes):
        for a in range(4):
            n = 16 * c + a
            low_at, high_at = at(ref, base, n), at(ref, base, n + 12)
            low, high = low_at[...], high_at[...]
            back = pltpu.roll(high, EX, 1)
            ahead = pltpu.roll(low, LANE - EX, 1)
            back = jnp.where(lane >= EX, back, jnp.where(odd, pltpu.roll(back, 1, 0), zero))
            ahead = jnp.where(lane < LANE - EX, ahead, jnp.where(odd, zero, pltpu.roll(ahead, SUB - 1, 0)))
            low_at[...] = low + back
            high_at[...] = high + ahead


def assemble(ref, base):
    _, sub = places()
    zero = jnp.zeros((SUB, LANE), jnp.float32)
    assemble_layers(ref, base, 4)
    for n in range(16):
        low_at, high_at = at(ref, base, n), at(ref, base, n + 48)
        low, high = low_at[...], high_at[...]
        low_at[...] = low + jnp.where(sub >= 2, pltpu.roll(high, 2, 0), zero)
        high_at[...] = high + jnp.where(sub < SUB - 2, pltpu.roll(low, SUB - 2, 0), zero)


def roll_sub(value, shift):
    shift = shift % SUB
    return value if shift == 0 else pltpu.roll(value, shift, 0)


def is_even():
    return lax.rem(lax.axis_index("space"), 2) == 0


def face_tiles(ref, base, b, low_first, high_first):
    _, sub = places()
    tiles = []
    for first, shift in ((low_first, 0), (high_first, 2)):
        pieces = [roll_sub(at(ref, base, first + 4 * b + a)[...], 2 * a + shift) for a in range(4)]
        tiles.append(
            jnp.where(
                sub < 4, jnp.where(sub < 2, pieces[0], pieces[1]), jnp.where(sub < 6, pieces[2], pieces[3])
            )
        )
    return tiles


def with_rim(value, node, near_ref, far_ref, rim_base):
    _, sub = places()
    zero = jnp.zeros((SUB, LANE), jnp.float32)
    c, b, a = node // 16, node // 4 % 4, node % 4
    if c not in (0, 3):
        return value
    near, far = at(near_ref, rim_base, b)[...], at(far_ref, rim_base, b)[...]
    if c == 0:
        return value + jnp.where(sub < 2, roll_sub(jnp.where(is_even(), far, near), -2 * a), zero)
    return value + jnp.where(sub >= 6, roll_sub(jnp.where(is_even(), near, far), 6 - 2 * a), zero)


def stiffness(ins, outs, stiff_ref, kern):
    for dim, lines in enumerate(LINES):
        for line in lines:
            stiff = [at(stiff_ref, 0, n)[...] for n in line]
            grads = []
            for (src, sbase), out in zip(ins, outs):
                g = derive(*[at(src, sbase, n)[...] for n in line])
                grads.append(g)
                if out is None:
                    continue
                dst, dbase = out
                back = derive_transposed(*[x * s for x, s in zip(g, stiff)])
                for n, x in zip(line, back):
                    place = at(dst, dbase, n)
                    place[...] = x if dim == 0 else place[...] + x
            if kern is not None:
                for i, n in enumerate(line):
                    place = at(kern, 0, n)
                    place[...] = place[...] + grads[0][i] * grads[1][i]


def place_kernel(
    owner_hbm, local_hbm, weights_hbm, records_hbm, out_ref, token_ref,
    owner_ref, local_ref, weights_ref, records_ref, spot_ref, data_ref, sorted_ref, sems,
):
    copies = [
        pltpu.make_async_copy(src, dst, sems.at[i])
        for i, (src, dst) in enumerate(
            (
                (owner_hbm, owner_ref),
                (local_hbm, local_ref),
                (weights_hbm, weights_ref),
                (records_hbm, records_ref),
            )
        )
    ]
    for copy in copies:
        copy.start()
    token_ref[...] = jnp.zeros_like(token_ref)
    stations = weights_ref.shape[1]
    rows = sorted_ref.shape[0]
    events = records_ref.shape[0]
    few = events * STEPS + 1
    packed = 2 * (NODES + few)
    slabs = out_ref.shape[0] // packed
    blocks = stations // LANE
    chunks = stations // CAP
    owner_id = lax.broadcasted_iota(jnp.int32, (slabs, LANE), 0)
    before = lax.broadcasted_iota(jnp.int32, (LANE, LANE), 0) < lax.broadcasted_iota(jnp.int32, (LANE, LANE), 1)
    counting = jnp.concatenate(
        [jnp.where(before, 1.0, 0.0), jnp.ones((LANE, LANE), jnp.float32)], axis=1
    ).astype(jnp.bfloat16)
    copies[0].wait()
    named = [jnp.where(owner_ref[b : b + 1, :] == owner_id, 1.0, 0.0) for b in range(blocks)]
    counts = jnp.dot(
        jnp.concatenate(named, axis=0).astype(jnp.bfloat16), counting, preferred_element_type=jnp.float32
    )
    total = jnp.zeros((slabs, LANE), jnp.float32)
    earlier = []
    for b in range(blocks):
        part = counts[b * slabs : (b + 1) * slabs]
        earlier.append(part[:, :LANE] + total)
        total = total + part[:, LANE:]
    start = jnp.zeros((1, LANE), jnp.float32)
    starts = []
    for slab in range(slabs):
        starts.append(start)
        start = start + total[slab : slab + 1]
    starts = jnp.concatenate(starts, axis=0)
    for b in range(blocks):
        spot_ref[b : b + 1, :] = jnp.sum(named[b] * (earlier[b] + starts), axis=0, keepdims=True)
    first, count = starts.astype(jnp.int32), total.astype(jnp.int32)
    begins = [first[slab, 0] for slab in range(slabs)]
    sizes = [count[slab, 0] for slab in range(slabs)]
    for copy in copies[1:]:
        copy.wait()
    extra = rows - NODES - events * STEPS
    for b in range(blocks):
        cut = slice(b * LANE, (b + 1) * LANE)
        ids = jnp.broadcast_to(local_ref[b : b + 1, :].astype(jnp.float32), (extra, LANE))
        full = jnp.concatenate(
            [weights_ref[:, cut]] + [records_ref[event, :, cut] for event in range(events)] + [ids], axis=0
        )
        high = full.astype(jnp.bfloat16)
        data_ref[:rows, cut] = high
        data_ref[rows:, cut] = (full - high.astype(jnp.float32)).astype(jnp.bfloat16)
    slot = lax.broadcasted_iota(jnp.int32, (CAP, LANE), 0).astype(jnp.bfloat16)
    lane = lax.broadcasted_iota(jnp.int32, (SUB, LANE), 1)
    sorted_ref[:, stations:] = jnp.zeros((rows, 3 * LANE), jnp.float32)

    def cut_block(slab):
        begin, size = begins[slab], sizes[slab]
        shift = lax.rem(begin, LANE)
        base = begin - shift
        late = lane >= shift
        slots = (jnp.where(late, lane - shift, lane + 2 * LANE - shift), lane + LANE - shift)
        for first in range(0, rows, SUB):
            tiles = [
                sorted_ref[first : first + SUB, pl.ds(pl.multiple_of(base + j * LANE, LANE), LANE)] for j in range(3)
            ]
            for j, piece in enumerate((jnp.where(late, tiles[0], tiles[2]), tiles[1])):
                if first < NODES:
                    out_ref[pl.ds(slab * packed + j * NODES + first, SUB), :] = piece
                else:
                    piece = jnp.where(slots[j] < size, piece, 0.0)
                    out_ref[pl.ds(slab * packed + 2 * NODES + j * few, few), :] = piece[:few]

    for chunk in range(chunks):
        spots = spot_ref[...] - float(chunk * CAP)
        wanted = jnp.where((spots >= 0.0) & (spots < CAP), spots, -1.0)
        hot = [
            jnp.where(slot == wanted[b : b + 1, :].astype(jnp.bfloat16), jnp.bfloat16(1), jnp.bfloat16(0))
            for b in range(blocks)
        ]
        placed = lax.dot_general(
            data_ref[...],
            jnp.concatenate(hot, axis=1),
            (((1,), (1,)), ((), ())),
            preferred_element_type=jnp.float32,
        )
        sorted_ref[:, chunk * CAP : (chunk + 1) * CAP] = placed[:rows] + placed[rows:]
        cut_block(chunk)
    for slab in range(chunks, slabs):
        cut_block(slab)


def split(full):
    high = full.astype(jnp.bfloat16)
    return jnp.concatenate([high, (full - high.astype(jnp.float32)).astype(jnp.bfloat16)], axis=0)


def land(got_ref, events, wants, acc_refs):
    few = events * STEPS + 1
    packed = 2 * (NODES + few)
    slabs = got_ref.shape[0] // packed
    group = min(slabs, 16)
    slot = lax.broadcasted_iota(jnp.int32, (CAP, LANE), 0).astype(jnp.bfloat16)
    if slabs > group:
        for acc_ref in acc_refs:
            acc_ref[...] = jnp.zeros_like(acc_ref)

    def one(g, _):
        items = {item: [] for _, chosen in wants for item in chosen}
        hot = [[] for _ in wants]
        for i in range(group):
            src = g * group + i
            for (first, last, step), found in items.items():
                for j in range(2):
                    weights = got_ref[pl.ds(src * packed + j * NODES + first, last - first), :]
                    samples = [
                        got_ref[pl.ds(src * packed + 2 * NODES + j * few + event * STEPS + step, 1), :]
                        for event in range(events)
                    ]
                    found.append(split(jnp.concatenate([weights * sample for sample in samples], axis=0)))
            ids = [
                got_ref[pl.ds(src * packed + 2 * NODES + (j + 1) * few - 1, 1), :].astype(jnp.int32) for j in range(2)
            ]
            for at_hot, (quarter, _) in zip(hot, wants):
                for half in ids:
                    wanted = jnp.where(half // CAP == quarter, half % CAP, -1).astype(jnp.float32).astype(jnp.bfloat16)
                    at_hot.append(jnp.where(slot == wanted, jnp.bfloat16(1), jnp.bfloat16(0)))
        left = {item: jnp.concatenate(found, axis=1) for item, found in items.items()}
        for at_hot, (_, chosen), acc_ref in zip(hot, wants, acc_refs):
            landed = lax.dot_general(
                jnp.concatenate([left[item] for item in chosen], axis=0),
                jnp.concatenate(at_hot, axis=1),
                (((1,), (1,)), ((), ())),
                preferred_element_type=jnp.float32,
            )
            at_in, at_out = 0, 0
            for first, last, _ in chosen:
                count = events * (last - first)
                rows = slice(at_out, at_out + count)
                both = landed[at_in : at_in + count] + landed[at_in + count : at_in + 2 * count]
                acc_ref[rows, :] = acc_ref[rows, :] + both if slabs > group else both
                at_in, at_out = at_in + 2 * count, at_out + count
        return 0

    if slabs > group:
        lax.fori_loop(0, slabs // group, one, 0)
    else:
        one(0, 0)


FACE_WANTS = ((0, ((0, 16, 0), (0, 16, 1))), (3, ((48, 64, 0), (48, 64, 1))))
FIRST_WANTS = ((0, ((0, NODES, 0), (0, NODES, 1))),) + tuple((q, ((0, NODES, 0),)) for q in range(1, 4))
LATER_WANTS = tuple((q, ((0, NODES, 1),)) for q in range(1, 4))


def sums(events, wants):
    return [
        ((sum(events * (last - first) for first, last, _ in chosen), CAP), jnp.float32) for _, chosen in wants
    ]


def spread_source(events, acc_refs, skip, out_ref):
    for event in range(events):
        for k in range(SUB):
            cut = slice(k % 2 * LANE, (k % 2 + 1) * LANE)
            first = event * NODES + (skip if k < 2 else 0)
            rows = slice(first, first + NODES)
            out_ref[pl.ds(event * FIELD + k, NODES, stride=SUB), :] = acc_refs[k // 2][rows, cut]
        assemble(out_ref, event * FIELD)


def land_faces_kernel(events, got_ref, faces_hbm, near_ref, far_ref, faces_ref, source_ref, low_ref, high_ref, sem):
    copy = pltpu.make_async_copy(faces_hbm, faces_ref, sem)
    copy.start()
    land(got_ref, events, FACE_WANTS, (low_ref, high_ref))
    source_ref[...] = jnp.zeros_like(source_ref)
    for each in range(STEPS * events):
        rows = slice(each * 16, (each + 1) * 16)
        for j in range(2):
            cut = slice(j * LANE, (j + 1) * LANE)
            source_ref[pl.ds(each * 16 * SUB + j, 16, stride=SUB), :] = low_ref[rows, cut]
            source_ref[pl.ds(each * 16 * SUB + SUB - 2 + j, 16, stride=SUB), :] = high_ref[rows, cut]
        assemble_layers(source_ref, each * 16 * SUB, 1)
    copy.wait()
    even = is_even()
    fields = 2 * events + 1
    for field in range(fields + events):
        for b in range(4):
            if field < fields:
                low = at(faces_ref, field * FACE, b)[...]
                high = at(faces_ref, (fields + field) * FACE, b)[...]
            if events <= field < 2 * events:
                source_low, source_high = face_tiles(source_ref, (field - events) * 16 * SUB, b, 0, 0)
                low, high = low - source_low, high - source_high
            if field >= fields:
                low, high = face_tiles(source_ref, (events + field - fields) * 16 * SUB, b, 0, 0)
            at(near_ref, field * FACE, b)[...] = jnp.where(even, high, low)
            at(far_ref, field * FACE, b)[...] = jnp.where(even, low, high)


def state_rows(events):
    counts = {"force": 2 * events, "mass": 1, "base": 2 * events, "stiff": 1, "kern": 1}
    rows, total = {}, 0
    for name, count in counts.items():
        rows[name] = total * FIELD
        total += count
    return rows, total * FIELD


def land_first_kernel(
    events, got_ref, state_hbm, now_hbm, state_ref, now_ref, acc0, source_ref, acc1, acc2, acc3, sems
):
    copies = [
        pltpu.make_async_copy(state_hbm, state_ref, sems.at[0]),
        pltpu.make_async_copy(now_hbm, now_ref, sems.at[1]),
    ]
    for copy in copies:
        copy.start()
    land(got_ref, events, FIRST_WANTS, (acc0, acc1, acc2, acc3))
    spread_source(events, (acc0, acc1, acc2, acc3), 0, source_ref)
    for copy in copies:
        copy.wait()
    rows, _ = state_rows(events)
    for event in range(events):
        for n in range(NODES):
            place = at(state_ref, rows["force"] + (events + event) * FIELD, n)
            place[...] = place[...] - at(source_ref, event * FIELD, n)[...]


def land_later_kernel(
    events, got_ref, new_ref, acc0, fwd_hbm, adj_hbm, source_ref, out_ref, acc1, acc2, acc3, sems
):
    copies = []
    for event in range(events):
        for field, out_hbm in ((event, fwd_hbm), (events + event, adj_hbm)):
            gather_back(new_ref, field * FIELD, out_ref, field)
            copies.append(pltpu.make_async_copy(out_ref.at[field], out_hbm.at[event], sems.at[field]))
            copies[-1].start()
    land(got_ref, events, LATER_WANTS, (acc1, acc2, acc3))
    spread_source(events, (acc0, acc1, acc2, acc3), events * NODES, source_ref)
    for copy in copies:
        copy.wait()


def first_kernel(
    events, fwd_ref, fwd_prev_ref, adj_ref, adj_prev_ref, shear_ref, density_ref, _, state_ref, now_ref, faces_ref, prev_ref
):
    rows, _ = state_rows(events)
    stiff_ref, kern_ref = (state_ref.at[pl.ds(rows[name], FIELD), :] for name in ("stiff", "kern"))
    spread(shear_ref, None, state_ref, rows["stiff"])
    for n in range(NODES):
        place = at(stiff_ref, 0, n)
        place[...] = place[...] * WEIGHT[n]
        at(kern_ref, 0, n)[...] = jnp.zeros((SUB, LANE), jnp.float32)
        at(state_ref, rows["mass"], n)[...] = density_ref[...] * WEIGHT[n]

    def one(event, _):
        u, v = event * FIELD, (events + event) * FIELD
        for now_src, prev_src, field in ((fwd_ref, fwd_prev_ref, u), (adj_ref, adj_prev_ref, v)):
            spread(now_src, event, now_ref, field)
            spread(prev_src, event, prev_ref, 0)
            for n in range(NODES):
                at(state_ref, rows["base"] + field, n)[...] = 2.0 * at(now_ref, field, n)[...] - at(prev_ref, 0, n)[...]
        stiffness(
            [(now_ref, u), (now_ref, v)],
            [(state_ref, rows["force"] + u), (state_ref, rows["force"] + v)],
            stiff_ref,
            kern_ref,
        )
        return 0

    lax.fori_loop(0, events, one, 0)
    fields = 2 * events + 1

    def join(field, _):
        assemble(state_ref, rows["force"] + field * FIELD)
        for b in range(4):
            low, high = face_tiles(state_ref, rows["force"] + field * FIELD, b, 0, 48)
            at(faces_ref, field * FACE, b)[...] = low
            at(faces_ref, (fields + field) * FACE, b)[...] = high
        return 0

    lax.fori_loop(0, fields, join, 0)


def second_kernel(
    events, share, position_ref, state_ref, now_ref, far_rim_ref, near_rim_ref,
    new_ref, base_ref, factor_ref, next_ref, parts_ref, near_ref, far_ref, later_ref, kern_ref,
):
    rows, _ = state_rows(events)
    stiff_ref = state_ref.at[pl.ds(rows["stiff"], FIELD), :]
    kern_ref[...] = state_ref[pl.ds(rows["kern"], FIELD), :]
    mass = 2 * events
    for side, rim_ref in enumerate((near_rim_ref, far_rim_ref)):
        for row in range(0, events * FACE, SUB):
            later_ref[side, row : row + SUB, :] = rim_ref[(mass + 1) * FACE + row : (mass + 1) * FACE + row + SUB, :]
    even = is_even()
    for n in range(NODES):
        at(factor_ref, 0, n)[...] = STEP_SQUARE / with_rim(
            at(state_ref, rows["mass"], n)[...], n, near_rim_ref, far_rim_ref, mass * FACE
        )

    def one(event, _):
        u, v = event * FIELD, (events + event) * FIELD
        for field, rim in ((u, event), (v, events + event)):
            for n in range(NODES):
                force = with_rim(at(state_ref, rows["force"] + field, n)[...], n, near_rim_ref, far_rim_ref, rim * FACE)
                new = at(state_ref, rows["base"] + field, n)[...] - at(factor_ref, 0, n)[...] * force
                at(new_ref, field, n)[...] = new
                at(base_ref, field, n)[...] = 2.0 * new - at(now_ref, field, n)[...]
        stiffness([(new_ref, u), (new_ref, v)], [(next_ref, u), (next_ref, v)], stiff_ref, kern_ref)
        assemble(next_ref, u)
        assemble(next_ref, v)
        for field in (u, v):
            for b in range(4):
                low, high = face_tiles(next_ref, field, b, 0, 48)
                at(near_ref, field // NODES * 4, b)[...] = jnp.where(even, high, low)
                at(far_ref, field // NODES * 4, b)[...] = jnp.where(even, low, high)
        return 0

    lax.fori_loop(0, events, one, 0)
    for n in range(NODES):
        place = at(kern_ref, 0, n)
        place[...] = -TIME_STEP * at(stiff_ref, 0, n)[...] * place[...]
    tiles = SUB // share
    for j in range(share):
        owner = lax.rem(position_ref[0] + j, share)
        for k in range(tiles):
            parts_ref[j, :, k * LANE : (k + 1) * LANE] = kern_ref[pl.ds(owner * tiles + k, NODES, stride=SUB), :]


def last_kernel(events, share, base_ref, factor_ref, next_ref, source_ref, later_ref, *rest):
    far_rim_ref, near_rim_ref, fwd_hbm, adj_hbm, kernel_hbm, done_ref, out_ref, kernel_ref, sems = rest[share:]
    total = rest[0][0]
    for part in rest[1:share]:
        total = total + part[0]
    kernel_ref[...] = total
    copies = [pltpu.make_async_copy(kernel_ref, kernel_hbm, sems.at[2 * events])]
    copies[0].start()
    for event in range(events):
        for field, out_hbm in ((events + event, adj_hbm), (event, fwd_hbm)):
            for n in range(NODES):
                force = with_rim(at(next_ref, field * FIELD, n)[...], n, near_rim_ref, far_rim_ref, field * FACE)
                if field >= events:
                    source = at(source_ref, event * FIELD, n)[...]
                    force = force - with_rim(source, n, later_ref.at[0], later_ref.at[1], event * FACE)
                at(done_ref, field * FIELD, n)[...] = at(base_ref, field * FIELD, n)[...] - at(factor_ref, 0, n)[...] * force
            gather_back(done_ref, field * FIELD, out_ref, field)
            copies.append(pltpu.make_async_copy(out_ref.at[field], out_hbm.at[event], sems.at[field]))
            copies[-1].start()
    for copy in copies:
        copy.wait()


def call(body, outs, scratch=(), cost=2_000_000, smem=0, count=0, outside=0, limit=24, written=0):
    in_specs = [pl.BlockSpec(memory_space=pltpu.SMEM)] * smem
    in_specs += [pl.BlockSpec(memory_space=pltpu.VMEM)] * (count - smem - outside)
    in_specs += [pl.BlockSpec(memory_space=pl.ANY)] * outside
    return pl.pallas_call(
        body,
        out_shape=[out if not isinstance(out, tuple) else jax.ShapeDtypeStruct(out, jnp.float32) for out in outs],
        in_specs=in_specs,
        out_specs=[pl.BlockSpec(memory_space=pl.ANY)] * written
        + [pl.BlockSpec(memory_space=pltpu.VMEM)] * (len(outs) - written),
        scratch_shapes=[pltpu.VMEM(*x) if isinstance(x, tuple) else x for x in scratch],
        compiler_params=pltpu.CompilerParams(vmem_limit_bytes=limit * 1024 * 1024),
        cost_estimate=pl.CostEstimate(flops=cost, bytes_accessed=cost, transcendentals=0),
    )


def near_core(shape):
    return pltpu.VMEM(shape, jnp.float32)


def off_core(shape):
    return pltpu.HBM(shape, jnp.float32)


def kept(*arrays):
    return [pltpu.with_memory_space_constraint(x, pltpu.VMEM) for x in arrays]


def far_off(*arrays):
    return [pltpu.with_memory_space_constraint(x, pltpu.HBM) for x in arrays]


def beside(near, far):
    count = lax.axis_size("space")
    inner = [pair for i in range(1, count - 1, 2) for pair in ((i, i + 1), (i + 1, i))]
    from_far = lax.ppermute(far, "space", inner)
    from_near = lax.ppermute(near, "space", [(i, i + 1 - 2 * (i % 2)) for i in range(count)])
    return from_near, from_far


def shards(
    fwd_now,
    fwd_prev,
    adj_now,
    adj_prev,
    shear_mod,
    density,
    station_owner,
    receiver_local,
    station_weights,
    adj_records,
):
    events = fwd_now.shape[0]
    stations = station_owner.shape[0]
    elements = fwd_now.shape[-1]
    slabs = lax.axis_size("space")
    share = lax.axis_size("event")
    f32 = jnp.float32
    rows = -(-(NODES + events * STEPS + 1) // SUB) * SUB
    packed = 2 * (NODES + events * STEPS + 1)
    blocks = stations // LANE

    send, token = call(
        place_kernel,
        [near_core((slabs * packed, LANE)), near_core((SUB, LANE))],
        [
            ((blocks, LANE), jnp.int32),
            ((blocks, LANE), jnp.int32),
            ((NODES, stations), f32),
            ((events, STEPS, stations), f32),
            ((blocks, LANE), f32),
            ((2 * rows, stations), jnp.bfloat16),
            ((rows, stations + 3 * LANE), f32),
            pltpu.SemaphoreType.DMA((4,)),
        ],
        count=4,
        outside=4,
        limit=48,
    )(
        *far_off(
            station_owner.reshape(blocks, LANE), receiver_local.reshape(blocks, LANE), station_weights, adj_records
        )
    )
    send = send.reshape(slabs, packed // 2, 2, LANE)
    got = lax.all_to_all(send, "space", split_axis=0, concat_axis=0, tiled=True).reshape(slabs * packed, LANE)

    fields = 2 * events + 1
    state, now, faces = call(
        functools.partial(first_kernel, events),
        [
            off_core((state_rows(events)[1], LANE)),
            off_core((2 * events * FIELD, LANE)),
            off_core((2 * fields * FACE, LANE)),
        ],
        [((FIELD, LANE), f32)],
        count=7,
    )(*far_off(fwd_now, fwd_prev, adj_now, adj_prev, shear_mod, density.reshape(SUB, LANE)), *kept(token))
    near, far = call(
        functools.partial(land_faces_kernel, events),
        [((fields + events) * FACE, LANE)] * 2,
        [((2 * fields * FACE, LANE), f32), ((STEPS * events * 16 * SUB, LANE), f32)]
        + sums(events, FACE_WANTS)
        + [pltpu.SemaphoreType.DMA(())],
        count=2,
        outside=1,
    )(got, *far_off(faces))
    near_rim, far_rim = beside(near, far)
    state, now, quarter = call(
        functools.partial(land_first_kernel, events),
        [near_core(state.shape), near_core(now.shape), near_core((STEPS * events * NODES, CAP))],
        [((events * FIELD, LANE), f32)] + sums(events, FIRST_WANTS[1:]) + [pltpu.SemaphoreType.DMA((2,))],
        count=3,
        outside=2,
        limit=40,
    )(got, *far_off(state, now))
    new, base, factor, after, parts, near, far, later = call(
        functools.partial(second_kernel, events, share),
        [
            near_core((2 * events * FIELD, LANE)),
            near_core((2 * events * FIELD, LANE)),
            near_core((FIELD, LANE)),
            near_core((2 * events * FIELD, LANE)),
            (share, NODES, elements // share),
            (2 * events * FACE, LANE),
            (2 * events * FACE, LANE),
            near_core((2, events * FACE, LANE)),
        ],
        [((FIELD, LANE), f32)],
        smem=1,
        count=5,
    )(lax.axis_index("event").reshape(1).astype(jnp.int32), *kept(state, now), far_rim, near_rim)
    near_rim, far_rim = beside(near, far)
    pieces = [parts[0:1]] + [
        lax.ppermute(parts[j : j + 1], "event", [(i, (i + j) % share) for i in range(share)]) for j in range(1, share)
    ]
    fwd_before, adj_before, source = call(
        functools.partial(land_later_kernel, events),
        [fwd_now.shape, adj_now.shape, near_core((events * FIELD, LANE))],
        [((2 * events, NODES, elements), f32)]
        + sums(events, LATER_WANTS)
        + [pltpu.SemaphoreType.DMA((2 * events,))],
        count=3,
        limit=40,
        written=2,
    )(got, *kept(new, quarter))
    fwd_last, adj_last, kernel = call(
        functools.partial(last_kernel, events, share),
        [fwd_now.shape, adj_now.shape, (NODES, elements // share)],
        [
            ((2 * events * FIELD, LANE), f32),
            ((2 * events, NODES, elements), f32),
            ((NODES, elements // share), f32),
            pltpu.SemaphoreType.DMA((2 * events + 1,)),
        ],
        count=7 + share,
        written=3,
    )(*kept(base, factor, after, source, later), *pieces, far_rim, near_rim)
    return fwd_last, fwd_before, adj_last, adj_before, kernel


def solution(mesh):
    in_specs = (
        P("event", None, "space"),
        P("event", None, "space"),
        P("event", None, "space"),
        P("event", None, "space"),
        P(None, "space"),
        P("space"),
        P("space", None),
        P("space"),
        P(None, "space"),
        P("event", None, "space"),
    )
    out_specs = (
        P("event", None, "space"),
        P("event", None, "space"),
        P("event", None, "space"),
        P("event", None, "space"),
        P(None, ("space", "event")),
    )
    return jax.shard_map(shards, mesh=mesh, in_specs=in_specs, out_specs=out_specs, check_vma=False)
```
